32 devices in a mesh: gx: 2 (over x), gy: 4 (over y, core), tx: 4 (over z).
Axes of the slice: x: 2, y: 2, z: 4, core: 2. Of those that a mesh axis runs over, the one named last changes fastest.
Arguments:
- src_cell: int32 [8], P('tx'), may hold values from 0 to 65535
- basis: bfloat16 [16, 2, 3, 8, 16, 512], P('tx', None, None, None, 'gx', 'gy'), as said below
- images: bfloat16 [16, 2, 3, 8, 16, 512], P('tx', None, None, None, 'gx', 'gy'), as said below
- induction: bfloat16 [3, 8, 16, 512], P(None, 'tx', 'gx', 'gy'), may hold values from 0.25 to 4
Outputs:
- solution: float32 [8, 2, 3, 8, 16, 512], P('tx', None, None, None, 'gx', 'gy')
- residual: float32 [8, 2, 3, 8, 16, 512], P('tx', None, None, None, 'gx', 'gy')
The draws below stay inside these ranges and needn't reach their ends.
Inputs may be any that keep to these rules, and one draw needn't show every extreme that they name: `basis`: entries of order one. `images`: entries of order one.
All inputs are finite; a program needn't handle non-finite values.
Results may differ from the reference program's by a relative error of at most 0.0003.
Values may be sent and summed in bfloat16 or wider, within the bound.
A program may use at most 64 MiB of HBM per device.

```python
import math
import jax
import jax.numpy as jnp
from jax import lax

NZ = 8
CYCLES = 2
ARNOLDI = 2
NX = 16
NY = 512
SOURCES = 8
VECS = 16


def shaped_modes():
    index = jnp.arange(VECS)
    p_wave = (index // 4).astype(jnp.float32)
    q_wave = (index % 4).astype(jnp.float32)
    x_pos = (jnp.arange(NX).astype(jnp.float32) + 0.5) / NX
    y_pos = (jnp.arange(NY).astype(jnp.float32) + 0.5) / NY
    z_pos = (jnp.arange(NZ).astype(jnp.float32) + 0.5) / NZ
    along_x = jnp.cos(math.pi * (p_wave[:, None] + 0.5) * x_pos[None, :])
    along_y = jnp.cos(math.pi * (q_wave[:, None] + 0.5) * y_pos[None, :])
    plane = along_x[:, :, None] * along_y[:, None, :]
    z_factor = 1.0 + 0.3 * jnp.cos(math.pi * z_pos)
    comp_factor = jnp.array([1.0, 0.7, 0.4], dtype=jnp.float32)
    part_factor = jnp.array([1.0, -0.5], dtype=jnp.float32)
    return plane[:, None, None, None, :, :] * part_factor[None, :, None, None, None, None] * comp_factor[None, None, :, None, None, None] * z_factor[None, None, None, :, None, None]


def rough_field(key):
    shape = (VECS, 2, 3, NZ, NX, NY)
    noise = jax.random.normal(key, shape, jnp.float32)
    return shaped_modes() * (1.0 + 0.5 * noise)


def draw_basis(key, part):
    return rough_field(jax.random.fold_in(key, 11)).astype(jnp.bfloat16)


def draw_images(key, part):
    return (2.0 * rough_field(jax.random.fold_in(key, 23))).astype(jnp.bfloat16)


def set_ends(entries, rng, least, high):
    extent = entries.shape
    index_at = [jax.random.randint(jax.random.fold_in(rng, axis), (), 0, extent[axis]) for axis in range(len(extent))]
    entries = entries.at[tuple(index_at)].set(least)
    longest = extent.index(max(extent))
    index_at[longest] = (index_at[longest] + 1) % extent[longest]
    return entries.at[tuple(index_at)].set(high)


def shard_levels(key, extent, pieces, least, largest):
    gain = 1.0
    for dim, blocks in pieces:
        heights = jax.random.uniform(jax.random.fold_in(jax.random.fold_in(key, 6), dim), (blocks,), jnp.float32, least / len(pieces), largest / len(pieces))
        gain = gain * jnp.repeat(jnp.exp(heights), extent[dim] // blocks).reshape((-1,) + (1,) * (len(extent) - 1 - dim))
    return gain


def setup_inputs(seed: int = 0) -> dict:
    splits = jax.random.split(jax.random.key(seed), 5)
    return {
        "src_cell": set_ends(jax.random.randint(splits[0], (SOURCES,), 0, NX * NY * NZ), jax.random.fold_in(splits[0], 1), 0, (NX * NY * NZ) - 1).astype(jnp.int32),
        "basis": draw_basis(jax.random.fold_in(splits[4], 71), 0),
        "images": draw_images(jax.random.fold_in(splits[4], 71), 0),
        "induction": jnp.clip(jnp.exp(math.log(4.0) - 2.7725887 * jax.random.uniform(splits[3], (3, NZ, NX, NY), jnp.float32) ** shard_levels(splits[3], (3, NZ, NX, NY), ((1, 4), (2, 2), (3, 4)), -0.2, 0.2)), 0.25, 4.0).astype(jnp.bfloat16),
    }


eps = 1e-06

def differ(field, axis, forward):
    axis = field.ndim + axis
    count = field.shape[axis]
    delta = lax.slice_in_dim(field, 1, count, axis=axis) - lax.slice_in_dim(field, 0, count - 1, axis=axis)
    zero = jnp.zeros_like(lax.slice_in_dim(field, 0, 1, axis=axis))
    if forward:
        return jnp.concatenate([delta, zero], axis=axis)
    return jnp.concatenate([zero, delta], axis=axis)

def curl_curl(padded):
    e_x = padded[..., 0, :, :, :]
    e_y = padded[..., 1, :, :, :]
    e_z = padded[..., 2, :, :, :]
    b_x = differ(e_z, -1, True) - differ(e_y, -3, True)
    b_y = differ(e_x, -3, True) - differ(e_z, -2, True)
    b_z = differ(e_y, -2, True) - differ(e_x, -1, True)
    c_x = differ(b_z, -1, False) - differ(b_y, -3, False)
    c_y = differ(b_x, -3, False) - differ(b_z, -2, False)
    c_z = differ(b_y, -2, False) - differ(b_x, -1, False)
    whole = jnp.stack([c_x, c_y, c_z], axis=-4)
    return whole[..., 1:-1, 1:-1, 1:-1]

def operator(padded, field, induct):
    curled = curl_curl(padded)
    real_part = curled[:, 0] - induct[None] * field[:, 1]
    imag_part = curled[:, 1] + induct[None] * field[:, 0]
    return jnp.stack([real_part, imag_part], axis=1)

def source_field(cells, z_pos, x_pos, y_pos, size_x, size_y, induct):
    plane = size_x * size_y
    src_z = cells // plane
    rest = cells % plane
    src_x = rest // size_y
    src_y = rest % size_y
    d_z = (z_pos[None, :] - src_z[:, None]).astype(jnp.float32)
    d_x = (x_pos[None, :] - src_x[:, None]).astype(jnp.float32)
    d_y = (y_pos[None, :] - src_y[:, None]).astype(jnp.float32)
    dist = jnp.sqrt(d_z[:, :, None, None] ** 2 + d_x[:, None, :, None] ** 2 + d_y[:, None, None, :] ** 2)
    primary = jnp.exp(-dist / ((size_x + size_y) / 8.0))
    weights = jnp.array([1.0, 0.5, 0.25], dtype=jnp.float32)
    real_part = (induct - 1.0)[None] * weights[None, :, None, None, None] * primary[:, None]
    return jnp.stack([real_part, 0.5 * real_part], axis=1)

def inner_basis(vectors, field):
    return jnp.einsum('kpczxy,spczxy->ks', vectors.astype(jnp.float32), field.astype(jnp.float32), precision=lax.Precision.HIGHEST, preferred_element_type=jnp.float32)

def combine(coeffs, vectors):
    return jnp.einsum('ks,kpczxy->spczxy', coeffs.astype(jnp.float32), vectors.astype(jnp.float32), precision=lax.Precision.HIGHEST, preferred_element_type=jnp.float32)

def per_source(left, right):
    return lax.optimization_barrier(jnp.sum(left * right, axis=(1, 2, 3, 4, 5)))

def expand(values):
    return values[:, None, None, None, None, None]

def small_solve(matrix, rhs):
    factor = jnp.linalg.cholesky(matrix)
    return jax.scipy.linalg.cho_solve((factor, True), rhs)

def reference(src_cell, basis, images, induction):
    induct = induction.astype(jnp.float32)
    z_pos = jnp.arange(NZ, dtype=jnp.int32)
    x_pos = jnp.arange(NX, dtype=jnp.int32)
    y_pos = jnp.arange(NY, dtype=jnp.int32)
    rhs = source_field(src_cell, z_pos, x_pos, y_pos, NX, NY, induct)
    gram = jnp.einsum('kpczxy,lpczxy->kl', images.astype(jnp.float32), images.astype(jnp.float32), preferred_element_type=jnp.float32)
    factor = jnp.linalg.cholesky(gram)
    h_zero = jax.scipy.linalg.cho_solve((factor, True), inner_basis(images, rhs))
    solution = combine(h_zero, basis)
    residual = rhs - combine(h_zero, images)
    widths = [(0, 0), (0, 0), (0, 0), (1, 1), (1, 1), (1, 1)]
    for cycle in range(CYCLES):
        beta = jnp.sqrt(per_source(residual, residual) + eps)
        krylov = [residual / expand(beta)]
        h_cols = []
        g_cols = []
        for step in range(ARNOLDI):
            current = krylov[step]
            work = operator(jnp.pad(current, widths), current, induct)
            g_now = jax.scipy.linalg.cho_solve((factor, True), inner_basis(images, work))
            work = work - combine(g_now, images)
            h_now = jnp.stack([per_source(vec, work) for vec in krylov])
            for index in range(step + 1):
                work = work - expand(h_now[index]) * krylov[index]
            h_next = jnp.sqrt(per_source(work, work) + eps)
            krylov.append(work / expand(h_next))
            pad_rows = jnp.zeros((ARNOLDI - step - 1, h_next.shape[0]), dtype=jnp.float32)
            h_cols.append(jnp.concatenate([h_now, h_next[None], pad_rows], axis=0))
            g_cols.append(g_now)
        hess = jnp.stack(h_cols, axis=1)
        g_all = jnp.stack(g_cols, axis=1)
        normal = jnp.einsum('ijs,iks->sjk', hess, hess, precision=lax.Precision.HIGHEST)
        target = beta[:, None] * jnp.transpose(hess[0])
        y_coef = jax.vmap(small_solve)(normal, target)
        update = expand(y_coef[:, 0]) * krylov[0]
        for step in range(1, ARNOLDI):
            update = update + expand(y_coef[:, step]) * krylov[step]
        u_coef = jnp.einsum('kjs,sj->ks', g_all, y_coef, precision=lax.Precision.HIGHEST)
        solution = solution + update - combine(u_coef, basis)
        first = jnp.zeros((ARNOLDI + 1, beta.shape[0]), dtype=jnp.float32).at[0].set(beta)
        t_coef = first - jnp.einsum('ijs,sj->is', hess, y_coef, precision=lax.Precision.HIGHEST)
        residual = expand(t_coef[0]) * krylov[0]
        for index in range(1, ARNOLDI + 1):
            residual = residual + expand(t_coef[index]) * krylov[index]
    return (solution, residual)
```

```python
import functools

import jax
import jax.numpy as jnp
from jax import lax
from jax.experimental import pallas as pl
from jax.experimental.pallas import tpu as pltpu
from jax.sharding import PartitionSpec as P

CYCLES = 2
ARNOLDI = 2
EPS = 1e-06
MESH = pl.DeviceIdType.MESH
F32 = jnp.float32


def kernel(
    dims, pos_ref, u_ref, c_ref, m_ref, sol_ref, res_ref,
    full_c, full_u, ind_all, induct, krylov, work, total, inverse, coef, outer,
    part, parts, row_out, row_in, col_out, col_in,
    gather_send, gather_recv, ind_send, ind_recv, sum_send, sum_recv, halo_send, halo_recv,
):
    n_gx, n_gy, n_tx = dims
    gx, gy, tx = lax.axis_index("gx"), lax.axis_index("gy"), lax.axis_index("tx")
    group = n_gx * n_gy
    rank = gx * n_gy + gy
    sources = pos_ref.shape[0]
    per_dev = c_ref.shape[0]
    rows = c_ref.shape[1]
    width_y = c_ref.shape[2]
    width_x = 8
    depth = induct.shape[1]
    tiles = rows // width_x
    vecs = full_c.shape[0]
    half = tiles // 2
    resid = res_ref

    def peer_of(offset):
        other = lax.rem(rank + offset, group)
        return (lax.div(other, n_gy), lax.rem(other, n_gy), tx)

    def along(offset):
        return (gx, gy, lax.rem(tx + offset, n_tx))

    barrier = pltpu.get_barrier_semaphore()
    for offset in range(1, group):
        pl.semaphore_signal(barrier, inc=1, device_id=peer_of(offset), device_id_type=MESH)
    for offset in range(1, n_tx):
        pl.semaphore_signal(barrier, inc=1, device_id=along(offset), device_id_type=MESH)
    pl.semaphore_wait(barrier, group - 1 + n_tx - 1)

    def slot(shard):
        return pl.ds(shard * per_dev, per_dev)

    def hop(which, way, step):
        full = (full_c, full_u)[which]
        sign = 1 if way == 0 else -1
        shard = tx - sign * (step - 1)
        source = (c_ref, u_ref)[which] if step == 1 else full.at[slot(shard)]
        return pltpu.make_async_remote_copy(
            src_ref=source,
            dst_ref=full.at[slot(shard)],
            send_sem=gather_send.at[which, way, step - 1],
            recv_sem=gather_recv.at[which, way, step - 1],
            device_id=(gx, gy, tx + sign),
            device_id_type=MESH,
        )

    def sends(way, step):
        if way == 0:
            return jnp.logical_and(tx + 1 < n_tx, tx - step + 1 >= 0)
        return jnp.logical_and(tx - 1 >= 0, tx + step - 1 < n_tx)

    def receives(way, step):
        return tx - step >= 0 if way == 0 else tx + step < n_tx

    def gather_start(which, step):
        for way in range(2):
            @pl.when(sends(way, step))
            def _():
                hop(which, way, step).start()

    def gather_arrive(which, step):
        for way in range(2):
            @pl.when(receives(way, step))
            def _():
                full = (full_c, full_u)[which]
                shard = tx - step if way == 0 else tx + step
                pltpu.make_async_remote_copy(
                    src_ref=(c_ref, u_ref)[which],
                    dst_ref=full.at[slot(shard)],
                    send_sem=gather_send.at[which, way, step - 1],
                    recv_sem=gather_recv.at[which, way, step - 1],
                    device_id=along(1),
                    device_id_type=MESH,
                ).wait_recv()

    def gather_sent(which):
        for step in range(1, n_tx):
            for way in range(2):
                @pl.when(sends(way, step))
                def _():
                    hop(which, way, step).wait_send()

    def ind_copy(offset):
        return pltpu.make_async_remote_copy(
            src_ref=m_ref,
            dst_ref=ind_all.at[tx],
            send_sem=ind_send.at[offset - 1],
            recv_sem=ind_recv.at[offset - 1],
            device_id=along(offset),
            device_id_type=MESH,
        )

    for offset in range(1, n_tx):
        ind_copy(offset).start()
    gather_start(0, 1)
    ind_all[pl.ds(tx, 1)] = m_ref[...][None]
    full_c[slot(tx)] = c_ref[...]
    full_u[slot(tx)] = u_ref[...]
    for offset in range(1, n_tx):
        ind_copy(offset).wait()
    layers = depth // n_tx
    for owner in range(n_tx):
        piece = ind_all[owner].astype(F32).reshape(3, layers, width_x, width_y)
        for layer in range(layers):
            induct[:, owner * layers + layer] = piece[:, layer]

    size_x, size_y = width_x * n_gx, width_y * n_gy
    shape = (depth, width_x, width_y)
    z_pos = lax.broadcasted_iota(jnp.int32, shape, 0).astype(F32)
    x_pos = (gx * width_x + lax.broadcasted_iota(jnp.int32, shape, 1)).astype(F32)
    y_pos = (gy * width_y + lax.broadcasted_iota(jnp.int32, shape, 2)).astype(F32)
    for s in range(sources):
        d_z, d_x, d_y = z_pos - pos_ref[s, 0], x_pos - pos_ref[s, 1], y_pos - pos_ref[s, 2]
        dist = jnp.sqrt(d_z * d_z + d_x * d_x + d_y * d_y)
        primary = jnp.exp(-dist / ((size_x + size_y) / 8.0))
        for comp, weight in enumerate((1.0, 0.5, 0.25)):
            real = (induct[comp] - 1.0) * weight * primary
            resid[s, pl.ds(comp * depth, depth)] = real
            resid[s, pl.ds(half + comp * depth, depth)] = 0.5 * real
    for step in range(2, n_tx):
        gather_arrive(0, step - 1)
        gather_start(0, step)
    gather_arrive(0, n_tx - 1)
    gather_start(1, 1)

    def sum_copy(index, count, offset):
        return pltpu.make_async_remote_copy(
            src_ref=part.at[index, pl.ds(0, count)],
            dst_ref=parts.at[index, rank, pl.ds(0, count)],
            send_sem=sum_send.at[index, offset - 1],
            recv_sem=sum_recv.at[index, offset - 1],
            device_id=peer_of(offset),
            device_id_type=MESH,
        )

    def group_sum(index, count):
        for offset in range(1, group):
            sum_copy(index, count, offset).start()
        parts[index, pl.ds(rank, 1), pl.ds(0, count)] = part[index, pl.ds(0, count)][None]
        for offset in range(1, group):
            sum_copy(index, count, offset).wait()
        return jnp.sum(parts[index, :, pl.ds(0, count)], axis=0)

    def images_inner(index, base, field):
        def body(k, _):
            vector = full_c[k].astype(F32).reshape(tiles, width_x, width_y)
            for s in range(sources):
                product = jnp.sum(vector * field[s], axis=0)
                part[index, pl.ds(base + s * vecs + k, 1)] = jnp.sum(product, axis=0, keepdims=True)
            return 0

        lax.fori_loop(0, vecs, body, 0)

    def inner(index, row, left, right, s):
        product = jnp.sum(left[s] * right[s], axis=0)
        part[index, pl.ds(row, 1)] = jnp.sum(product, axis=0, keepdims=True)

    def spread(value):
        return jnp.broadcast_to(value, (width_x, width_y))

    def combine(out, terms, rows_of, stack, extra=None):
        for s in range(sources):
            for k in range(vecs):
                coef[s, k] = spread(rows_of[s][:, k : k + 1])
        wide = [[spread(c[s]) for s in range(sources)] for _, c in terms]
        wide_extra = [[spread(c[s]) for s in range(sources)] for _, c in extra[1]] if extra else []

        def body(j, _):
            at = pl.ds(pl.multiple_of(j * 16, 16), 16)
            pair = pl.ds(j * 2, 2)
            totals = []
            for s in range(sources):
                value = None
                for (ref, _), w in zip(terms, wide):
                    now = ref[s, pair] * w[s][None]
                    value = now if value is None else value + now
                totals.append(value)
            if extra:
                out2, terms2, keep = extra
                for s in range(sources):
                    value = out2[s, pair] if keep else None
                    for (ref, _), w in zip(terms2, wide_extra):
                        now = ref[s, pair] * w[s][None]
                        value = now if value is None else value + now
                    out2[s, pair] = value
            for k in range(vecs):
                vector = stack[k, at, :].astype(F32).reshape(2, width_x, width_y)
                for s in range(sources):
                    totals[s] = totals[s] + vector * coef[s, k][None]
            for s in range(sources):
                out[s, pair] = totals[s]
            return 0

        lax.fori_loop(0, tiles // 2, body, 0)

    east, west = gx + 1 < n_gx, gx >= 1
    north, south = gy + 1 < n_gy, gy >= 1
    lane2 = lax.broadcasted_iota(jnp.int32, (depth, width_y), 1)
    layer2 = lax.broadcasted_iota(jnp.int32, (depth, width_y), 0)
    layer3 = lax.broadcasted_iota(jnp.int32, shape, 0)
    row3 = lax.broadcasted_iota(jnp.int32, shape, 1)
    lane3 = lax.broadcasted_iota(jnp.int32, shape, 2)
    both = jnp.logical_and
    links = (
        (row_out, 1, row_in, 0, (1, 0), east, west),
        (row_out, 0, row_in, 1, (-1, 0), west, east),
        (col_out, 1, col_in, 0, (0, 1), north, south),
        (col_out, 0, col_in, 1, (0, -1), south, north),
        (col_out, 1, col_in, 2, (-1, 1), both(west, north), both(east, south)),
        (col_out, 0, col_in, 3, (1, -1), both(east, south), both(west, north)),
    )

    def halo_copy(index, number):
        src, which, dst, place, (d_x, d_y), _, _ = links[number]
        return pltpu.make_async_remote_copy(
            src_ref=src.at[index, which],
            dst_ref=dst.at[index, place],
            send_sem=halo_send.at[index, number],
            recv_sem=halo_recv.at[index, number],
            device_id=(gx + d_x, gy + d_y, tx),
            device_id_type=MESH,
        )

    def exchange(index, field):
        lanes = lax.broadcasted_iota(jnp.int32, (tiles, width_x, width_y), 2)
        places = lax.broadcasted_iota(jnp.int32, (tiles, width_x, width_y), 0)
        first = jnp.zeros((width_x, width_y), F32)
        last = jnp.zeros((width_x, width_y), F32)
        for s in range(sources):
            value = field[s]
            here = lanes == places + s * tiles
            first = first + jnp.sum(jnp.where(here, value[:, :, 0:1], 0.0), axis=0)
            last = last + jnp.sum(jnp.where(here, value[:, :, width_y - 1 : width_y], 0.0), axis=0)
            row_out[index, 0, pl.ds(s * tiles, tiles)] = value[:, 0, :]
            row_out[index, 1, pl.ds(s * tiles, tiles)] = value[:, width_x - 1, :]
        col_out[index, 0] = first
        col_out[index, 1] = last
        for number in range(len(links)):
            @pl.when(links[number][5])
            def _():
                halo_copy(index, number).start()
        for number in range(len(links)):
            dst, place, got = links[number][2], links[number][3], links[number][6]

            @pl.when(jnp.logical_not(got))
            def _():
                dst[index, place] = jnp.zeros(dst.shape[2:], F32)

            @pl.when(got)
            def _():
                halo_copy(index, number).wait_recv()

    def apply(index, field, out):
        exchange(index, field)

        def columns(place, at):
            packed = col_in[index, place][None]
            return jnp.sum(jnp.where(lane3 == layer3 + at, packed, 0.0), axis=2, keepdims=True)

        def corner(place, row, at):
            packed = col_in[index, place, row : row + 1]
            return jnp.sum(jnp.where(lane2 == layer2 + at, packed, 0.0), axis=1, keepdims=True)

        def plus_y(f, edge):
            return jnp.where(lane3 == width_y - 1, edge, pltpu.roll(f, width_y - 1, 2))

        def minus_y(f, edge):
            return jnp.where(lane3 == 0, edge, pltpu.roll(f, 1, 2))

        def plus_x(f, row):
            return jnp.where(row3 == width_x - 1, row[:, None, :], pltpu.roll(f, width_x - 1, 1))

        def minus_x(f, row):
            return jnp.where(row3 == 0, row[:, None, :], pltpu.roll(f, 1, 1))

        zero = jnp.zeros((1, width_x, width_y), F32)

        def plus_z(f):
            return jnp.concatenate([f[1:], zero], axis=0)

        def minus_z(f):
            return jnp.concatenate([zero, f[:-1]], axis=0)

        def body(s, _):
            for p in range(2):
                def comp(c):
                    return field[s, pl.ds(p * half + c * depth, depth)]

                def at(c):
                    return s * tiles + p * half + c * depth

                def row(place, c):
                    return row_in[index, place, pl.ds(pl.multiple_of(at(c), 8), depth)]

                e_x, e_y, e_z = comp(0), comp(1), comp(2)
                xp_y = plus_y(e_x, columns(1, at(0)))
                xm_y = minus_y(e_x, columns(0, at(0)))
                t = xp_y - e_x
                hx = row(0, 0)
                hx_up = jnp.where(lane2 == width_y - 1, corner(3, width_x - 1, at(0)), pltpu.roll(hx, width_y - 1, 1))
                dt = t - minus_x(t, hx_up - hx)
                c = e_x - minus_x(e_x, hx)
                a = e_y - minus_y(e_y, columns(0, at(1)))
                hy = row(1, 1)
                hy_down = jnp.where(lane2 == 0, corner(2, 0, at(1)), pltpu.roll(hy, 1, 1))
                da = plus_x(a, hy - hy_down) - a
                y2 = plus_x(e_y, hy) + minus_x(e_y, row(0, 1)) - 2.0 * e_y
                zp_x = plus_x(e_z, row(1, 2))
                zp_y = plus_y(e_z, columns(1, at(2)))
                z2 = zp_x + minus_x(e_z, row(0, 2)) + zp_y + minus_y(e_z, columns(0, at(2))) - 4.0 * e_z
                fx_z = zp_x - e_z
                fy_z = zp_y - e_z
                k_x = da - (xp_y + xm_y + plus_z(e_x) + minus_z(e_x) - 4.0 * e_x) + (fx_z - minus_z(fx_z))
                k_y = (fy_z - minus_z(fy_z)) - (plus_z(e_y) + minus_z(e_y) - 2.0 * e_y) - y2 + dt
                ca = c + a
                k_z = (plus_z(ca) - ca) - z2
                for number, value in enumerate((k_x, k_y, k_z)):
                    cross = induct[number] * field[s, pl.ds((1 - p) * half + number * depth, depth)]
                    value = value - cross if p == 0 else value + cross
                    out[s, pl.ds(p * half + number * depth, depth)] = value
            return 0

        lax.fori_loop(0, sources, body, 0)

    total[...] = jnp.zeros_like(total)

    def gram_body(j, _):
        block = full_c[:, pl.ds(pl.multiple_of(j * 16, 16), 16), :].reshape(vecs * 16, width_y)
        total[...] += lax.dot_general(block, block, (((1,), (1,)), ((), ())), preferred_element_type=F32)
        return 0

    lax.fori_loop(0, rows // 16, gram_body, 0)
    wide = vecs * 16
    same = lax.rem(lax.broadcasted_iota(jnp.int32, (wide, wide), 0), 16) == lax.rem(
        lax.broadcasted_iota(jnp.int32, (wide, wide), 1), 16
    )
    folded = jnp.sum(jnp.where(same, total[...], 0.0).reshape(vecs, 16, wide), axis=1)
    halves = wide // width_y
    for h in range(halves):
        part[0, pl.ds(h * vecs, vecs)] = folded[:, h * width_y : (h + 1) * width_y]
    gram_rows = halves * vecs
    images_inner(0, gram_rows, resid)
    first_sum = group_sum(0, gram_rows + sources * vecs)
    gram = jnp.zeros((vecs, vecs), F32)
    for h in range(halves):
        lane = lax.broadcasted_iota(jnp.int32, (width_y, vecs), 0)
        column = lax.broadcasted_iota(jnp.int32, (width_y, vecs), 1)
        pick = (lax.div(lane, 16) + h * (width_y // 16) == column).astype(F32)
        gram = gram + jnp.dot(
            first_sum[h * vecs : (h + 1) * vecs], pick,
            precision=lax.Precision.HIGHEST, preferred_element_type=F32,
        )
    row_id = lax.broadcasted_iota(jnp.int32, (vecs, vecs), 0)
    eye = (row_id == lax.broadcasted_iota(jnp.int32, (vecs, vecs), 1)).astype(F32)
    wide_row = lax.broadcasted_iota(jnp.int32, (vecs, 2 * vecs), 0)
    system = jnp.concatenate([gram, eye], axis=1)
    for k in range(vecs):
        pivot = system[k : k + 1] / system[k : k + 1, k : k + 1]
        system = jnp.where(wide_row == k, pivot, system - system[:, k : k + 1] * pivot)
    inverse[...] = system[:, vecs:]

    def solve(column):
        answer = jnp.sum(inverse[...] * column, axis=0, keepdims=True)
        flat = jnp.sum(eye * column, axis=0, keepdims=True)
        return answer, jnp.sum(answer * flat, axis=1, keepdims=True)

    start = jnp.sum(first_sum[gram_rows:], axis=1, keepdims=True)
    weights = [solve(start[s * vecs : (s + 1) * vecs])[0] for s in range(sources)]
    one = jnp.ones((1, 1), F32)
    combine(resid, [(resid, [one] * sources)], [-w for w in weights], full_c)

    every = range(sources)
    base = sources * vecs
    for cycle in range(CYCLES):
        index = 2 * cycle
        apply(index, resid, work)
        images_inner(index + 1, 0, work)
        for s in every:
            inner(index + 1, base + 4 * s, resid, resid, s)
            inner(index + 1, base + 4 * s + 1, resid, work, s)
            inner(index + 1, base + 4 * s + 2, work, work, s)
            part[index + 1, pl.ds(base + 4 * s + 3, 1)] = jnp.zeros((1, width_y), F32)
        sums = jnp.sum(group_sum(index + 1, base + 4 * sources), axis=1, keepdims=True)
        state = []
        for s in every:
            def got(i):
                return sums[base + 4 * s + i : base + 4 * s + i + 1]

            beta = jnp.sqrt(got(0) + EPS)
            scale = 1.0 / beta
            raw, quad = solve(sums[s * vecs : (s + 1) * vecs])
            g_0 = raw * scale
            n_00 = got(0) * scale * scale
            h_00 = got(1) * scale * scale
            left = (got(2) - quad) * scale * scale - 2.0 * h_00 * h_00 + h_00 * h_00 * n_00
            left = jnp.maximum(left, 0.0)
            h_10 = jnp.sqrt(left + EPS)
            state.append((beta, scale, g_0, n_00, h_00, left, h_10))
        combine(
            krylov,
            [(work, [v[1] / v[6] for v in state]), (resid, [-v[4] * v[1] / v[6] for v in state])],
            [-v[2] / v[6] for v in state],
            full_c,
        )
        if cycle + 1 < n_tx - 1:
            gather_arrive(1, cycle + 1)
            gather_start(1, cycle + 2)
        apply(index + 1, krylov, work)
        images_inner(index + 2, 0, work)
        for s in every:
            inner(index + 2, base + 4 * s, resid, work, s)
            inner(index + 2, base + 4 * s + 1, krylov, work, s)
            inner(index + 2, base + 4 * s + 2, work, work, s)
            inner(index + 2, base + 4 * s + 3, krylov, krylov, s)
        sums = jnp.sum(group_sum(index + 2, base + 4 * sources), axis=1, keepdims=True)
        in_r, in_v, in_w, in_g, out_r, out_v = [], [], [], [], [], []
        for s in every:
            def got(i):
                return sums[base + 4 * s + i : base + 4 * s + i + 1]

            beta, scale, g_0, n_00, h_00, _, h_10 = state[s]
            g_1, quad = solve(sums[s * vecs : (s + 1) * vecs])
            h_01 = got(0) * scale
            h_11 = got(1)
            n_11 = got(3)
            n_01 = h_00 * (1.0 - n_00) / h_10
            left = (
                got(2) - quad - 2.0 * (h_01 * h_01 + h_11 * h_11)
                + h_01 * h_01 * n_00 + h_11 * h_11 * n_11 + 2.0 * h_01 * h_11 * n_01
            )
            h_21 = jnp.sqrt(jnp.maximum(left, 0.0) + EPS)
            a_00 = h_00 * h_00 + h_10 * h_10
            a_01 = h_00 * h_01 + h_10 * h_11
            a_11 = h_01 * h_01 + h_11 * h_11 + h_21 * h_21
            l_00 = jnp.sqrt(a_00)
            l_10 = a_01 / l_00
            l_11 = jnp.sqrt(a_11 - l_10 * l_10)
            f_0 = beta * h_00 / l_00
            f_1 = (beta * h_01 - l_10 * f_0) / l_11
            y_1 = f_1 / l_11
            y_0 = (f_0 - l_10 * y_1) / l_00
            t_0 = beta - h_00 * y_0 - h_01 * y_1
            t_1 = -(h_10 * y_0 + h_11 * y_1)
            t_2 = -h_21 * y_1
            share = t_2 / h_21
            in_r.append((t_0 - share * h_01) * scale)
            in_v.append(t_1 - share * h_11)
            in_w.append(share)
            in_g.append(-share * g_1)
            out_r.append(y_0 * scale)
            out_v.append(y_1)
            weights[s] = weights[s] - (g_0 * y_0 + g_1 * y_1)
        update = (sol_ref, [(resid, out_r), (krylov, out_v)], cycle > 0)
        combine(resid, [(resid, in_r), (krylov, in_v), (work, in_w)], in_g, full_c, update)

    for step in range(CYCLES + 1, n_tx - 1):
        gather_arrive(1, step)
        gather_start(1, step + 1)
    gather_arrive(1, n_tx - 1)
    combine(sol_ref, [(sol_ref, [one] * sources)], weights, full_u)
    gather_sent(0)
    gather_sent(1)
    for index in range(2 * CYCLES):
        for number in range(len(links)):
            @pl.when(links[number][5])
            def _():
                halo_copy(index, number).wait_send()


def on_device(dims, src_cell, basis, images, induction):
    n_gx, n_gy, n_tx = dims
    per_dev, _, _, depth, width_x, width_y = basis.shape
    sources = src_cell.shape[0]
    size_x, size_y = width_x * n_gx, width_y * n_gy
    rest = src_cell % (size_x * size_y)
    place = jnp.stack([src_cell // (size_x * size_y), rest // size_y, rest % size_y], axis=1)
    tiles = 6 * depth
    rows = tiles * width_x
    vecs = per_dev * n_tx
    group = n_gx * n_gy
    field = (sources, tiles, width_x, width_y)
    ind_rows = 3 * induction.shape[1] * width_x
    most = vecs * 16 // width_y * vecs + sources * vecs
    sums, halos = 2 * CYCLES + 1, 2 * CYCLES
    dma = pltpu.SemaphoreType.DMA
    vmem = pl.BlockSpec(memory_space=pltpu.VMEM)
    out = pl.pallas_call(
        functools.partial(kernel, dims),
        out_shape=(jax.ShapeDtypeStruct(field, F32),) * 2,
        in_specs=[pl.BlockSpec(memory_space=pltpu.SMEM), vmem, vmem, vmem],
        out_specs=(vmem, vmem),
        scratch_shapes=[
            pltpu.VMEM((vecs, rows, width_y), jnp.bfloat16),
            pltpu.VMEM((vecs, rows, width_y), jnp.bfloat16),
            pltpu.VMEM((n_tx, ind_rows, width_y), jnp.bfloat16),
            pltpu.VMEM((3, depth, width_x, width_y), F32),
            pltpu.VMEM(field, F32),
            pltpu.VMEM(field, F32),
            pltpu.VMEM((vecs * 16, vecs * 16), F32),
            pltpu.VMEM((vecs, vecs), F32),
            pltpu.VMEM((sources, vecs, width_x, width_y), F32),
            pltpu.VMEM((8, width_y), F32),
            pltpu.VMEM((sums, most, width_y), F32),
            pltpu.VMEM((sums, group, most, width_y), F32),
            pltpu.VMEM((halos, 2, sources * tiles, width_y), F32),
            pltpu.VMEM((halos, 2, sources * tiles, width_y), F32),
            pltpu.VMEM((halos, 2, width_x, width_y), F32),
            pltpu.VMEM((halos, 4, width_x, width_y), F32),
            dma((2, 2, n_tx - 1)),
            dma((2, 2, n_tx - 1)),
            dma((n_tx - 1,)),
            dma((n_tx - 1,)),
            dma((sums, group - 1)),
            dma((sums, group - 1)),
            dma((halos, 6)),
            dma((halos, 6)),
        ],
        compiler_params=pltpu.CompilerParams(
            collective_id=0, has_side_effects=True, vmem_limit_bytes=48 * 1024 * 1024
        ),
        cost_estimate=pl.CostEstimate(flops=400_000_000, bytes_accessed=2_000_000, transcendentals=20_000),
    )(
        place.astype(F32),
        basis.reshape(per_dev, rows, width_y),
        images.reshape(per_dev, rows, width_y),
        induction.reshape(ind_rows, width_y),
    )
    shape = (sources, 2, 3, depth, width_x, width_y)
    return tuple(o.reshape(shape) for o in out)


def solution(mesh):
    dims = (mesh.shape["gx"], mesh.shape["gy"], mesh.shape["tx"])
    spec = P("tx", None, None, None, "gx", "gy")
    return jax.shard_map(
        functools.partial(on_device, dims),
        mesh=mesh,
        in_specs=(P("tx"), spec, spec, P(None, "tx", "gx", "gy")),
        out_specs=(spec, spec),
        check_vma=False,
    )
```

```python
import functools

import jax
import jax.numpy as jnp
from jax import lax
from jax.experimental import pallas as pl
from jax.experimental.pallas import tpu as pltpu
from jax.sharding import PartitionSpec as P

CYCLES = 2
ARNOLDI = 2
EPS = 1e-06
MESH = pl.DeviceIdType.MESH
F32 = jnp.float32


def kernel(
    dims, pos_ref, u_ref, c_ref, m_ref, sol_ref, res_ref,
    full_c, full_u, ind_all, induct, krylov, work, total, inverse, coef, outer,
    part, parts, row_out, row_in, col_out, col_in,
    img_row_out, img_row_in, img_col_out, img_col_in, row_r, row_v, col_r, col_v,
    own_sem, gather_send, gather_recv, ind_send, ind_recv, sum_send, sum_recv, halo_send, halo_recv,
    img_send, img_recv,
):
    n_gx, n_gy, n_tx = dims
    gx, gy, tx = lax.axis_index("gx"), lax.axis_index("gy"), lax.axis_index("tx")
    group = n_gx * n_gy
    rank = gx * n_gy + gy
    sources = pos_ref.shape[0]
    per_dev = c_ref.shape[0]
    rows = c_ref.shape[1]
    width_y = c_ref.shape[2]
    width_x = 8
    depth = induct.shape[1]
    tiles = rows // width_x
    vecs = full_c.shape[0]
    half = tiles // 2
    resid = res_ref
    chunk = 16 * width_x
    chunks = rows // chunk

    def peer_of(offset):
        other = lax.rem(rank + offset, group)
        return (lax.div(other, n_gy), lax.rem(other, n_gy), tx)

    def along(offset):
        return (gx, gy, lax.rem(tx + offset, n_tx))

    barrier = pltpu.get_barrier_semaphore()
    for offset in range(1, group):
        pl.semaphore_signal(barrier, inc=1, device_id=peer_of(offset), device_id_type=MESH)
    for offset in range(1, n_tx):
        pl.semaphore_signal(barrier, inc=1, device_id=along(offset), device_id_type=MESH)
    pl.semaphore_wait(barrier, group - 1 + n_tx - 1)

    def slot(shard):
        return pl.ds(shard * per_dev, per_dev)

    def rows_at(which, piece):
        return pl.ds(piece * chunk, chunk) if which == 0 else pl.ds(0, rows)

    pieces = (chunks, 1)

    def hop(which, way, step, piece):
        full = (full_c, full_u)[which]
        at = rows_at(which, piece)
        sign = 1 if way == 0 else -1
        shard = tx - sign * (step - 1)
        source = (c_ref, u_ref)[which].at[:, at] if step == 1 else full.at[slot(shard), at]
        return pltpu.make_async_remote_copy(
            src_ref=source,
            dst_ref=full.at[slot(shard), at],
            send_sem=gather_send.at[which, way, step - 1, piece],
            recv_sem=gather_recv.at[which, way, step - 1, piece],
            device_id=(gx, gy, tx + sign),
            device_id_type=MESH,
        )

    def sends(way, step):
        if way == 0:
            return jnp.logical_and(tx + 1 < n_tx, tx - step + 1 >= 0)
        return jnp.logical_and(tx - 1 >= 0, tx + step - 1 < n_tx)

    def receives(way, step):
        return tx - step >= 0 if way == 0 else tx + step < n_tx

    def gather_start(which, step, piece):
        for way in range(2):
            @pl.when(sends(way, step))
            def _():
                hop(which, way, step, piece).start()

    def gather_arrive(which, step, piece, then=False):
        for way in range(2):
            @pl.when(receives(way, step))
            def _():
                full = (full_c, full_u)[which]
                at = rows_at(which, piece)
                shard = tx - step if way == 0 else tx + step
                pltpu.make_async_remote_copy(
                    src_ref=full.at[slot(shard), at],
                    dst_ref=full.at[slot(shard), at],
                    send_sem=gather_send.at[which, way, step - 1, piece],
                    recv_sem=gather_recv.at[which, way, step - 1, piece],
                    device_id=along(1),
                    device_id_type=MESH,
                ).wait_recv()

            if then:
                @pl.when(sends(way, step + 1))
                def _():
                    hop(which, way, step + 1, piece).start()

    def gather_sent(which):
        for piece in range(pieces[which]):
            for step in range(1, n_tx):
                for way in range(2):
                    @pl.when(sends(way, step))
                    def _():
                        hop(which, way, step, piece).wait_send()

    own = [
        pltpu.make_async_copy(ref, full.at[slot(tx)], own_sem.at[number])
        for number, (ref, full) in enumerate(((c_ref, full_c), (u_ref, full_u)))
    ]

    def ind_copy(offset):
        return pltpu.make_async_remote_copy(
            src_ref=m_ref,
            dst_ref=ind_all.at[tx],
            send_sem=ind_send.at[offset - 1],
            recv_sem=ind_recv.at[offset - 1],
            device_id=along(offset),
            device_id_type=MESH,
        )

    for offset in range(1, n_tx):
        ind_copy(offset).start()
    gather_start(0, 1, 0)
    gather_start(0, 1, 1)
    for copy in own:
        copy.start()
    ind_all[pl.ds(tx, 1)] = m_ref[...][None]
    for offset in range(1, n_tx):
        ind_copy(offset).wait()
    layers = depth // n_tx
    for owner in range(n_tx):
        piece = ind_all[owner].astype(F32).reshape(3, layers, width_x, width_y)
        for layer in range(layers):
            induct[:, owner * layers + layer] = piece[:, layer]

    size_x, size_y = width_x * n_gx, width_y * n_gy
    shape = (depth, width_x, width_y)
    z_pos = lax.broadcasted_iota(jnp.int32, shape, 0).astype(F32)
    x_pos = (gx * width_x + lax.broadcasted_iota(jnp.int32, shape, 1)).astype(F32)
    y_pos = (gy * width_y + lax.broadcasted_iota(jnp.int32, shape, 2)).astype(F32)
    for s in range(sources):
        cell = pos_ref[s]
        rest = lax.rem(cell, size_x * size_y)
        d_z = z_pos - lax.div(cell, size_x * size_y).astype(F32)
        d_x = x_pos - lax.div(rest, size_y).astype(F32)
        d_y = y_pos - lax.rem(rest, size_y).astype(F32)
        dist = jnp.sqrt(d_z * d_z + d_x * d_x + d_y * d_y)
        primary = jnp.exp(-dist / ((size_x + size_y) / 8.0))
        for comp, weight in enumerate((1.0, 0.5, 0.25)):
            real = (induct[comp] - 1.0) * weight * primary
            resid[s, pl.ds(comp * depth, depth)] = real
            resid[s, pl.ds(half + comp * depth, depth)] = 0.5 * real

    def sum_copy(index, count, offset):
        return pltpu.make_async_remote_copy(
            src_ref=part.at[index, pl.ds(0, count)],
            dst_ref=parts.at[index, rank, pl.ds(0, count)],
            send_sem=sum_send.at[index, offset - 1],
            recv_sem=sum_recv.at[index, offset - 1],
            device_id=peer_of(offset),
            device_id_type=MESH,
        )

    def group_send(index, count):
        for offset in range(1, group):
            sum_copy(index, count, offset).start()
        parts[index, pl.ds(rank, 1), pl.ds(0, count)] = part[index, pl.ds(0, count)][None]

    def group_sum(index, count):
        for offset in range(1, group):
            sum_copy(index, count, offset).wait()
        return jnp.sum(parts[index, :, pl.ds(0, count)], axis=0)

    def images_inner(index, base, field, piece=None):
        size = tiles if piece is None else 16
        at = 0 if piece is None else piece * 16

        def body(k, _):
            vector = full_c[k, pl.ds(at * width_x, size * width_x)]
            vector = vector.astype(F32).reshape(size, width_x, width_y)
            for s in range(sources):
                product = jnp.sum(vector * field[s, pl.ds(at, size)], axis=0)
                product = jnp.sum(product, axis=0, keepdims=True)
                place = pl.ds(base + s * vecs + k, 1)
                if piece:
                    product = product + part[index, place]
                part[index, place] = product
            return 0

        lax.fori_loop(0, vecs, body, 0)

    def inner(index, row, left, right, s):
        product = jnp.sum(left[s] * right[s], axis=0)
        part[index, pl.ds(row, 1)] = jnp.sum(product, axis=0, keepdims=True)

    def spread(value):
        return jnp.broadcast_to(value, (width_x, width_y))

    def combine(out, terms, rows_of, stack, extra=None):
        for s in range(sources):
            for k in range(vecs):
                coef[s, k] = spread(rows_of[s][:, k : k + 1])
        wide = [[spread(c[s]) for s in range(sources)] for _, c in terms]
        wide_extra = [[spread(c[s]) for s in range(sources)] for _, c in extra[1]] if extra else []

        def body(j, _):
            at = pl.ds(pl.multiple_of(j * 16, 16), 16)
            pair = pl.ds(j * 2, 2)
            totals = []
            for s in range(sources):
                value = None
                for (ref, _), w in zip(terms, wide):
                    now = ref[s, pair] * w[s][None]
                    value = now if value is None else value + now
                totals.append(value)
            if extra:
                out2, terms2, keep = extra
                for s in range(sources):
                    value = out2[s, pair] if keep else None
                    for (ref, _), w in zip(terms2, wide_extra):
                        now = ref[s, pair] * w[s][None]
                        value = now if value is None else value + now
                    out2[s, pair] = value
            for k in range(vecs):
                vector = stack[k, at, :].astype(F32).reshape(2, width_x, width_y)
                for s in range(sources):
                    totals[s] = totals[s] + vector * coef[s, k][None]
            for s in range(sources):
                out[s, pair] = totals[s]
            return 0

        lax.fori_loop(0, tiles // 2, body, 0)

    east, west = gx + 1 < n_gx, gx >= 1
    north, south = gy + 1 < n_gy, gy >= 1
    lane2 = lax.broadcasted_iota(jnp.int32, (depth, width_y), 1)
    layer2 = lax.broadcasted_iota(jnp.int32, (depth, width_y), 0)
    layer3 = lax.broadcasted_iota(jnp.int32, shape, 0)
    row3 = lax.broadcasted_iota(jnp.int32, shape, 1)
    lane3 = lax.broadcasted_iota(jnp.int32, shape, 2)
    both = jnp.logical_and
    links = (
        (row_out, 1, row_in, 0, (1, 0), east, west),
        (row_out, 0, row_in, 1, (-1, 0), west, east),
        (col_out, 1, col_in, 0, (0, 1), north, south),
        (col_out, 0, col_in, 1, (0, -1), south, north),
        (col_out, 1, col_in, 2, (-1, 1), both(west, north), both(east, south)),
        (col_out, 0, col_in, 3, (1, -1), both(east, south), both(west, north)),
    )

    def halo_copy(index, number):
        src, which, dst, place, (d_x, d_y), _, _ = links[number]
        return pltpu.make_async_remote_copy(
            src_ref=src.at[index, which],
            dst_ref=dst.at[index, place],
            send_sem=halo_send.at[index, number],
            recv_sem=halo_recv.at[index, number],
            device_id=(gx + d_x, gy + d_y, tx),
            device_id_type=MESH,
        )

    lanes = lax.broadcasted_iota(jnp.int32, (tiles, width_x, width_y), 2)
    places = lax.broadcasted_iota(jnp.int32, (tiles, width_x, width_y), 0)

    def exchange_start(index, field):
        first = jnp.zeros((width_x, width_y), F32)
        last = jnp.zeros((width_x, width_y), F32)
        for s in range(sources):
            value = field[s]
            here = lanes == places + s * tiles
            first = first + jnp.sum(jnp.where(here, value[:, :, 0:1], 0.0), axis=0)
            last = last + jnp.sum(jnp.where(here, value[:, :, width_y - 1 : width_y], 0.0), axis=0)
            row_out[index, 0, pl.ds(s * tiles, tiles)] = value[:, 0, :]
            row_out[index, 1, pl.ds(s * tiles, tiles)] = value[:, width_x - 1, :]
        col_out[index, 0] = first
        col_out[index, 1] = last
        for number in range(len(links)):
            @pl.when(links[number][5])
            def _():
                halo_copy(index, number).start()

    def exchange_wait(index):
        for number in range(len(links)):
            dst, place, got = links[number][2], links[number][3], links[number][6]

            @pl.when(jnp.logical_not(got))
            def _():
                dst[index, place] = jnp.zeros(dst.shape[2:], F32)

            @pl.when(got)
            def _():
                halo_copy(index, number).wait_recv()

    def image_copy(number, piece):
        _, which, _, place, (d_x, d_y), _, _ = links[number]
        if number < 2:
            src, dst, sem = img_row_out.at[which, piece], img_row_in.at[place, piece], number * chunks + piece
        else:
            src, dst, sem = img_col_out.at[which], img_col_in.at[place], 2 * chunks + number - 2
        return pltpu.make_async_remote_copy(
            src_ref=src,
            dst_ref=dst,
            send_sem=img_send.at[sem],
            recv_sem=img_recv.at[sem],
            device_id=(gx + d_x, gy + d_y, tx),
            device_id_type=MESH,
        )

    image_copies = [(number, piece) for number in range(2) for piece in range(chunks)]
    image_copies += [(number, 0) for number in range(2, len(links))]

    def image_start(number, piece):
        @pl.when(links[number][5])
        def _():
            image_copy(number, piece).start()

    def image_pack(piece):
        size = (16, width_x, width_y)
        lane = lax.broadcasted_iota(jnp.int32, size, 2)
        tile = lax.broadcasted_iota(jnp.int32, size, 0) + piece * 16
        here = lane == tile
        for s in range(1, sources):
            here = jnp.logical_or(here, lane == tile + s * tiles)

        def body(k, _):
            value = full_c[k, pl.ds(piece * chunk, chunk)].astype(F32).reshape(size)
            for side, (row, col) in enumerate(((0, 0), (width_x - 1, width_y - 1))):
                img_row_out[side, piece, pl.ds(pl.multiple_of(k * 16, 16), 16)] = value[:, row, :]
                column = jnp.sum(jnp.where(here, value[:, :, col : col + 1], 0.0), axis=0)
                if piece:
                    column = column + img_col_out[side, k]
                img_col_out[side, k] = column
            return 0

        lax.fori_loop(0, vecs, body, 0)
        for number in range(2):
            image_start(number, piece)

    def image_wait():
        for number, piece in image_copies:
            place, got = links[number][3], links[number][6]

            @pl.when(jnp.logical_not(got))
            def _():
                if number < 2:
                    img_row_in[place, piece] = jnp.zeros(img_row_in.shape[2:], F32)
                else:
                    img_col_in[place] = jnp.zeros(img_col_in.shape[1:], F32)

            @pl.when(got)
            def _():
                image_copy(number, piece).wait_recv()

    def by_lane(values):
        lane = lax.broadcasted_iota(jnp.int32, (width_x, width_y), 1)
        result = values[0]
        for s in range(1, sources):
            result = jnp.where(lane >= s * tiles, values[s], result)
        return result

    def combine_halo(row, col, terms):
        wide = [[spread(c[s]) for s in range(sources)] for _, _, c in terms]

        def body(i, _):
            place, piece = lax.div(i, chunks), lax.rem(i, chunks)
            totals = []
            for s in range(sources):
                at = pl.ds(pl.multiple_of(s * tiles + piece * 16, 8), 16)
                value = None
                for (ref, _, _), w in zip(terms, wide):
                    now = ref[place, at].reshape(2, width_x, width_y) * w[s][None]
                    value = now if value is None else value + now
                totals.append(value)
            for k in range(vecs):
                vector = img_row_in[place, piece, pl.ds(k * 16, 16)].reshape(2, width_x, width_y)
                for s in range(sources):
                    totals[s] = totals[s] + vector * coef[s, k][None]
            for s in range(sources):
                at = pl.ds(pl.multiple_of(s * tiles + piece * 16, 8), 16)
                row[place, at] = totals[s].reshape(16, width_y)
            return 0

        lax.fori_loop(0, 2 * chunks, body, 0)
        values = [None] * 4
        for (_, ref, _), w in zip(terms, wide):
            scale = by_lane(w)
            for place in range(4):
                now = ref[place] * scale
                values[place] = now if values[place] is None else values[place] + now
        for k in range(vecs):
            scale = by_lane([coef[s, k] for s in range(sources)])
            for place in range(4):
                values[place] = values[place] + img_col_in[place, k] * scale
        for place in range(4):
            col[place] = values[place]

    def apply(field, row_halo, col_halo, out):
        def columns(place, at):
            packed = col_halo[place][None]
            return jnp.sum(jnp.where(lane3 == layer3 + at, packed, 0.0), axis=2, keepdims=True)

        def corner(place, row, at):
            packed = col_halo[place, row : row + 1]
            return jnp.sum(jnp.where(lane2 == layer2 + at, packed, 0.0), axis=1, keepdims=True)

        def plus_y(f, edge):
            return jnp.where(lane3 == width_y - 1, edge, pltpu.roll(f, width_y - 1, 2))

        def minus_y(f, edge):
            return jnp.where(lane3 == 0, edge, pltpu.roll(f, 1, 2))

        def plus_x(f, row):
            return jnp.where(row3 == width_x - 1, row[:, None, :], pltpu.roll(f, width_x - 1, 1))

        def minus_x(f, row):
            return jnp.where(row3 == 0, row[:, None, :], pltpu.roll(f, 1, 1))

        zero = jnp.zeros((1, width_x, width_y), F32)

        def plus_z(f):
            return jnp.concatenate([f[1:], zero], axis=0)

        def minus_z(f):
            return jnp.concatenate([zero, f[:-1]], axis=0)

        def body(s, _):
            for p in range(2):
                def comp(c):
                    return field[s, pl.ds(p * half + c * depth, depth)]

                def at(c):
                    return s * tiles + p * half + c * depth

                def row(place, c):
                    return row_halo[place, pl.ds(pl.multiple_of(at(c), 8), depth)]

                e_x, e_y, e_z = comp(0), comp(1), comp(2)
                xp_y = plus_y(e_x, columns(1, at(0)))
                xm_y = minus_y(e_x, columns(0, at(0)))
                t = xp_y - e_x
                hx = row(0, 0)
                hx_up = jnp.where(lane2 == width_y - 1, corner(3, width_x - 1, at(0)), pltpu.roll(hx, width_y - 1, 1))
                dt = t - minus_x(t, hx_up - hx)
                c = e_x - minus_x(e_x, hx)
                a = e_y - minus_y(e_y, columns(0, at(1)))
                hy = row(1, 1)
                hy_down = jnp.where(lane2 == 0, corner(2, 0, at(1)), pltpu.roll(hy, 1, 1))
                da = plus_x(a, hy - hy_down) - a
                y2 = plus_x(e_y, hy) + minus_x(e_y, row(0, 1)) - 2.0 * e_y
                zp_x = plus_x(e_z, row(1, 2))
                zp_y = plus_y(e_z, columns(1, at(2)))
                z2 = zp_x + minus_x(e_z, row(0, 2)) + zp_y + minus_y(e_z, columns(0, at(2))) - 4.0 * e_z
                fx_z = zp_x - e_z
                fy_z = zp_y - e_z
                k_x = da - (xp_y + xm_y + plus_z(e_x) + minus_z(e_x) - 4.0 * e_x) + (fx_z - minus_z(fx_z))
                k_y = (fy_z - minus_z(fy_z)) - (plus_z(e_y) + minus_z(e_y) - 2.0 * e_y) - y2 + dt
                ca = c + a
                k_z = (plus_z(ca) - ca) - z2
                for number, value in enumerate((k_x, k_y, k_z)):
                    cross = induct[number] * field[s, pl.ds((1 - p) * half + number * depth, depth)]
                    value = value - cross if p == 0 else value + cross
                    out[s, pl.ds(p * half + number * depth, depth)] = value
            return 0

        lax.fori_loop(0, sources, body, 0)

    exchange_start(0, resid)
    total[...] = jnp.zeros_like(total)

    def gram_body(j, _):
        block = full_c[:, pl.ds(pl.multiple_of(j * 16, 16), 16), :].reshape(vecs * 16, width_y)
        total[...] += lax.dot_general(block, block, (((1,), (1,)), ((), ())), preferred_element_type=F32)
        return 0

    wide = vecs * 16
    halves = wide // width_y
    gram_rows = halves * vecs
    own[0].wait()
    for piece in range(chunks):
        for step in range(1, n_tx - 1):
            gather_arrive(0, step, piece, True)
        if piece + 2 < chunks:
            gather_start(0, 1, piece + 2)
        elif piece + 1 == chunks:
            gather_start(1, 1, 0)
        gather_arrive(0, n_tx - 1, piece)
        lax.fori_loop(piece * (chunk // 16), (piece + 1) * (chunk // 16), gram_body, 0)
        images_inner(0, gram_rows, resid, piece)
        if piece + 1 < chunks:
            image_pack(piece)
    same = lax.rem(lax.broadcasted_iota(jnp.int32, (wide, wide), 0), 16) == lax.rem(
        lax.broadcasted_iota(jnp.int32, (wide, wide), 1), 16
    )
    folded = jnp.sum(jnp.where(same, total[...], 0.0).reshape(vecs, 16, wide), axis=1)
    for h in range(halves):
        part[0, pl.ds(h * vecs, vecs)] = folded[:, h * width_y : (h + 1) * width_y]
    group_send(0, gram_rows + sources * vecs)
    image_pack(chunks - 1)
    for number in range(2, len(links)):
        image_start(number, 0)
    first_sum = group_sum(0, gram_rows + sources * vecs)
    gram = jnp.zeros((vecs, vecs), F32)
    for h in range(halves):
        lane = lax.broadcasted_iota(jnp.int32, (width_y, vecs), 0)
        column = lax.broadcasted_iota(jnp.int32, (width_y, vecs), 1)
        pick = (lax.div(lane, 16) + h * (width_y // 16) == column).astype(F32)
        gram = gram + jnp.dot(
            first_sum[h * vecs : (h + 1) * vecs], pick,
            precision=lax.Precision.HIGHEST, preferred_element_type=F32,
        )
    row_id = lax.broadcasted_iota(jnp.int32, (vecs, vecs), 0)
    eye = (row_id == lax.broadcasted_iota(jnp.int32, (vecs, vecs), 1)).astype(F32)
    wide_row = lax.broadcasted_iota(jnp.int32, (vecs, 2 * vecs), 0)
    system = jnp.concatenate([gram, eye], axis=1)
    for k in range(vecs):
        pivot = system[k : k + 1] / system[k : k + 1, k : k + 1]
        system = jnp.where(wide_row == k, pivot, system - system[:, k : k + 1] * pivot)
    inverse[...] = system[:, vecs:]

    def solve(column):
        answer = jnp.sum(inverse[...] * column, axis=0, keepdims=True)
        flat = jnp.sum(eye * column, axis=0, keepdims=True)
        return answer, jnp.sum(answer * flat, axis=1, keepdims=True)

    start = jnp.sum(first_sum[gram_rows:], axis=1, keepdims=True)
    weights = [solve(start[s * vecs : (s + 1) * vecs])[0] for s in range(sources)]
    one = jnp.ones((1, 1), F32)
    combine(resid, [(resid, [one] * sources)], [-w for w in weights], full_c)
    exchange_wait(0)
    image_wait()
    combine_halo(row_r, col_r, [(row_in.at[0], col_in.at[0], [one] * sources)])

    every = range(sources)
    base = sources * vecs
    for cycle in range(CYCLES):
        index = 2 * cycle
        apply(resid, row_r, col_r, work)
        exchange_start(index + 1, work)
        images_inner(index + 1, 0, work)
        for s in every:
            inner(index + 1, base + 4 * s, resid, resid, s)
            inner(index + 1, base + 4 * s + 1, resid, work, s)
            inner(index + 1, base + 4 * s + 2, work, work, s)
            part[index + 1, pl.ds(base + 4 * s + 3, 1)] = jnp.zeros((1, width_y), F32)
        group_send(index + 1, base + 4 * sources)
        sums = jnp.sum(group_sum(index + 1, base + 4 * sources), axis=1, keepdims=True)
        state = []
        for s in every:
            def got(i):
                return sums[base + 4 * s + i : base + 4 * s + i + 1]

            beta = jnp.sqrt(got(0) + EPS)
            scale = 1.0 / beta
            raw, quad = solve(sums[s * vecs : (s + 1) * vecs])
            g_0 = raw * scale
            n_00 = got(0) * scale * scale
            h_00 = got(1) * scale * scale
            left = (got(2) - quad) * scale * scale - 2.0 * h_00 * h_00 + h_00 * h_00 * n_00
            left = jnp.maximum(left, 0.0)
            h_10 = jnp.sqrt(left + EPS)
            state.append((beta, scale, g_0, n_00, h_00, left, h_10))
        of_w = [v[1] / v[6] for v in state]
        of_r = [-v[4] * v[1] / v[6] for v in state]
        combine(krylov, [(work, of_w), (resid, of_r)], [-v[2] / v[6] for v in state], full_c)
        exchange_wait(index + 1)
        now = (row_in.at[index + 1], col_in.at[index + 1])
        combine_halo(row_v, col_v, [now + (of_w,), (row_r, col_r, of_r)])
        if cycle + 1 < n_tx - 1:
            gather_arrive(1, cycle + 1, 0, True)
        apply(krylov, row_v, col_v, work)
        if cycle + 1 < CYCLES:
            exchange_start(index + 2, work)
        images_inner(index + 2, 0, work)
        for s in every:
            inner(index + 2, base + 4 * s, resid, work, s)
            inner(index + 2, base + 4 * s + 1, krylov, work, s)
            inner(index + 2, base + 4 * s + 2, work, work, s)
            inner(index + 2, base + 4 * s + 3, krylov, krylov, s)
        group_send(index + 2, base + 4 * sources)
        sums = jnp.sum(group_sum(index + 2, base + 4 * sources), axis=1, keepdims=True)
        in_r, in_v, in_w, in_g, out_r, out_v = [], [], [], [], [], []
        for s in every:
            def got(i):
                return sums[base + 4 * s + i : base + 4 * s + i + 1]

            beta, scale, g_0, n_00, h_00, _, h_10 = state[s]
            g_1, quad = solve(sums[s * vecs : (s + 1) * vecs])
            h_01 = got(0) * scale
            h_11 = got(1)
            n_11 = got(3)
            n_01 = h_00 * (1.0 - n_00) / h_10
            left = (
                got(2) - quad - 2.0 * (h_01 * h_01 + h_11 * h_11)
                + h_01 * h_01 * n_00 + h_11 * h_11 * n_11 + 2.0 * h_01 * h_11 * n_01
            )
            h_21 = jnp.sqrt(jnp.maximum(left, 0.0) + EPS)
            a_00 = h_00 * h_00 + h_10 * h_10
            a_01 = h_00 * h_01 + h_10 * h_11
            a_11 = h_01 * h_01 + h_11 * h_11 + h_21 * h_21
            l_00 = jnp.sqrt(a_00)
            l_10 = a_01 / l_00
            l_11 = jnp.sqrt(a_11 - l_10 * l_10)
            f_0 = beta * h_00 / l_00
            f_1 = (beta * h_01 - l_10 * f_0) / l_11
            y_1 = f_1 / l_11
            y_0 = (f_0 - l_10 * y_1) / l_00
            t_0 = beta - h_00 * y_0 - h_01 * y_1
            t_1 = -(h_10 * y_0 + h_11 * y_1)
            t_2 = -h_21 * y_1
            share = t_2 / h_21
            in_r.append((t_0 - share * h_01) * scale)
            in_v.append(t_1 - share * h_11)
            in_w.append(share)
            in_g.append(-share * g_1)
            out_r.append(y_0 * scale)
            out_v.append(y_1)
            weights[s] = weights[s] - (g_0 * y_0 + g_1 * y_1)
        update = (sol_ref, [(resid, out_r), (krylov, out_v)], cycle > 0)
        combine(resid, [(resid, in_r), (krylov, in_v), (work, in_w)], in_g, full_c, update)
        if cycle + 1 < CYCLES:
            exchange_wait(index + 2)
            now = (row_in.at[index + 2], col_in.at[index + 2])
            combine_halo(row_r, col_r, [(row_r, col_r, in_r), (row_v, col_v, in_v), now + (in_w,)])

    for step in range(CYCLES + 1, n_tx - 1):
        gather_arrive(1, step, 0, True)
    gather_arrive(1, n_tx - 1, 0)
    own[1].wait()
    combine(sol_ref, [(sol_ref, [one] * sources)], weights, full_u)
    gather_sent(0)
    gather_sent(1)
    for index in range(2 * CYCLES):
        for number in range(len(links)):
            @pl.when(links[number][5])
            def _():
                halo_copy(index, number).wait_send()
    for number, piece in image_copies:
        @pl.when(links[number][5])
        def _():
            image_copy(number, piece).wait_send()


def on_device(dims, src_cell, basis, images, induction):
    n_gx, n_gy, n_tx = dims
    per_dev, _, _, depth, width_x, width_y = basis.shape
    sources = src_cell.shape[0]
    tiles = 6 * depth
    rows = tiles * width_x
    vecs = per_dev * n_tx
    group = n_gx * n_gy
    field = (sources, tiles, width_x, width_y)
    ind_rows = 3 * induction.shape[1] * width_x
    most = vecs * 16 // width_y * vecs + sources * vecs
    sums, halos = 2 * CYCLES + 1, 2 * CYCLES
    dma = pltpu.SemaphoreType.DMA
    vmem = pl.BlockSpec(memory_space=pltpu.VMEM)
    hbm = pl.BlockSpec(memory_space=pl.ANY)
    chunks = tiles // 16
    out = pl.pallas_call(
        functools.partial(kernel, dims),
        out_shape=(jax.ShapeDtypeStruct(field, F32),) * 2,
        in_specs=[pl.BlockSpec(memory_space=pltpu.SMEM), hbm, hbm, vmem],
        out_specs=(vmem, vmem),
        scratch_shapes=[
            pltpu.VMEM((vecs, rows, width_y), jnp.bfloat16),
            pltpu.VMEM((vecs, rows, width_y), jnp.bfloat16),
            pltpu.VMEM((n_tx, ind_rows, width_y), jnp.bfloat16),
            pltpu.VMEM((3, depth, width_x, width_y), F32),
            pltpu.VMEM(field, F32),
            pltpu.VMEM(field, F32),
            pltpu.VMEM((vecs * 16, vecs * 16), F32),
            pltpu.VMEM((vecs, vecs), F32),
            pltpu.VMEM((sources, vecs, width_x, width_y), F32),
            pltpu.VMEM((8, width_y), F32),
            pltpu.VMEM((sums, most, width_y), F32),
            pltpu.VMEM((sums, group, most, width_y), F32),
            pltpu.VMEM((halos, 2, sources * tiles, width_y), F32),
            pltpu.VMEM((halos, 2, sources * tiles, width_y), F32),
            pltpu.VMEM((halos, 2, width_x, width_y), F32),
            pltpu.VMEM((halos, 4, width_x, width_y), F32),
            pltpu.VMEM((2, chunks, vecs * 16, width_y), F32),
            pltpu.VMEM((2, chunks, vecs * 16, width_y), F32),
            pltpu.VMEM((2, vecs, width_x, width_y), F32),
            pltpu.VMEM((4, vecs, width_x, width_y), F32),
            pltpu.VMEM((2, sources * tiles, width_y), F32),
            pltpu.VMEM((2, sources * tiles, width_y), F32),
            pltpu.VMEM((4, width_x, width_y), F32),
            pltpu.VMEM((4, width_x, width_y), F32),
            dma((2,)),
            dma((2, 2, n_tx - 1, chunks)),
            dma((2, 2, n_tx - 1, chunks)),
            dma((n_tx - 1,)),
            dma((n_tx - 1,)),
            dma((sums, group - 1)),
            dma((sums, group - 1)),
            dma((halos, 6)),
            dma((halos, 6)),
            dma((2 * chunks + 4,)),
            dma((2 * chunks + 4,)),
        ],
        compiler_params=pltpu.CompilerParams(
            collective_id=0, has_side_effects=True, vmem_limit_bytes=48 * 1024 * 1024
        ),
        cost_estimate=pl.CostEstimate(flops=400_000_000, bytes_accessed=2_000_000, transcendentals=20_000),
    )(
        src_cell,
        basis.reshape(per_dev, rows, width_y),
        images.reshape(per_dev, rows, width_y),
        induction.reshape(ind_rows, width_y),
    )
    shape = (sources, 2, 3, depth, width_x, width_y)
    return tuple(o.reshape(shape) for o in out)


def solution(mesh):
    dims = (mesh.shape["gx"], mesh.shape["gy"], mesh.shape["tx"])
    spec = P("tx", None, None, None, "gx", "gy")
    return jax.shard_map(
        functools.partial(on_device, dims),
        mesh=mesh,
        in_specs=(P("tx"), spec, spec, P(None, "tx", "gx", "gy")),
        out_specs=(spec, spec),
        check_vma=False,
    )
```

```python
import functools

import jax
import jax.numpy as jnp
from jax import lax
from jax.experimental import pallas as pl
from jax.experimental.pallas import tpu as pltpu
from jax.sharding import PartitionSpec as P

CYCLES = 2
ARNOLDI = 2
EPS = 1e-06
MESH = pl.DeviceIdType.MESH
F32 = jnp.float32


def kernel(
    dims, pos_ref, u_ref, c_ref, m_ref, sol_ref, res_ref,
    full_c, full_u, ind_all, induct, krylov, work, total, inverse, coef,
    part, parts, row_out, row_in, col_out, col_in,
    img_row_out, img_row_in, img_col_out, img_col_in, row_r, row_v, col_r, col_v,
    own_sem, gather_send, gather_recv, ind_send, ind_recv, sum_send, sum_recv, halo_send, halo_recv,
    img_send, img_recv,
):
    n_gx, n_gy, n_tx = dims
    gx, gy, tx = lax.axis_index("gx"), lax.axis_index("gy"), lax.axis_index("tx")
    group = n_gx * n_gy
    rank = gx * n_gy + gy
    sources = pos_ref.shape[0]
    per_dev = c_ref.shape[0]
    rows = c_ref.shape[1]
    width_y = c_ref.shape[2]
    width_x = 8
    depth = induct.shape[1]
    tiles = rows // width_x
    vecs = full_c.shape[0]
    half = tiles // 2
    resid = res_ref
    chunk = 16 * width_x
    chunks = rows // chunk

    def peer_of(offset):
        other = lax.rem(rank + offset, group)
        return (lax.div(other, n_gy), lax.rem(other, n_gy), tx)

    def along(offset):
        return (gx, gy, lax.rem(tx + offset, n_tx))

    barrier = pltpu.get_barrier_semaphore()
    for offset in range(1, group):
        pl.semaphore_signal(barrier, inc=1, device_id=peer_of(offset), device_id_type=MESH)
    for offset in range(1, n_tx):
        pl.semaphore_signal(barrier, inc=1, device_id=along(offset), device_id_type=MESH)
    pl.semaphore_wait(barrier, group - 1 + n_tx - 1)

    def slot(shard):
        return pl.ds(shard * per_dev, per_dev)

    def rows_at(which, piece):
        return pl.ds(piece * chunk, chunk) if which == 0 else pl.ds(0, rows)

    pieces = (chunks, 1)

    def hop(which, way, step, piece):
        full = (full_c, full_u)[which]
        at = rows_at(which, piece)
        sign = 1 if way == 0 else -1
        shard = tx - sign * (step - 1)
        source = (c_ref, u_ref)[which].at[:, at] if step == 1 else full.at[slot(shard), at]
        return pltpu.make_async_remote_copy(
            src_ref=source,
            dst_ref=full.at[slot(shard), at],
            send_sem=gather_send.at[which, way, step - 1, piece],
            recv_sem=gather_recv.at[which, way, step - 1, piece],
            device_id=(gx, gy, tx + sign),
            device_id_type=MESH,
        )

    def sends(way, step):
        if way == 0:
            return jnp.logical_and(tx + 1 < n_tx, tx - step + 1 >= 0)
        return jnp.logical_and(tx - 1 >= 0, tx + step - 1 < n_tx)

    def receives(way, step):
        return tx - step >= 0 if way == 0 else tx + step < n_tx

    def gather_start(which, step, piece):
        for way in range(2):
            @pl.when(sends(way, step))
            def _():
                hop(which, way, step, piece).start()

    def gather_arrive(which, step, piece, then=False):
        for way in range(2):
            @pl.when(receives(way, step))
            def _():
                full = (full_c, full_u)[which]
                at = rows_at(which, piece)
                shard = tx - step if way == 0 else tx + step
                pltpu.make_async_remote_copy(
                    src_ref=full.at[slot(shard), at],
                    dst_ref=full.at[slot(shard), at],
                    send_sem=gather_send.at[which, way, step - 1, piece],
                    recv_sem=gather_recv.at[which, way, step - 1, piece],
                    device_id=along(1),
                    device_id_type=MESH,
                ).wait_recv()

            if then:
                @pl.when(sends(way, step + 1))
                def _():
                    hop(which, way, step + 1, piece).start()

    def gather_sent(which):
        for piece in range(pieces[which]):
            for step in range(1, n_tx):
                for way in range(2):
                    @pl.when(sends(way, step))
                    def _():
                        hop(which, way, step, piece).wait_send()

    own = [
        pltpu.make_async_copy(ref, full.at[slot(tx)], own_sem.at[number])
        for number, (ref, full) in enumerate(((c_ref, full_c), (u_ref, full_u)))
    ]

    def ind_copy(offset):
        return pltpu.make_async_remote_copy(
            src_ref=m_ref,
            dst_ref=ind_all.at[tx],
            send_sem=ind_send.at[offset - 1],
            recv_sem=ind_recv.at[offset - 1],
            device_id=along(offset),
            device_id_type=MESH,
        )

    for offset in range(1, n_tx):
        ind_copy(offset).start()
    gather_start(0, 1, 0)
    gather_start(0, 1, 1)
    for copy in own:
        copy.start()
    ind_all[pl.ds(tx, 1)] = m_ref[...][None]
    for offset in range(1, n_tx):
        ind_copy(offset).wait()
    layers = depth // n_tx
    for owner in range(n_tx):
        piece = ind_all[owner].astype(F32).reshape(3, layers, width_x, width_y)
        for layer in range(layers):
            induct[:, owner * layers + layer] = piece[:, layer]

    size_x, size_y = width_x * n_gx, width_y * n_gy
    shape = (depth, width_x, width_y)
    z_pos = lax.broadcasted_iota(jnp.int32, shape, 0).astype(F32)
    x_pos = (gx * width_x + lax.broadcasted_iota(jnp.int32, shape, 1)).astype(F32)
    y_pos = (gy * width_y + lax.broadcasted_iota(jnp.int32, shape, 2)).astype(F32)
    for s in range(sources):
        cell = pos_ref[s]
        rest = lax.rem(cell, size_x * size_y)
        d_z = z_pos - lax.div(cell, size_x * size_y).astype(F32)
        d_x = x_pos - lax.div(rest, size_y).astype(F32)
        d_y = y_pos - lax.rem(rest, size_y).astype(F32)
        dist = jnp.sqrt(d_z * d_z + d_x * d_x + d_y * d_y)
        primary = jnp.exp(-dist / ((size_x + size_y) / 8.0))
        for comp, weight in enumerate((1.0, 0.5, 0.25)):
            real = (induct[comp] - 1.0) * weight * primary
            resid[s, pl.ds(comp * depth, depth)] = real
            resid[s, pl.ds(half + comp * depth, depth)] = 0.5 * real

    base = sources * vecs

    def sum_copy(index, count, offset):
        return pltpu.make_async_remote_copy(
            src_ref=part.at[index, pl.ds(0, count)],
            dst_ref=parts.at[index, rank, pl.ds(0, count)],
            send_sem=sum_send.at[index, offset - 1],
            recv_sem=sum_recv.at[index, offset - 1],
            device_id=peer_of(offset),
            device_id_type=MESH,
        )

    def group_send(index, count):
        for offset in range(1, group):
            sum_copy(index, count, offset).start()
        parts[index, pl.ds(rank, 1), pl.ds(0, count)] = part[index, pl.ds(0, count)][None]

    def group_sum(index, count):
        for offset in range(1, group):
            sum_copy(index, count, offset).wait()
        return jnp.sum(parts[index, :, pl.ds(0, count)], axis=0)

    def products(field, pairs, first, count, sums):
        def body(j, sums):
            sums = list(sums)
            at = pl.ds(pl.multiple_of(j * 16, 16), 16)
            pair = pl.ds(j * 2, 2)
            values = [field[s, pair] for s in range(sources)]
            for k in range(vecs):
                vector = full_c[k, at].astype(F32).reshape(2, width_x, width_y)
                for s in range(sources):
                    sums[s * vecs + k] += jnp.sum(vector * values[s], axis=0)
            for i, (left, right) in enumerate(pairs):
                for s in range(sources):
                    sums[base + s * len(pairs) + i] += jnp.sum(left[s, pair] * right[s, pair], axis=0)
            return tuple(sums)

        return lax.fori_loop(first, first + count, body, tuple(sums), unroll=2)

    def blank(count):
        return [jnp.zeros((width_x, width_y), F32)] * count

    def pack_sums(sums):
        lane = lax.broadcasted_iota(jnp.int32, (width_x, width_y), 1)
        packed = jnp.zeros((width_x, width_y), F32)
        for i, value in enumerate(sums):
            packed = jnp.where(lane == i, jnp.sum(value, axis=1, keepdims=True), packed)
        return packed

    def unpack_sums(packed, count):
        row = jnp.sum(packed, axis=0, keepdims=True)
        size = (count, width_y)
        mask = lax.broadcasted_iota(jnp.int32, size, 0) == lax.broadcasted_iota(jnp.int32, size, 1)
        return jnp.sum(jnp.where(mask, row, 0.0), axis=1, keepdims=True)

    def step_sums(index, field, pairs):
        count = base + sources * len(pairs)
        part[index, pl.ds(0, 8)] = pack_sums(products(field, pairs, 0, tiles // 2, blank(count)))
        group_send(index, 8)
        return unpack_sums(group_sum(index, 8), count)

    def spread(value):
        return jnp.broadcast_to(value, (width_x, width_y))

    def combine(out, terms, rows_of, stack, extra=None):
        for s in range(sources):
            for k in range(vecs):
                coef[s, k] = spread(rows_of[s][:, k : k + 1])
        wide = [[spread(c[s]) for s in range(sources)] for _, c in terms]
        wide_extra = [[spread(c[s]) for s in range(sources)] for _, c in extra[1]] if extra else []

        def body(j, _):
            at = pl.ds(pl.multiple_of(j * 16, 16), 16)
            pair = pl.ds(j * 2, 2)
            totals = []
            for s in range(sources):
                value = None
                for (ref, _), w in zip(terms, wide):
                    now = ref[s, pair] * w[s][None]
                    value = now if value is None else value + now
                totals.append(value)
            if extra:
                out2, terms2, keep = extra
                for s in range(sources):
                    value = out2[s, pair] if keep else None
                    for (ref, _), w in zip(terms2, wide_extra):
                        now = ref[s, pair] * w[s][None]
                        value = now if value is None else value + now
                    out2[s, pair] = value
            for k in range(vecs):
                vector = stack[k, at, :].astype(F32).reshape(2, width_x, width_y)
                for s in range(sources):
                    totals[s] = totals[s] + vector * coef[s, k][None]
            for s in range(sources):
                out[s, pair] = totals[s]
            return 0

        lax.fori_loop(0, tiles // 2, body, 0, unroll=3)

    east, west = gx + 1 < n_gx, gx >= 1
    north, south = gy + 1 < n_gy, gy >= 1
    lane2 = lax.broadcasted_iota(jnp.int32, (depth, width_y), 1)
    layer2 = lax.broadcasted_iota(jnp.int32, (depth, width_y), 0)
    layer3 = lax.broadcasted_iota(jnp.int32, shape, 0)
    row3 = lax.broadcasted_iota(jnp.int32, shape, 1)
    lane3 = lax.broadcasted_iota(jnp.int32, shape, 2)
    both = jnp.logical_and
    links = (
        (row_out, 1, row_in, 0, (1, 0), east, west),
        (row_out, 0, row_in, 1, (-1, 0), west, east),
        (col_out, 1, col_in, 0, (0, 1), north, south),
        (col_out, 0, col_in, 1, (0, -1), south, north),
        (col_out, 1, col_in, 2, (-1, 1), both(west, north), both(east, south)),
        (col_out, 0, col_in, 3, (1, -1), both(east, south), both(west, north)),
    )

    def halo_copy(index, number):
        src, which, dst, place, (d_x, d_y), _, _ = links[number]
        return pltpu.make_async_remote_copy(
            src_ref=src.at[index, which],
            dst_ref=dst.at[index, place],
            send_sem=halo_send.at[index, number],
            recv_sem=halo_recv.at[index, number],
            device_id=(gx + d_x, gy + d_y, tx),
            device_id_type=MESH,
        )

    lanes = lax.broadcasted_iota(jnp.int32, (tiles, width_x, width_y), 2)
    places = lax.broadcasted_iota(jnp.int32, (tiles, width_x, width_y), 0)

    def exchange_start(index, field):
        first = jnp.zeros((width_x, width_y), F32)
        last = jnp.zeros((width_x, width_y), F32)
        for s in range(sources):
            value = field[s]
            here = lanes == places + s * tiles
            first = first + jnp.sum(jnp.where(here, value[:, :, 0:1], 0.0), axis=0)
            last = last + jnp.sum(jnp.where(here, value[:, :, width_y - 1 : width_y], 0.0), axis=0)
            row_out[index, 0, pl.ds(s * tiles, tiles)] = value[:, 0, :]
            row_out[index, 1, pl.ds(s * tiles, tiles)] = value[:, width_x - 1, :]
        col_out[index, 0] = first
        col_out[index, 1] = last
        for number in range(len(links)):
            @pl.when(links[number][5])
            def _():
                halo_copy(index, number).start()

    def exchange_wait(index):
        for number in range(len(links)):
            dst, place, got = links[number][2], links[number][3], links[number][6]

            @pl.when(jnp.logical_not(got))
            def _():
                dst[index, place] = jnp.zeros(dst.shape[2:], F32)

            @pl.when(got)
            def _():
                halo_copy(index, number).wait_recv()

    def image_copy(number, piece):
        _, which, _, place, (d_x, d_y), _, _ = links[number]
        if number < 2:
            src, dst, sem = img_row_out.at[which, piece], img_row_in.at[place, piece], number * chunks + piece
        else:
            src, dst, sem = img_col_out.at[which], img_col_in.at[place], 2 * chunks + number - 2
        return pltpu.make_async_remote_copy(
            src_ref=src,
            dst_ref=dst,
            send_sem=img_send.at[sem],
            recv_sem=img_recv.at[sem],
            device_id=(gx + d_x, gy + d_y, tx),
            device_id_type=MESH,
        )

    image_copies = [(number, piece) for number in range(2) for piece in range(chunks)]
    image_copies += [(number, 0) for number in range(2, len(links))]

    def image_start(number, piece):
        @pl.when(links[number][5])
        def _():
            image_copy(number, piece).start()

    def image_pack(piece):
        size = (16, width_x, width_y)
        lane = lax.broadcasted_iota(jnp.int32, size, 2)
        tile = lax.broadcasted_iota(jnp.int32, size, 0) + piece * 16
        here = lane == tile
        for s in range(1, sources):
            here = jnp.logical_or(here, lane == tile + s * tiles)

        def body(k, _):
            value = full_c[k, pl.ds(piece * chunk, chunk)].astype(F32).reshape(size)
            for side, (row, col) in enumerate(((0, 0), (width_x - 1, width_y - 1))):
                img_row_out[side, piece, pl.ds(pl.multiple_of(k * 16, 16), 16)] = value[:, row, :]
                column = jnp.sum(jnp.where(here, value[:, :, col : col + 1], 0.0), axis=0)
                if piece:
                    column = column + img_col_out[side, k]
                img_col_out[side, k] = column
            return 0

        lax.fori_loop(0, vecs, body, 0)
        for number in range(2):
            image_start(number, piece)

    def image_wait():
        for number, piece in image_copies:
            place, got = links[number][3], links[number][6]

            @pl.when(jnp.logical_not(got))
            def _():
                if number < 2:
                    img_row_in[place, piece] = jnp.zeros(img_row_in.shape[2:], F32)
                else:
                    img_col_in[place] = jnp.zeros(img_col_in.shape[1:], F32)

            @pl.when(got)
            def _():
                image_copy(number, piece).wait_recv()

    def by_lane(values):
        lane = lax.broadcasted_iota(jnp.int32, (width_x, width_y), 1)
        result = values[0]
        for s in range(1, sources):
            result = jnp.where(lane >= s * tiles, values[s], result)
        return result

    def combine_halo(row, col, terms):
        wide = [[spread(c[s]) for s in range(sources)] for _, _, c in terms]

        def body(i, _):
            place, piece = lax.div(i, chunks), lax.rem(i, chunks)
            totals = []
            for s in range(sources):
                at = pl.ds(pl.multiple_of(s * tiles + piece * 16, 8), 16)
                value = None
                for (ref, _, _), w in zip(terms, wide):
                    now = ref[place, at].reshape(2, width_x, width_y) * w[s][None]
                    value = now if value is None else value + now
                totals.append(value)
            for k in range(vecs):
                vector = img_row_in[place, piece, pl.ds(k * 16, 16)].reshape(2, width_x, width_y)
                for s in range(sources):
                    totals[s] = totals[s] + vector * coef[s, k][None]
            for s in range(sources):
                at = pl.ds(pl.multiple_of(s * tiles + piece * 16, 8), 16)
                row[place, at] = totals[s].reshape(16, width_y)
            return 0

        lax.fori_loop(0, 2 * chunks, body, 0)
        values = [None] * 4
        for (_, ref, _), w in zip(terms, wide):
            scale = by_lane(w)
            for place in range(4):
                now = ref[place] * scale
                values[place] = now if values[place] is None else values[place] + now
        for k in range(vecs):
            scale = by_lane([coef[s, k] for s in range(sources)])
            for place in range(4):
                values[place] = values[place] + img_col_in[place, k] * scale
        for place in range(4):
            col[place] = values[place]

    def apply(field, row_halo, col_halo, out):
        def columns(place, at):
            packed = col_halo[place][None]
            return jnp.sum(jnp.where(lane3 == layer3 + at, packed, 0.0), axis=2, keepdims=True)

        def corner(place, row, at):
            packed = col_halo[place, row : row + 1]
            return jnp.sum(jnp.where(lane2 == layer2 + at, packed, 0.0), axis=1, keepdims=True)

        def plus_y(f, edge):
            return jnp.where(lane3 == width_y - 1, edge, pltpu.roll(f, width_y - 1, 2))

        def minus_y(f, edge):
            return jnp.where(lane3 == 0, edge, pltpu.roll(f, 1, 2))

        def plus_x(f, row):
            return jnp.where(row3 == width_x - 1, row[:, None, :], pltpu.roll(f, width_x - 1, 1))

        def minus_x(f, row):
            return jnp.where(row3 == 0, row[:, None, :], pltpu.roll(f, 1, 1))

        zero = jnp.zeros((1, width_x, width_y), F32)

        def plus_z(f):
            return jnp.concatenate([f[1:], zero], axis=0)

        def minus_z(f):
            return jnp.concatenate([zero, f[:-1]], axis=0)

        def body(s, _):
            for p in range(2):
                def comp(c):
                    return field[s, pl.ds(p * half + c * depth, depth)]

                def at(c):
                    return s * tiles + p * half + c * depth

                def row(place, c):
                    return row_halo[place, pl.ds(pl.multiple_of(at(c), 8), depth)]

                e_x, e_y, e_z = comp(0), comp(1), comp(2)
                xp_y = plus_y(e_x, columns(1, at(0)))
                xm_y = minus_y(e_x, columns(0, at(0)))
                t = xp_y - e_x
                hx = row(0, 0)
                hx_up = jnp.where(lane2 == width_y - 1, corner(3, width_x - 1, at(0)), pltpu.roll(hx, width_y - 1, 1))
                dt = t - minus_x(t, hx_up - hx)
                c = e_x - minus_x(e_x, hx)
                a = e_y - minus_y(e_y, columns(0, at(1)))
                hy = row(1, 1)
                hy_down = jnp.where(lane2 == 0, corner(2, 0, at(1)), pltpu.roll(hy, 1, 1))
                da = plus_x(a, hy - hy_down) - a
                y2 = plus_x(e_y, hy) + minus_x(e_y, row(0, 1)) - 2.0 * e_y
                zp_x = plus_x(e_z, row(1, 2))
                zp_y = plus_y(e_z, columns(1, at(2)))
                z2 = zp_x + minus_x(e_z, row(0, 2)) + zp_y + minus_y(e_z, columns(0, at(2))) - 4.0 * e_z
                fx_z = zp_x - e_z
                fy_z = zp_y - e_z
                k_x = da - (xp_y + xm_y + plus_z(e_x) + minus_z(e_x) - 4.0 * e_x) + (fx_z - minus_z(fx_z))
                k_y = (fy_z - minus_z(fy_z)) - (plus_z(e_y) + minus_z(e_y) - 2.0 * e_y) - y2 + dt
                ca = c + a
                k_z = (plus_z(ca) - ca) - z2
                for number, value in enumerate((k_x, k_y, k_z)):
                    cross = induct[number] * field[s, pl.ds((1 - p) * half + number * depth, depth)]
                    value = value - cross if p == 0 else value + cross
                    out[s, pl.ds(p * half + number * depth, depth)] = value
            return 0

        lax.fori_loop(0, sources, body, 0)

    exchange_start(0, resid)
    total[...] = jnp.zeros_like(total)

    def gram_body(j, _):
        block = full_c[:, pl.ds(pl.multiple_of(j * 16, 16), 16), :].reshape(vecs * 16, width_y)
        total[...] += lax.dot_general(block, block, (((1,), (1,)), ((), ())), preferred_element_type=F32)
        return 0

    wide = vecs * 16
    halves = wide // width_y
    start = blank(base)
    own[0].wait()
    for piece in range(chunks):
        for step in range(1, n_tx - 1):
            gather_arrive(0, step, piece, True)
        if piece + 2 < chunks:
            gather_start(0, 1, piece + 2)
        elif piece + 1 == chunks:
            gather_start(1, 1, 0)
        gather_arrive(0, n_tx - 1, piece)
        lax.fori_loop(piece * (chunk // 16), (piece + 1) * (chunk // 16), gram_body, 0)
        start = products(resid, [], piece * 8, 8, start)
        if piece + 1 < chunks:
            image_pack(piece)
    same = lax.rem(lax.broadcasted_iota(jnp.int32, (wide, wide), 0), 16) == lax.rem(
        lax.broadcasted_iota(jnp.int32, (wide, wide), 1), 16
    )
    folded = jnp.sum(jnp.where(same, total[...], 0.0).reshape(vecs, 16, wide), axis=1)
    gram = jnp.zeros((vecs, width_y), F32)
    lane = lax.broadcasted_iota(jnp.int32, (width_y, width_y), 0)
    column = lax.broadcasted_iota(jnp.int32, (width_y, width_y), 1)
    for h in range(halves):
        pick = (lax.div(lane, 16) + h * (width_y // 16) == column).astype(F32)
        gram = gram + jnp.dot(
            folded[:, h * width_y : (h + 1) * width_y], pick,
            precision=lax.Precision.HIGHEST, preferred_element_type=F32,
        )
    part[0, pl.ds(0, vecs)] = gram
    part[0, pl.ds(vecs, 8)] = pack_sums(start)
    group_send(0, vecs + 8)
    image_pack(chunks - 1)
    for number in range(2, len(links)):
        image_start(number, 0)
    first_sum = group_sum(0, vecs + 8)
    gram = first_sum[:vecs, :vecs]
    start = unpack_sums(first_sum[vecs:], base)
    row_id = lax.broadcasted_iota(jnp.int32, (vecs, vecs), 0)
    eye = (row_id == lax.broadcasted_iota(jnp.int32, (vecs, vecs), 1)).astype(F32)
    wide_row = lax.broadcasted_iota(jnp.int32, (vecs, 2 * vecs), 0)
    system = jnp.concatenate([gram, eye], axis=1)
    for k in range(vecs):
        pivot = system[k : k + 1] / system[k : k + 1, k : k + 1]
        system = jnp.where(wide_row == k, pivot, system - system[:, k : k + 1] * pivot)
    inverse[...] = system[:, vecs:]

    def solve(column):
        answer = jnp.sum(inverse[...] * column, axis=0, keepdims=True)
        flat = jnp.sum(eye * column, axis=0, keepdims=True)
        return answer, jnp.sum(answer * flat, axis=1, keepdims=True)

    weights = [solve(start[s * vecs : (s + 1) * vecs])[0] for s in range(sources)]
    one = jnp.ones((1, 1), F32)
    combine(resid, [(resid, [one] * sources)], [-w for w in weights], full_c)
    exchange_wait(0)
    image_wait()
    combine_halo(row_r, col_r, [(row_in.at[0], col_in.at[0], [one] * sources)])

    every = range(sources)
    for cycle in range(CYCLES):
        index = 2 * cycle
        apply(resid, row_r, col_r, work)
        exchange_start(index + 1, work)
        sums = step_sums(index + 1, work, [(resid, resid), (resid, work), (work, work)])
        state = []
        for s in every:
            def got(i):
                return sums[base + 3 * s + i : base + 3 * s + i + 1]

            beta = jnp.sqrt(got(0) + EPS)
            scale = 1.0 / beta
            raw, quad = solve(sums[s * vecs : (s + 1) * vecs])
            g_0 = raw * scale
            n_00 = got(0) * scale * scale
            h_00 = got(1) * scale * scale
            left = (got(2) - quad) * scale * scale - 2.0 * h_00 * h_00 + h_00 * h_00 * n_00
            left = jnp.maximum(left, 0.0)
            h_10 = jnp.sqrt(left + EPS)
            state.append((beta, scale, g_0, n_00, h_00, left, h_10))
        of_w = [v[1] / v[6] for v in state]
        of_r = [-v[4] * v[1] / v[6] for v in state]
        combine(krylov, [(work, of_w), (resid, of_r)], [-v[2] / v[6] for v in state], full_c)
        exchange_wait(index + 1)
        now = (row_in.at[index + 1], col_in.at[index + 1])
        combine_halo(row_v, col_v, [now + (of_w,), (row_r, col_r, of_r)])
        if cycle + 1 < n_tx - 1:
            gather_arrive(1, cycle + 1, 0, True)
        apply(krylov, row_v, col_v, work)
        if cycle + 1 < CYCLES:
            exchange_start(index + 2, work)
        pairs = [(resid, work), (krylov, work), (work, work), (krylov, krylov)]
        sums = step_sums(index + 2, work, pairs)
        in_r, in_v, in_w, in_g, out_r, out_v = [], [], [], [], [], []
        for s in every:
            def got(i):
                return sums[base + 4 * s + i : base + 4 * s + i + 1]

            beta, scale, g_0, n_00, h_00, _, h_10 = state[s]
            g_1, quad = solve(sums[s * vecs : (s + 1) * vecs])
            h_01 = got(0) * scale
            h_11 = got(1)
            n_11 = got(3)
            n_01 = h_00 * (1.0 - n_00) / h_10
            left = (
                got(2) - quad - 2.0 * (h_01 * h_01 + h_11 * h_11)
                + h_01 * h_01 * n_00 + h_11 * h_11 * n_11 + 2.0 * h_01 * h_11 * n_01
            )
            h_21 = jnp.sqrt(jnp.maximum(left, 0.0) + EPS)
            a_00 = h_00 * h_00 + h_10 * h_10
            a_01 = h_00 * h_01 + h_10 * h_11
            a_11 = h_01 * h_01 + h_11 * h_11 + h_21 * h_21
            l_00 = jnp.sqrt(a_00)
            l_10 = a_01 / l_00
            l_11 = jnp.sqrt(a_11 - l_10 * l_10)
            f_0 = beta * h_00 / l_00
            f_1 = (beta * h_01 - l_10 * f_0) / l_11
            y_1 = f_1 / l_11
            y_0 = (f_0 - l_10 * y_1) / l_00
            t_0 = beta - h_00 * y_0 - h_01 * y_1
            t_1 = -(h_10 * y_0 + h_11 * y_1)
            t_2 = -h_21 * y_1
            share = t_2 / h_21
            in_r.append((t_0 - share * h_01) * scale)
            in_v.append(t_1 - share * h_11)
            in_w.append(share)
            in_g.append(-share * g_1)
            out_r.append(y_0 * scale)
            out_v.append(y_1)
            weights[s] = weights[s] - (g_0 * y_0 + g_1 * y_1)
        update = (sol_ref, [(resid, out_r), (krylov, out_v)], cycle > 0)
        combine(resid, [(resid, in_r), (krylov, in_v), (work, in_w)], in_g, full_c, update)
        if cycle + 1 < CYCLES:
            exchange_wait(index + 2)
            now = (row_in.at[index + 2], col_in.at[index + 2])
            combine_halo(row_r, col_r, [(row_r, col_r, in_r), (row_v, col_v, in_v), now + (in_w,)])

    for step in range(CYCLES + 1, n_tx - 1):
        gather_arrive(1, step, 0, True)
    gather_arrive(1, n_tx - 1, 0)
    own[1].wait()
    combine(sol_ref, [(sol_ref, [one] * sources)], weights, full_u)
    gather_sent(0)
    gather_sent(1)
    for index in range(2 * CYCLES):
        for number in range(len(links)):
            @pl.when(links[number][5])
            def _():
                halo_copy(index, number).wait_send()
    for number, piece in image_copies:
        @pl.when(links[number][5])
        def _():
            image_copy(number, piece).wait_send()


def on_device(dims, src_cell, basis, images, induction):
    n_gx, n_gy, n_tx = dims
    per_dev, _, _, depth, width_x, width_y = basis.shape
    sources = src_cell.shape[0]
    tiles = 6 * depth
    rows = tiles * width_x
    vecs = per_dev * n_tx
    group = n_gx * n_gy
    field = (sources, tiles, width_x, width_y)
    ind_rows = 3 * induction.shape[1] * width_x
    most = vecs + 8
    sums, halos = 2 * CYCLES + 1, 2 * CYCLES
    dma = pltpu.SemaphoreType.DMA
    vmem = pl.BlockSpec(memory_space=pltpu.VMEM)
    hbm = pl.BlockSpec(memory_space=pl.ANY)
    chunks = tiles // 16
    out = pl.pallas_call(
        functools.partial(kernel, dims),
        out_shape=(jax.ShapeDtypeStruct(field, F32),) * 2,
        in_specs=[pl.BlockSpec(memory_space=pltpu.SMEM), hbm, hbm, vmem],
        out_specs=(vmem, vmem),
        scratch_shapes=[
            pltpu.VMEM((vecs, rows, width_y), jnp.bfloat16),
            pltpu.VMEM((vecs, rows, width_y), jnp.bfloat16),
            pltpu.VMEM((n_tx, ind_rows, width_y), jnp.bfloat16),
            pltpu.VMEM((3, depth, width_x, width_y), F32),
            pltpu.VMEM(field, F32),
            pltpu.VMEM(field, F32),
            pltpu.VMEM((vecs * 16, vecs * 16), F32),
            pltpu.VMEM((vecs, vecs), F32),
            pltpu.VMEM((sources, vecs, width_x, width_y), F32),
            pltpu.VMEM((sums, most, width_y), F32),
            pltpu.VMEM((sums, group, most, width_y), F32),
            pltpu.VMEM((halos, 2, sources * tiles, width_y), F32),
            pltpu.VMEM((halos, 2, sources * tiles, width_y), F32),
            pltpu.VMEM((halos, 2, width_x, width_y), F32),
            pltpu.VMEM((halos, 4, width_x, width_y), F32),
            pltpu.VMEM((2, chunks, vecs * 16, width_y), F32),
            pltpu.VMEM((2, chunks, vecs * 16, width_y), F32),
            pltpu.VMEM((2, vecs, width_x, width_y), F32),
            pltpu.VMEM((4, vecs, width_x, width_y), F32),
            pltpu.VMEM((2, sources * tiles, width_y), F32),
            pltpu.VMEM((2, sources * tiles, width_y), F32),
            pltpu.VMEM((4, width_x, width_y), F32),
            pltpu.VMEM((4, width_x, width_y), F32),
            dma((2,)),
            dma((2, 2, n_tx - 1, chunks)),
            dma((2, 2, n_tx - 1, chunks)),
            dma((n_tx - 1,)),
            dma((n_tx - 1,)),
            dma((sums, group - 1)),
            dma((sums, group - 1)),
            dma((halos, 6)),
            dma((halos, 6)),
            dma((2 * chunks + 4,)),
            dma((2 * chunks + 4,)),
        ],
        compiler_params=pltpu.CompilerParams(
            collective_id=0, has_side_effects=True, vmem_limit_bytes=60 * 1024 * 1024
        ),
        cost_estimate=pl.CostEstimate(flops=400_000_000, bytes_accessed=2_000_000, transcendentals=20_000),
    )(
        src_cell,
        basis.reshape(per_dev, rows, width_y),
        images.reshape(per_dev, rows, width_y),
        induction.reshape(ind_rows, width_y),
    )
    shape = (sources, 2, 3, depth, width_x, width_y)
    return tuple(o.reshape(shape) for o in out)


def solution(mesh):
    dims = (mesh.shape["gx"], mesh.shape["gy"], mesh.shape["tx"])
    spec = P("tx", None, None, None, "gx", "gy")
    return jax.shard_map(
        functools.partial(on_device, dims),
        mesh=mesh,
        in_specs=(P("tx"), spec, spec, P(None, "tx", "gx", "gy")),
        out_specs=(spec, spec),
        check_vma=False,
    )
```

```python
import functools

import jax
import jax.numpy as jnp
from jax import lax
from jax.experimental import pallas as pl
from jax.experimental.pallas import tpu as pltpu
from jax.sharding import PartitionSpec as P

CYCLES = 2
ARNOLDI = 2
EPS = 1e-06
MESH = pl.DeviceIdType.MESH
F32 = jnp.float32


def kernel(
    dims, pos_ref, u_ref, c_ref, m_ref, sol_ref, res_ref,
    full_c, full_u, ind_all, induct, krylov, work, total, inverse, coef, held,
    part, parts, row_out, row_in, col_out, col_in,
    img_row_out, img_row_in, img_col_out, img_col_in, row_r, row_v, col_r, col_v,
    own_sem, gather_send, gather_recv, ind_send, ind_recv, sum_send, sum_recv, halo_send, halo_recv,
    img_send, img_recv,
):
    n_gx, n_gy, n_tx = dims
    gx, gy, tx = lax.axis_index("gx"), lax.axis_index("gy"), lax.axis_index("tx")
    group = n_gx * n_gy
    rank = gx * n_gy + gy
    sources = pos_ref.shape[0]
    per_dev = c_ref.shape[0]
    rows = c_ref.shape[1]
    width_y = c_ref.shape[2]
    width_x = 8
    depth = induct.shape[1]
    tiles = rows // width_x
    vecs = full_c.shape[0]
    half = tiles // 2
    chunk = 16 * width_x
    chunks = rows // chunk

    def peer_of(offset):
        other = lax.rem(rank + offset, group)
        return (lax.div(other, n_gy), lax.rem(other, n_gy), tx)

    def along(offset):
        return (gx, gy, lax.rem(tx + offset, n_tx))

    barrier = pltpu.get_barrier_semaphore()
    for offset in range(1, group):
        pl.semaphore_signal(barrier, inc=1, device_id=peer_of(offset), device_id_type=MESH)
    for offset in range(1, n_tx):
        pl.semaphore_signal(barrier, inc=1, device_id=along(offset), device_id_type=MESH)
    pl.semaphore_wait(barrier, group - 1 + n_tx - 1)

    def slot(shard):
        return pl.ds(shard * per_dev, per_dev)

    def rows_at(which, piece):
        return pl.ds(piece * chunk, chunk) if which == 0 else pl.ds(0, rows)

    pieces = (chunks, 1)

    def hop(which, way, step, piece):
        full = (full_c, full_u)[which]
        at = rows_at(which, piece)
        sign = 1 if way == 0 else -1
        shard = tx - sign * (step - 1)
        source = (c_ref, u_ref)[which].at[:, at] if step == 1 else full.at[slot(shard), at]
        return pltpu.make_async_remote_copy(
            src_ref=source,
            dst_ref=full.at[slot(shard), at],
            send_sem=gather_send.at[which, way, step - 1, piece],
            recv_sem=gather_recv.at[which, way, step - 1, piece],
            device_id=(gx, gy, tx + sign),
            device_id_type=MESH,
        )

    def sends(way, step):
        if way == 0:
            return jnp.logical_and(tx + 1 < n_tx, tx - step + 1 >= 0)
        return jnp.logical_and(tx - 1 >= 0, tx + step - 1 < n_tx)

    def receives(way, step):
        return tx - step >= 0 if way == 0 else tx + step < n_tx

    def gather_start(which, step, piece):
        for way in range(2):
            @pl.when(sends(way, step))
            def _():
                hop(which, way, step, piece).start()

    def gather_arrive(which, step, piece, then=False):
        for way in range(2):
            @pl.when(receives(way, step))
            def _():
                full = (full_c, full_u)[which]
                at = rows_at(which, piece)
                shard = tx - step if way == 0 else tx + step
                pltpu.make_async_remote_copy(
                    src_ref=full.at[slot(shard), at],
                    dst_ref=full.at[slot(shard), at],
                    send_sem=gather_send.at[which, way, step - 1, piece],
                    recv_sem=gather_recv.at[which, way, step - 1, piece],
                    device_id=along(1),
                    device_id_type=MESH,
                ).wait_recv()

            if then:
                @pl.when(sends(way, step + 1))
                def _():
                    hop(which, way, step + 1, piece).start()

    def gather_sent(which):
        for piece in range(pieces[which]):
            for step in range(1, n_tx):
                for way in range(2):
                    @pl.when(sends(way, step))
                    def _():
                        hop(which, way, step, piece).wait_send()

    own = [
        pltpu.make_async_copy(ref, full.at[slot(tx)], own_sem.at[number])
        for number, (ref, full) in enumerate(((c_ref, full_c), (u_ref, full_u)))
    ]

    def ind_copy(offset):
        return pltpu.make_async_remote_copy(
            src_ref=m_ref,
            dst_ref=ind_all.at[tx],
            send_sem=ind_send.at[offset - 1],
            recv_sem=ind_recv.at[offset - 1],
            device_id=along(offset),
            device_id_type=MESH,
        )

    for offset in range(1, n_tx):
        ind_copy(offset).start()
    gather_start(0, 1, 0)
    gather_start(0, 1, 1)
    for copy in own:
        copy.start()
    ind_all[pl.ds(tx, 1)] = m_ref[...][None]
    for offset in range(1, n_tx):
        ind_copy(offset).wait()
    layers = depth // n_tx
    for owner in range(n_tx):
        piece = ind_all[owner].astype(F32).reshape(3, layers, width_x, width_y)
        for layer in range(layers):
            induct[:, owner * layers + layer] = piece[:, layer]

    size_x, size_y = width_x * n_gx, width_y * n_gy
    shape = (depth, width_x, width_y)
    z_pos = lax.broadcasted_iota(jnp.int32, shape, 0).astype(F32)
    x_pos = (gx * width_x + lax.broadcasted_iota(jnp.int32, shape, 1)).astype(F32)
    y_pos = (gy * width_y + lax.broadcasted_iota(jnp.int32, shape, 2)).astype(F32)
    for s in range(sources):
        cell = pos_ref[s]
        rest = lax.rem(cell, size_x * size_y)
        d_z = z_pos - lax.div(cell, size_x * size_y).astype(F32)
        d_x = x_pos - lax.div(rest, size_y).astype(F32)
        d_y = y_pos - lax.rem(rest, size_y).astype(F32)
        dist = jnp.sqrt(d_z * d_z + d_x * d_x + d_y * d_y)
        primary = jnp.exp(-dist / ((size_x + size_y) / 8.0))
        for comp, weight in enumerate((1.0, 0.5, 0.25)):
            real = (induct[comp] - 1.0) * weight * primary
            res_ref[s, pl.ds(comp * depth, depth)] = real
            res_ref[s, pl.ds(half + comp * depth, depth)] = 0.5 * real

    base = sources * vecs

    def sum_copy(index, count, offset):
        return pltpu.make_async_remote_copy(
            src_ref=part.at[index, pl.ds(0, count)],
            dst_ref=parts.at[index, rank, pl.ds(0, count)],
            send_sem=sum_send.at[index, offset - 1],
            recv_sem=sum_recv.at[index, offset - 1],
            device_id=peer_of(offset),
            device_id_type=MESH,
        )

    def group_send(index, count):
        for offset in range(1, group):
            sum_copy(index, count, offset).start()
        parts[index, pl.ds(rank, 1), pl.ds(0, count)] = part[index, pl.ds(0, count)][None]

    def group_sum(index, count):
        for offset in range(1, group):
            sum_copy(index, count, offset).wait()
        return jnp.sum(parts[index, :, pl.ds(0, count)], axis=0)

    def products(field, pairs, first, count, sums):
        def body(j, sums):
            sums = list(sums)
            at = pl.ds(pl.multiple_of(j * 16, 16), 16)
            pair = pl.ds(j * 2, 2)
            values = [field[s, pair] for s in range(sources)]
            for k in range(vecs):
                vector = full_c[k, at].astype(F32).reshape(2, width_x, width_y)
                for s in range(sources):
                    sums[s * vecs + k] += jnp.sum(vector * values[s], axis=0)
            for i, (left, right) in enumerate(pairs):
                for s in range(sources):
                    sums[base + s * len(pairs) + i] += jnp.sum(left[s, pair] * right[s, pair], axis=0)
            return tuple(sums)

        return lax.fori_loop(first, first + count, body, tuple(sums), unroll=2)

    def blank(count):
        return [jnp.zeros((width_x, width_y), F32)] * count

    def pack_sums(sums):
        lane = lax.broadcasted_iota(jnp.int32, (width_x, width_y), 1)
        packed = jnp.zeros((width_x, width_y), F32)
        for i, value in enumerate(sums):
            packed = jnp.where(lane == i, jnp.sum(value, axis=1, keepdims=True), packed)
        return packed

    def unpack_sums(packed, count):
        row = jnp.sum(packed, axis=0, keepdims=True)
        size = (count, width_y)
        mask = lax.broadcasted_iota(jnp.int32, size, 0) == lax.broadcasted_iota(jnp.int32, size, 1)
        return jnp.sum(jnp.where(mask, row, 0.0), axis=1, keepdims=True)

    def step_sums(index, field, pairs, meanwhile):
        count = base + sources * len(pairs)
        part[index, pl.ds(0, 8)] = pack_sums(products(field, pairs, 0, tiles // 2, blank(count)))
        group_send(index, 8)
        meanwhile()
        return unpack_sums(group_sum(index, 8), count)

    def spread(value):
        return jnp.broadcast_to(value, (width_x, width_y))

    def combine(out, terms, rows_of, stack):
        for s in range(sources):
            for k in range(vecs):
                coef[s, k] = spread(rows_of[s][:, k : k + 1])
        wide = [[spread(c[s]) for s in range(sources)] for _, c in terms]

        def body(j, _):
            at = pl.ds(pl.multiple_of(j * 16, 16), 16)
            pair = pl.ds(j * 2, 2)
            totals = []
            for s in range(sources):
                value = None
                for (ref, _), w in zip(terms, wide):
                    now = ref[s, pair] * w[s][None]
                    value = now if value is None else value + now
                totals.append(value)
            for k in range(vecs):
                vector = stack[k, at, :].astype(F32).reshape(2, width_x, width_y)
                for s in range(sources):
                    totals[s] = totals[s] + vector * coef[s, k][None]
            for s in range(sources):
                out[s, pair] = totals[s]
            return 0

        lax.fori_loop(0, tiles // 2, body, 0, unroll=3)

    def accumulate(cycle, of_r, of_v):
        wide = [[spread(c[s]) for s in range(sources)] for c in (of_r, of_v)]

        def body(j, _):
            pair = pl.ds(j * 4, 4)
            for s in range(sources):
                value = held[cycle, s, pair] * wide[0][s][None] + krylov[s, pair] * wide[1][s][None]
                if cycle:
                    value = value + sol_ref[s, pair]
                sol_ref[s, pair] = value
            return 0

        lax.fori_loop(0, tiles // 4, body, 0)

    east, west = gx + 1 < n_gx, gx >= 1
    north, south = gy + 1 < n_gy, gy >= 1
    lane2 = lax.broadcasted_iota(jnp.int32, (depth, width_y), 1)
    layer2 = lax.broadcasted_iota(jnp.int32, (depth, width_y), 0)
    layer3 = lax.broadcasted_iota(jnp.int32, shape, 0)
    row3 = lax.broadcasted_iota(jnp.int32, shape, 1)
    lane3 = lax.broadcasted_iota(jnp.int32, shape, 2)
    both = jnp.logical_and
    links = (
        (row_out, 1, row_in, 0, (1, 0), east, west),
        (row_out, 0, row_in, 1, (-1, 0), west, east),
        (col_out, 1, col_in, 0, (0, 1), north, south),
        (col_out, 0, col_in, 1, (0, -1), south, north),
        (col_out, 1, col_in, 2, (-1, 1), both(west, north), both(east, south)),
        (col_out, 0, col_in, 3, (1, -1), both(east, south), both(west, north)),
    )

    def halo_copy(index, number):
        src, which, dst, place, (d_x, d_y), _, _ = links[number]
        return pltpu.make_async_remote_copy(
            src_ref=src.at[index, which],
            dst_ref=dst.at[index, place],
            send_sem=halo_send.at[index, number],
            recv_sem=halo_recv.at[index, number],
            device_id=(gx + d_x, gy + d_y, tx),
            device_id_type=MESH,
        )

    lanes = lax.broadcasted_iota(jnp.int32, (tiles, width_x, width_y), 2)
    places = lax.broadcasted_iota(jnp.int32, (tiles, width_x, width_y), 0)

    def exchange_start(index, field):
        first = jnp.zeros((width_x, width_y), F32)
        last = jnp.zeros((width_x, width_y), F32)
        for s in range(sources):
            value = field[s]
            here = lanes == places + s * tiles
            first = first + jnp.sum(jnp.where(here, value[:, :, 0:1], 0.0), axis=0)
            last = last + jnp.sum(jnp.where(here, value[:, :, width_y - 1 : width_y], 0.0), axis=0)
            row_out[index, 0, pl.ds(s * tiles, tiles)] = value[:, 0, :]
            row_out[index, 1, pl.ds(s * tiles, tiles)] = value[:, width_x - 1, :]
        col_out[index, 0] = first
        col_out[index, 1] = last
        for number in range(len(links)):
            @pl.when(links[number][5])
            def _():
                halo_copy(index, number).start()

    def exchange_wait(index):
        for number in range(len(links)):
            dst, place, got = links[number][2], links[number][3], links[number][6]

            @pl.when(jnp.logical_not(got))
            def _():
                dst[index, place] = jnp.zeros(dst.shape[2:], F32)

            @pl.when(got)
            def _():
                halo_copy(index, number).wait_recv()

    def image_copy(number, piece):
        _, which, _, place, (d_x, d_y), _, _ = links[number]
        if number < 2:
            src, dst, sem = img_row_out.at[which, piece], img_row_in.at[place, piece], number * chunks + piece
        else:
            src, dst, sem = img_col_out.at[which], img_col_in.at[place], 2 * chunks + number - 2
        return pltpu.make_async_remote_copy(
            src_ref=src,
            dst_ref=dst,
            send_sem=img_send.at[sem],
            recv_sem=img_recv.at[sem],
            device_id=(gx + d_x, gy + d_y, tx),
            device_id_type=MESH,
        )

    image_copies = [(number, piece) for number in range(2) for piece in range(chunks)]
    image_copies += [(number, 0) for number in range(2, len(links))]

    def image_start(number, piece):
        @pl.when(links[number][5])
        def _():
            image_copy(number, piece).start()

    def image_pack(piece):
        size = (16, width_x, width_y)
        lane = lax.broadcasted_iota(jnp.int32, size, 2)
        tile = lax.broadcasted_iota(jnp.int32, size, 0) + piece * 16
        here = lane == tile
        for s in range(1, sources):
            here = jnp.logical_or(here, lane == tile + s * tiles)

        def body(k, _):
            value = full_c[k, pl.ds(piece * chunk, chunk)].astype(F32).reshape(size)
            for side, (row, col) in enumerate(((0, 0), (width_x - 1, width_y - 1))):
                img_row_out[side, piece, pl.ds(pl.multiple_of(k * 16, 16), 16)] = value[:, row, :]
                column = jnp.sum(jnp.where(here, value[:, :, col : col + 1], 0.0), axis=0)
                if piece:
                    column = column + img_col_out[side, k]
                img_col_out[side, k] = column
            return 0

        lax.fori_loop(0, vecs, body, 0, unroll=4)
        for number in range(2):
            image_start(number, piece)

    def image_wait():
        for number, piece in image_copies:
            place, got = links[number][3], links[number][6]

            @pl.when(jnp.logical_not(got))
            def _():
                if number < 2:
                    img_row_in[place, piece] = jnp.zeros(img_row_in.shape[2:], F32)
                else:
                    img_col_in[place] = jnp.zeros(img_col_in.shape[1:], F32)

            @pl.when(got)
            def _():
                image_copy(number, piece).wait_recv()

    def by_lane(values):
        lane = lax.broadcasted_iota(jnp.int32, (width_x, width_y), 1)
        result = values[0]
        for s in range(1, sources):
            result = jnp.where(lane >= s * tiles, values[s], result)
        return result

    def combine_halo(row, col, terms):
        wide = [[spread(c[s]) for s in range(sources)] for _, _, c in terms]

        def body(i, _):
            place, piece = lax.div(i, chunks), lax.rem(i, chunks)
            totals = []
            for s in range(sources):
                at = pl.ds(pl.multiple_of(s * tiles + piece * 16, 8), 16)
                value = None
                for (ref, _, _), w in zip(terms, wide):
                    now = ref[place, at].reshape(2, width_x, width_y) * w[s][None]
                    value = now if value is None else value + now
                totals.append(value)
            for k in range(vecs):
                vector = img_row_in[place, piece, pl.ds(k * 16, 16)].reshape(2, width_x, width_y)
                for s in range(sources):
                    totals[s] = totals[s] + vector * coef[s, k][None]
            for s in range(sources):
                at = pl.ds(pl.multiple_of(s * tiles + piece * 16, 8), 16)
                row[place, at] = totals[s].reshape(16, width_y)
            return 0

        lax.fori_loop(0, 2 * chunks, body, 0)
        values = [None] * 4
        for (_, ref, _), w in zip(terms, wide):
            scale = by_lane(w)
            for place in range(4):
                now = ref[place] * scale
                values[place] = now if values[place] is None else values[place] + now
        for k in range(vecs):
            scale = by_lane([coef[s, k] for s in range(sources)])
            for place in range(4):
                values[place] = values[place] + img_col_in[place, k] * scale
        for place in range(4):
            col[place] = values[place]

    def apply(field, row_halo, col_halo, out):
        def columns(place, at):
            packed = col_halo[place][None]
            return jnp.sum(jnp.where(lane3 == layer3 + at, packed, 0.0), axis=2, keepdims=True)

        def corner(place, row, at):
            packed = col_halo[place, row : row + 1]
            return jnp.sum(jnp.where(lane2 == layer2 + at, packed, 0.0), axis=1, keepdims=True)

        def plus_y(f, edge):
            return jnp.where(lane3 == width_y - 1, edge, pltpu.roll(f, width_y - 1, 2))

        def minus_y(f, edge):
            return jnp.where(lane3 == 0, edge, pltpu.roll(f, 1, 2))

        def plus_x(f, row):
            return jnp.where(row3 == width_x - 1, row[:, None, :], pltpu.roll(f, width_x - 1, 1))

        def minus_x(f, row):
            return jnp.where(row3 == 0, row[:, None, :], pltpu.roll(f, 1, 1))

        zero = jnp.zeros((1, width_x, width_y), F32)

        def plus_z(f):
            return jnp.concatenate([f[1:], zero], axis=0)

        def minus_z(f):
            return jnp.concatenate([zero, f[:-1]], axis=0)

        for s in range(sources):
            for p in range(2):
                def comp(c):
                    return field[s, pl.ds(p * half + c * depth, depth)]

                def at(c):
                    return s * tiles + p * half + c * depth

                def row(place, c):
                    return row_halo[place, pl.ds(at(c), depth)]

                e_x, e_y, e_z = comp(0), comp(1), comp(2)
                xp_y = plus_y(e_x, columns(1, at(0)))
                xm_y = minus_y(e_x, columns(0, at(0)))
                t = xp_y - e_x
                hx = row(0, 0)
                hx_up = jnp.where(lane2 == width_y - 1, corner(3, width_x - 1, at(0)), pltpu.roll(hx, width_y - 1, 1))
                dt = t - minus_x(t, hx_up - hx)
                c = e_x - minus_x(e_x, hx)
                a = e_y - minus_y(e_y, columns(0, at(1)))
                hy = row(1, 1)
                hy_down = jnp.where(lane2 == 0, corner(2, 0, at(1)), pltpu.roll(hy, 1, 1))
                da = plus_x(a, hy - hy_down) - a
                y2 = plus_x(e_y, hy) + minus_x(e_y, row(0, 1)) - 2.0 * e_y
                zp_x = plus_x(e_z, row(1, 2))
                zp_y = plus_y(e_z, columns(1, at(2)))
                z2 = zp_x + minus_x(e_z, row(0, 2)) + zp_y + minus_y(e_z, columns(0, at(2))) - 4.0 * e_z
                fx_z = zp_x - e_z
                fy_z = zp_y - e_z
                k_x = da - (xp_y + xm_y + plus_z(e_x) + minus_z(e_x) - 4.0 * e_x) + (fx_z - minus_z(fx_z))
                k_y = (fy_z - minus_z(fy_z)) - (plus_z(e_y) + minus_z(e_y) - 2.0 * e_y) - y2 + dt
                ca = c + a
                k_z = (plus_z(ca) - ca) - z2
                for number, value in enumerate((k_x, k_y, k_z)):
                    cross = induct[number] * field[s, pl.ds((1 - p) * half + number * depth, depth)]
                    value = value - cross if p == 0 else value + cross
                    out[s, pl.ds(p * half + number * depth, depth)] = value

    exchange_start(0, res_ref)
    total[...] = jnp.zeros_like(total)

    def gram_body(j, _):
        block = full_c[:, pl.ds(pl.multiple_of(j * 16, 16), 16), :].reshape(vecs * 16, width_y)
        total[...] += lax.dot_general(block, block, (((1,), (1,)), ((), ())), preferred_element_type=F32)
        return 0

    wide = vecs * 16
    halves = wide // width_y
    start = blank(base)
    own[0].wait()
    for piece in range(chunks):
        for step in range(1, n_tx - 1):
            gather_arrive(0, step, piece, True)
        if piece + 2 < chunks:
            gather_start(0, 1, piece + 2)
        elif piece + 1 == chunks:
            gather_start(1, 1, 0)
        gather_arrive(0, n_tx - 1, piece)
        lax.fori_loop(piece * (chunk // 16), (piece + 1) * (chunk // 16), gram_body, 0)
        start = products(res_ref, [], piece * 8, 8, start)
        if piece + 1 < chunks:
            image_pack(piece)
    same = lax.rem(lax.broadcasted_iota(jnp.int32, (wide, wide), 0), 16) == lax.rem(
        lax.broadcasted_iota(jnp.int32, (wide, wide), 1), 16
    )
    folded = jnp.sum(jnp.where(same, total[...], 0.0).reshape(vecs, 16, wide), axis=1)
    gram = jnp.zeros((vecs, width_y), F32)
    lane = lax.broadcasted_iota(jnp.int32, (width_y, width_y), 0)
    column = lax.broadcasted_iota(jnp.int32, (width_y, width_y), 1)
    for h in range(halves):
        pick = (lax.div(lane, 16) + h * (width_y // 16) == column).astype(F32)
        gram = gram + jnp.dot(
            folded[:, h * width_y : (h + 1) * width_y], pick,
            precision=lax.Precision.HIGHEST, preferred_element_type=F32,
        )
    part[0, pl.ds(0, vecs)] = gram
    part[0, pl.ds(vecs, 8)] = pack_sums(start)
    group_send(0, vecs + 8)
    image_pack(chunks - 1)
    for number in range(2, len(links)):
        image_start(number, 0)
    first_sum = group_sum(0, vecs + 8)
    gram = first_sum[:vecs, :vecs]
    start = unpack_sums(first_sum[vecs:], base)
    row_id = lax.broadcasted_iota(jnp.int32, (vecs, vecs), 0)
    eye = (row_id == lax.broadcasted_iota(jnp.int32, (vecs, vecs), 1)).astype(F32)
    wide_row = lax.broadcasted_iota(jnp.int32, (vecs, 2 * vecs), 0)
    system = jnp.concatenate([gram, eye], axis=1)
    for k in range(0, vecs, 2):
        col_0 = jnp.broadcast_to(system[:, k : k + 1], (vecs, 2 * vecs))
        col_1 = jnp.broadcast_to(system[:, k + 1 : k + 2], (vecs, 2 * vecs))
        top, low = system[k : k + 1], system[k + 1 : k + 2]
        p_00, p_01 = col_0[k : k + 1], col_1[k : k + 1]
        p_10, p_11 = col_0[k + 1 : k + 2], col_1[k + 1 : k + 2]
        scale = 1.0 / (p_00 * p_11 - p_01 * p_10)
        new_0 = (p_11 * top - p_01 * low) * scale
        new_1 = (p_00 * low - p_10 * top) * scale
        system = system - col_0 * new_0 - col_1 * new_1
        system = jnp.where(wide_row == k, new_0, jnp.where(wide_row == k + 1, new_1, system))
    inverse[...] = system[:, vecs:]

    def solve(column):
        answer = jnp.sum(inverse[...] * column, axis=0, keepdims=True)
        flat = jnp.sum(eye * column, axis=0, keepdims=True)
        return answer, jnp.sum(answer * flat, axis=1, keepdims=True)

    weights = [solve(start[s * vecs : (s + 1) * vecs])[0] for s in range(sources)]
    one = jnp.ones((1, 1), F32)
    combine(held.at[0], [(res_ref, [one] * sources)], [-w for w in weights], full_c)
    exchange_wait(0)
    image_wait()
    combine_halo(row_r, col_r, [(row_in.at[0], col_in.at[0], [one] * sources)])

    every = range(sources)
    for cycle in range(CYCLES):
        index = 2 * cycle
        resid = held.at[cycle]
        apply(resid, row_r, col_r, work)

        def meanwhile():
            exchange_start(index + 1, work)
            if cycle:
                accumulate(cycle - 1, *update)

        sums = step_sums(index + 1, work, [(resid, resid), (resid, work), (work, work)], meanwhile)
        state = []
        for s in every:
            def got(i):
                return sums[base + 3 * s + i : base + 3 * s + i + 1]

            beta = jnp.sqrt(got(0) + EPS)
            scale = 1.0 / beta
            raw, quad = solve(sums[s * vecs : (s + 1) * vecs])
            g_0 = raw * scale
            n_00 = got(0) * scale * scale
            h_00 = got(1) * scale * scale
            left = (got(2) - quad) * scale * scale - 2.0 * h_00 * h_00 + h_00 * h_00 * n_00
            left = jnp.maximum(left, 0.0)
            h_10 = jnp.sqrt(left + EPS)
            state.append((beta, scale, g_0, n_00, h_00, left, h_10))
        of_w = [v[1] / v[6] for v in state]
        of_r = [-v[4] * v[1] / v[6] for v in state]
        combine(krylov, [(work, of_w), (resid, of_r)], [-v[2] / v[6] for v in state], full_c)
        exchange_wait(index + 1)
        now = (row_in.at[index + 1], col_in.at[index + 1])
        combine_halo(row_v, col_v, [now + (of_w,), (row_r, col_r, of_r)])
        if cycle + 1 < n_tx - 1:
            gather_arrive(1, cycle + 1, 0, True)
        apply(krylov, row_v, col_v, work)

        def meanwhile():
            if cycle + 1 < CYCLES:
                exchange_start(index + 2, work)

        pairs = [(resid, work), (krylov, work), (work, work), (krylov, krylov)]
        sums = step_sums(index + 2, work, pairs, meanwhile)
        in_r, in_v, in_w, in_g, out_r, out_v = [], [], [], [], [], []
        for s in every:
            def got(i):
                return sums[base + 4 * s + i : base + 4 * s + i + 1]

            beta, scale, g_0, n_00, h_00, _, h_10 = state[s]
            g_1, quad = solve(sums[s * vecs : (s + 1) * vecs])
            h_01 = got(0) * scale
            h_11 = got(1)
            n_11 = got(3)
            n_01 = h_00 * (1.0 - n_00) / h_10
            left = (
                got(2) - quad - 2.0 * (h_01 * h_01 + h_11 * h_11)
                + h_01 * h_01 * n_00 + h_11 * h_11 * n_11 + 2.0 * h_01 * h_11 * n_01
            )
            h_21 = jnp.sqrt(jnp.maximum(left, 0.0) + EPS)
            a_00 = h_00 * h_00 + h_10 * h_10
            a_01 = h_00 * h_01 + h_10 * h_11
            a_11 = h_01 * h_01 + h_11 * h_11 + h_21 * h_21
            l_00 = jnp.sqrt(a_00)
            l_10 = a_01 / l_00
            l_11 = jnp.sqrt(a_11 - l_10 * l_10)
            f_0 = beta * h_00 / l_00
            f_1 = (beta * h_01 - l_10 * f_0) / l_11
            y_1 = f_1 / l_11
            y_0 = (f_0 - l_10 * y_1) / l_00
            t_0 = beta - h_00 * y_0 - h_01 * y_1
            t_1 = -(h_10 * y_0 + h_11 * y_1)
            t_2 = -h_21 * y_1
            share = t_2 / h_21
            in_r.append((t_0 - share * h_01) * scale)
            in_v.append(t_1 - share * h_11)
            in_w.append(share)
            in_g.append(-share * g_1)
            out_r.append(y_0 * scale)
            out_v.append(y_1)
            weights[s] = weights[s] - (g_0 * y_0 + g_1 * y_1)
        update = (out_r, out_v)
        target = held.at[cycle + 1] if cycle + 1 < CYCLES else res_ref
        combine(target, [(resid, in_r), (krylov, in_v), (work, in_w)], in_g, full_c)
        if cycle + 1 < CYCLES:
            exchange_wait(index + 2)
            now = (row_in.at[index + 2], col_in.at[index + 2])
            combine_halo(row_r, col_r, [(row_r, col_r, in_r), (row_v, col_v, in_v), now + (in_w,)])

    for step in range(CYCLES + 1, n_tx - 1):
        gather_arrive(1, step, 0, True)
    gather_arrive(1, n_tx - 1, 0)
    own[1].wait()
    terms = [(held.at[CYCLES - 1], update[0]), (krylov, update[1])]
    if CYCLES > 1:
        terms.append((sol_ref, [one] * sources))
    combine(sol_ref, terms, weights, full_u)
    gather_sent(0)
    gather_sent(1)
    for index in range(2 * CYCLES):
        for number in range(len(links)):
            @pl.when(links[number][5])
            def _():
                halo_copy(index, number).wait_send()
    for number, piece in image_copies:
        @pl.when(links[number][5])
        def _():
            image_copy(number, piece).wait_send()


def on_device(dims, src_cell, basis, images, induction):
    n_gx, n_gy, n_tx = dims
    per_dev, _, _, depth, width_x, width_y = basis.shape
    sources = src_cell.shape[0]
    tiles = 6 * depth
    rows = tiles * width_x
    vecs = per_dev * n_tx
    group = n_gx * n_gy
    field = (sources, tiles, width_x, width_y)
    ind_rows = 3 * induction.shape[1] * width_x
    most = vecs + 8
    sums, halos = 2 * CYCLES + 1, 2 * CYCLES
    dma = pltpu.SemaphoreType.DMA
    vmem = pl.BlockSpec(memory_space=pltpu.VMEM)
    hbm = pl.BlockSpec(memory_space=pl.ANY)
    chunks = tiles // 16
    out = pl.pallas_call(
        functools.partial(kernel, dims),
        out_shape=(jax.ShapeDtypeStruct(field, F32),) * 2,
        in_specs=[pl.BlockSpec(memory_space=pltpu.SMEM), hbm, hbm, vmem],
        out_specs=(vmem, vmem),
        scratch_shapes=[
            pltpu.VMEM((vecs, rows, width_y), jnp.bfloat16),
            pltpu.VMEM((vecs, rows, width_y), jnp.bfloat16),
            pltpu.VMEM((n_tx, ind_rows, width_y), jnp.bfloat16),
            pltpu.VMEM((3, depth, width_x, width_y), F32),
            pltpu.VMEM(field, F32),
            pltpu.VMEM(field, F32),
            pltpu.VMEM((vecs * 16, vecs * 16), F32),
            pltpu.VMEM((vecs, vecs), F32),
            pltpu.VMEM((sources, vecs, width_x, width_y), F32),
            pltpu.VMEM((CYCLES,) + field, F32),
            pltpu.VMEM((sums, most, width_y), F32),
            pltpu.VMEM((sums, group, most, width_y), F32),
            pltpu.VMEM((halos, 2, sources * tiles, width_y), F32),
            pltpu.VMEM((halos, 2, sources * tiles, width_y), F32),
            pltpu.VMEM((halos, 2, width_x, width_y), F32),
            pltpu.VMEM((halos, 4, width_x, width_y), F32),
            pltpu.VMEM((2, chunks, vecs * 16, width_y), F32),
            pltpu.VMEM((2, chunks, vecs * 16, width_y), F32),
            pltpu.VMEM((2, vecs, width_x, width_y), F32),
            pltpu.VMEM((4, vecs, width_x, width_y), F32),
            pltpu.VMEM((2, sources * tiles, width_y), F32),
            pltpu.VMEM((2, sources * tiles, width_y), F32),
            pltpu.VMEM((4, width_x, width_y), F32),
            pltpu.VMEM((4, width_x, width_y), F32),
            dma((2,)),
            dma((2, 2, n_tx - 1, chunks)),
            dma((2, 2, n_tx - 1, chunks)),
            dma((n_tx - 1,)),
            dma((n_tx - 1,)),
            dma((sums, group - 1)),
            dma((sums, group - 1)),
            dma((halos, 6)),
            dma((halos, 6)),
            dma((2 * chunks + 4,)),
            dma((2 * chunks + 4,)),
        ],
        compiler_params=pltpu.CompilerParams(
            collective_id=0, has_side_effects=True, vmem_limit_bytes=60 * 1024 * 1024
        ),
        cost_estimate=pl.CostEstimate(flops=400_000_000, bytes_accessed=2_000_000, transcendentals=20_000),
    )(
        src_cell,
        basis.reshape(per_dev, rows, width_y),
        images.reshape(per_dev, rows, width_y),
        induction.reshape(ind_rows, width_y),
    )
    shape = (sources, 2, 3, depth, width_x, width_y)
    return tuple(o.reshape(shape) for o in out)


def solution(mesh):
    dims = (mesh.shape["gx"], mesh.shape["gy"], mesh.shape["tx"])
    spec = P("tx", None, None, None, "gx", "gy")
    return jax.shard_map(
        functools.partial(on_device, dims),
        mesh=mesh,
        in_specs=(P("tx"), spec, spec, P(None, "tx", "gx", "gy")),
        out_specs=(spec, spec),
        check_vma=False,
    )
```

```python
import functools

import jax
import jax.numpy as jnp
from jax import lax
from jax.experimental import pallas as pl
from jax.experimental.pallas import tpu as pltpu
from jax.sharding import PartitionSpec as P

CYCLES = 2
ARNOLDI = 2
EPS = 1e-06
MESH = pl.DeviceIdType.MESH
F32 = jnp.float32


def kernel(
    dims, pos_ref, u_ref, c_ref, m_ref, sol_ref, res_ref,
    full_c, full_u, ind_all, induct, krylov, work, total, inverse, coef, held,
    part, parts, row_out, row_in, col_out, col_in,
    img_row_out, img_row_in, img_col_out, img_col_in, row_r, row_v, col_r, col_v,
    own_sem, gather_send, gather_recv, ind_send, ind_recv, sum_send, sum_recv, halo_send, halo_recv,
    img_send, img_recv,
):
    n_gx, n_gy, n_tx = dims
    gx, gy, tx = lax.axis_index("gx"), lax.axis_index("gy"), lax.axis_index("tx")
    group = n_gx * n_gy
    rank = gx * n_gy + gy
    sources = pos_ref.shape[0]
    per_dev = c_ref.shape[0]
    rows = c_ref.shape[1]
    width_y = c_ref.shape[2]
    width_x = 8
    depth = induct.shape[1]
    tiles = rows // width_x
    vecs = full_c.shape[0]
    half = tiles // 2
    chunk = 16 * width_x
    chunks = rows // chunk

    def peer_of(offset):
        other = lax.rem(rank + offset, group)
        return (lax.div(other, n_gy), lax.rem(other, n_gy), tx)

    def along(offset):
        return (gx, gy, lax.rem(tx + offset, n_tx))

    barrier = pltpu.get_barrier_semaphore()
    for offset in range(1, group):
        pl.semaphore_signal(barrier, inc=1, device_id=peer_of(offset), device_id_type=MESH)
    for offset in range(1, n_tx):
        pl.semaphore_signal(barrier, inc=1, device_id=along(offset), device_id_type=MESH)
    pl.semaphore_wait(barrier, group - 1 + n_tx - 1)

    def slot(shard):
        return pl.ds(shard * per_dev, per_dev)

    def rows_at(which, piece):
        return pl.ds(piece * chunk, chunk) if which == 0 else pl.ds(0, rows)

    pieces = (chunks, 1)

    def hop(which, way, step, piece):
        full = (full_c, full_u)[which]
        at = rows_at(which, piece)
        sign = 1 if way == 0 else -1
        shard = tx - sign * (step - 1)
        source = (c_ref, u_ref)[which].at[:, at] if step == 1 else full.at[slot(shard), at]
        return pltpu.make_async_remote_copy(
            src_ref=source,
            dst_ref=full.at[slot(shard), at],
            send_sem=gather_send.at[which, way, step - 1, piece],
            recv_sem=gather_recv.at[which, way, step - 1, piece],
            device_id=(gx, gy, tx + sign),
            device_id_type=MESH,
        )

    def sends(way, step):
        if way == 0:
            return jnp.logical_and(tx + 1 < n_tx, tx - step + 1 >= 0)
        return jnp.logical_and(tx - 1 >= 0, tx + step - 1 < n_tx)

    def receives(way, step):
        return tx - step >= 0 if way == 0 else tx + step < n_tx

    def forwards(way, step):
        return sends(way, step + 1)

    def gather_start(which, way, piece, when):
        @pl.when(jnp.logical_and(sends(way, 1), when))
        def _():
            hop(which, way, 1, piece).start()

    def gather_arrive(which, way, step, piece, when):
        @pl.when(jnp.logical_and(receives(way, step), when))
        def _():
            full = (full_c, full_u)[which]
            at = rows_at(which, piece)
            shard = tx - step if way == 0 else tx + step
            pltpu.make_async_remote_copy(
                src_ref=full.at[slot(shard), at],
                dst_ref=full.at[slot(shard), at],
                send_sem=gather_send.at[which, way, step - 1, piece],
                recv_sem=gather_recv.at[which, way, step - 1, piece],
                device_id=along(1),
                device_id_type=MESH,
            ).wait_recv()

    def gather_forward(which, step, piece):
        for way in range(2):
            gather_arrive(which, way, step, piece, forwards(way, step))

            @pl.when(forwards(way, step))
            def _():
                hop(which, way, step + 1, piece).start()

    def gather_rest(which, piece):
        for step in range(1, n_tx):
            for way in range(2):
                gather_arrive(which, way, step, piece, jnp.logical_not(forwards(way, step)))

    def gather_sent(which):
        for piece in range(pieces[which]):
            for step in range(1, n_tx):
                for way in range(2):
                    @pl.when(sends(way, step))
                    def _():
                        hop(which, way, step, piece).wait_send()

    own = [
        pltpu.make_async_copy(ref, full.at[slot(tx)], own_sem.at[number])
        for number, (ref, full) in enumerate(((c_ref, full_c), (u_ref, full_u)))
    ]
    own.append(pltpu.make_async_copy(m_ref, ind_all.at[tx], own_sem.at[2]))

    def ind_copy(offset):
        return pltpu.make_async_remote_copy(
            src_ref=m_ref,
            dst_ref=ind_all.at[tx],
            send_sem=ind_send.at[offset - 1],
            recv_sem=ind_recv.at[offset - 1],
            device_id=along(offset),
            device_id_type=MESH,
        )

    for offset in range(1, n_tx):
        ind_copy(offset).start()
    for piece in range(chunks):
        for way in range(2):
            gather_start(0, way, piece, True)
    for way in range(2):
        gather_start(1, way, 0, jnp.logical_not(forwards(way, 1)))
    for copy in own:
        copy.start()
    own[2].wait()
    for offset in range(1, n_tx):
        ind_copy(offset).wait()
    layers = depth // n_tx
    for owner in range(n_tx):
        piece = ind_all[owner].astype(F32).reshape(3, layers, width_x, width_y)
        for layer in range(layers):
            induct[:, owner * layers + layer] = piece[:, layer]

    size_x, size_y = width_x * n_gx, width_y * n_gy
    shape = (depth, width_x, width_y)
    z_pos = lax.broadcasted_iota(jnp.int32, shape, 0).astype(F32)
    x_pos = (gx * width_x + lax.broadcasted_iota(jnp.int32, shape, 1)).astype(F32)
    y_pos = (gy * width_y + lax.broadcasted_iota(jnp.int32, shape, 2)).astype(F32)
    for s in range(sources):
        cell = pos_ref[s]
        rest = lax.rem(cell, size_x * size_y)
        d_z = z_pos - lax.div(cell, size_x * size_y).astype(F32)
        d_x = x_pos - lax.div(rest, size_y).astype(F32)
        d_y = y_pos - lax.rem(rest, size_y).astype(F32)
        dist = jnp.sqrt(d_z * d_z + d_x * d_x + d_y * d_y)
        primary = jnp.exp(-dist / ((size_x + size_y) / 8.0))
        for comp, weight in enumerate((1.0, 0.5, 0.25)):
            real = (induct[comp] - 1.0) * weight * primary
            res_ref[s, pl.ds(comp * depth, depth)] = real
            res_ref[s, pl.ds(half + comp * depth, depth)] = 0.5 * real

    base = sources * vecs

    def sum_copy(index, count, offset):
        return pltpu.make_async_remote_copy(
            src_ref=part.at[index, pl.ds(0, count)],
            dst_ref=parts.at[index, rank, pl.ds(0, count)],
            send_sem=sum_send.at[index, offset - 1],
            recv_sem=sum_recv.at[index, offset - 1],
            device_id=peer_of(offset),
            device_id_type=MESH,
        )

    def group_send(index, count):
        for offset in range(1, group):
            sum_copy(index, count, offset).start()
        parts[index, pl.ds(rank, 1), pl.ds(0, count)] = part[index, pl.ds(0, count)][None]

    def group_sum(index, count):
        for offset in range(1, group):
            sum_copy(index, count, offset).wait()
        return jnp.sum(parts[index, :, pl.ds(0, count)], axis=0)

    def products(field, pairs, first, count, sums):
        def body(j, sums):
            sums = list(sums)
            at = pl.ds(pl.multiple_of(j * 16, 16), 16)
            pair = pl.ds(j * 2, 2)
            values = [field[s, pair] for s in range(sources)]
            for k in range(vecs):
                vector = full_c[k, at].astype(F32).reshape(2, width_x, width_y)
                for s in range(sources):
                    sums[s * vecs + k] += jnp.sum(vector * values[s], axis=0)
            for i, (left, right) in enumerate(pairs):
                for s in range(sources):
                    sums[base + s * len(pairs) + i] += jnp.sum(left[s, pair] * right[s, pair], axis=0)
            return tuple(sums)

        return lax.fori_loop(first, first + count, body, tuple(sums), unroll=2)

    def blank(count):
        return [jnp.zeros((width_x, width_y), F32)] * count

    def pack_sums(sums):
        lane = lax.broadcasted_iota(jnp.int32, (width_x, width_y), 1)
        packed = jnp.zeros((width_x, width_y), F32)
        for i, value in enumerate(sums):
            packed = jnp.where(lane == i, jnp.sum(value, axis=1, keepdims=True), packed)
        return packed

    def unpack_sums(packed, count):
        row = jnp.sum(packed, axis=0, keepdims=True)
        size = (count, width_y)
        mask = lax.broadcasted_iota(jnp.int32, size, 0) == lax.broadcasted_iota(jnp.int32, size, 1)
        return jnp.sum(jnp.where(mask, row, 0.0), axis=1, keepdims=True)

    def step_sums(index, field, pairs, meanwhile):
        count = base + sources * len(pairs)
        part[index, pl.ds(0, 8)] = pack_sums(products(field, pairs, 0, tiles // 2, blank(count)))
        group_send(index, 8)
        meanwhile()
        return unpack_sums(group_sum(index, 8), count)

    def spread(value):
        return jnp.broadcast_to(value, (width_x, width_y))

    def combine(out, terms, rows_of, stack):
        for s in range(sources):
            for k in range(vecs):
                coef[s, k] = spread(rows_of[s][:, k : k + 1])
        wide = [[spread(c[s]) for s in range(sources)] for _, c in terms]

        def body(j, _):
            at = pl.ds(pl.multiple_of(j * 16, 16), 16)
            pair = pl.ds(j * 2, 2)
            totals = []
            for s in range(sources):
                value = None
                for (ref, _), w in zip(terms, wide):
                    now = ref[s, pair] * w[s][None]
                    value = now if value is None else value + now
                totals.append(value)
            for k in range(vecs):
                vector = stack[k, at, :].astype(F32).reshape(2, width_x, width_y)
                for s in range(sources):
                    totals[s] = totals[s] + vector * coef[s, k][None]
            for s in range(sources):
                out[s, pair] = totals[s]
            return 0

        lax.fori_loop(0, tiles // 2, body, 0, unroll=3)

    def accumulate(cycle, of_r, of_v):
        wide = [[spread(c[s]) for s in range(sources)] for c in (of_r, of_v)]

        def body(j, _):
            pair = pl.ds(j * 4, 4)
            for s in range(sources):
                value = held[cycle, s, pair] * wide[0][s][None] + krylov[s, pair] * wide[1][s][None]
                if cycle:
                    value = value + sol_ref[s, pair]
                sol_ref[s, pair] = value
            return 0

        lax.fori_loop(0, tiles // 4, body, 0)

    east, west = gx + 1 < n_gx, gx >= 1
    north, south = gy + 1 < n_gy, gy >= 1
    lane2 = lax.broadcasted_iota(jnp.int32, (depth, width_y), 1)
    layer2 = lax.broadcasted_iota(jnp.int32, (depth, width_y), 0)
    layer3 = lax.broadcasted_iota(jnp.int32, shape, 0)
    row3 = lax.broadcasted_iota(jnp.int32, shape, 1)
    lane3 = lax.broadcasted_iota(jnp.int32, shape, 2)
    both = jnp.logical_and
    links = (
        (row_out, 1, row_in, 0, (1, 0), east, west),
        (row_out, 0, row_in, 1, (-1, 0), west, east),
        (col_out, 1, col_in, 0, (0, 1), north, south),
        (col_out, 0, col_in, 1, (0, -1), south, north),
        (col_out, 1, col_in, 2, (-1, 1), both(west, north), both(east, south)),
        (col_out, 0, col_in, 3, (1, -1), both(east, south), both(west, north)),
    )

    def halo_copy(index, number):
        src, which, dst, place, (d_x, d_y), _, _ = links[number]
        return pltpu.make_async_remote_copy(
            src_ref=src.at[index, which],
            dst_ref=dst.at[index, place],
            send_sem=halo_send.at[index, number],
            recv_sem=halo_recv.at[index, number],
            device_id=(gx + d_x, gy + d_y, tx),
            device_id_type=MESH,
        )

    lanes = lax.broadcasted_iota(jnp.int32, (tiles, width_x, width_y), 2)
    places = lax.broadcasted_iota(jnp.int32, (tiles, width_x, width_y), 0)

    def exchange_start(index, field):
        first = jnp.zeros((width_x, width_y), F32)
        last = jnp.zeros((width_x, width_y), F32)
        for s in range(sources):
            value = field[s]
            here = lanes == places + s * tiles
            first = first + jnp.sum(jnp.where(here, value[:, :, 0:1], 0.0), axis=0)
            last = last + jnp.sum(jnp.where(here, value[:, :, width_y - 1 : width_y], 0.0), axis=0)
            row_out[index, 0, pl.ds(s * tiles, tiles)] = value[:, 0, :]
            row_out[index, 1, pl.ds(s * tiles, tiles)] = value[:, width_x - 1, :]
        col_out[index, 0] = first
        col_out[index, 1] = last
        for number in range(len(links)):
            @pl.when(links[number][5])
            def _():
                halo_copy(index, number).start()

    def exchange_wait(index):
        for number in range(len(links)):
            dst, place, got = links[number][2], links[number][3], links[number][6]

            @pl.when(jnp.logical_not(got))
            def _():
                dst[index, place] = jnp.zeros(dst.shape[2:], F32)

            @pl.when(got)
            def _():
                halo_copy(index, number).wait_recv()

    def image_copy(number, piece):
        _, which, _, place, (d_x, d_y), _, _ = links[number]
        if number < 2:
            src, dst, sem = img_row_out.at[which, piece], img_row_in.at[place, piece], number * chunks + piece
        else:
            src, dst, sem = img_col_out.at[which], img_col_in.at[place], 2 * chunks + number - 2
        return pltpu.make_async_remote_copy(
            src_ref=src,
            dst_ref=dst,
            send_sem=img_send.at[sem],
            recv_sem=img_recv.at[sem],
            device_id=(gx + d_x, gy + d_y, tx),
            device_id_type=MESH,
        )

    image_copies = [(number, piece) for number in range(2) for piece in range(chunks)]
    image_copies += [(number, 0) for number in range(2, len(links))]

    def image_start(number, piece):
        @pl.when(links[number][5])
        def _():
            image_copy(number, piece).start()

    def image_pack(piece):
        size = (16, width_x, width_y)
        lane = lax.broadcasted_iota(jnp.int32, size, 2)
        tile = lax.broadcasted_iota(jnp.int32, size, 0) + piece * 16
        here = lane == tile
        for s in range(1, sources):
            here = jnp.logical_or(here, lane == tile + s * tiles)

        def body(k, _):
            value = full_c[k, pl.ds(piece * chunk, chunk)].astype(F32).reshape(size)
            for side, (row, col) in enumerate(((0, 0), (width_x - 1, width_y - 1))):
                img_row_out[side, piece, pl.ds(pl.multiple_of(k * 16, 16), 16)] = value[:, row, :]
                column = jnp.sum(jnp.where(here, value[:, :, col : col + 1], 0.0), axis=0)
                if piece:
                    column = column + img_col_out[side, k]
                img_col_out[side, k] = column
            return 0

        lax.fori_loop(0, vecs, body, 0, unroll=4)
        for number in range(2):
            image_start(number, piece)

    def image_wait():
        for number, piece in image_copies:
            place, got = links[number][3], links[number][6]

            @pl.when(jnp.logical_not(got))
            def _():
                if number < 2:
                    img_row_in[place, piece] = jnp.zeros(img_row_in.shape[2:], F32)
                else:
                    img_col_in[place] = jnp.zeros(img_col_in.shape[1:], F32)

            @pl.when(got)
            def _():
                image_copy(number, piece).wait_recv()

    def by_lane(values):
        lane = lax.broadcasted_iota(jnp.int32, (width_x, width_y), 1)
        result = values[0]
        for s in range(1, sources):
            result = jnp.where(lane >= s * tiles, values[s], result)
        return result

    def combine_halo(row, col, terms):
        wide = [[spread(c[s]) for s in range(sources)] for _, _, c in terms]

        def body(i, _):
            place, piece = lax.div(i, chunks), lax.rem(i, chunks)
            totals = []
            for s in range(sources):
                at = pl.ds(pl.multiple_of(s * tiles + piece * 16, 8), 16)
                value = None
                for (ref, _, _), w in zip(terms, wide):
                    now = ref[place, at].reshape(2, width_x, width_y) * w[s][None]
                    value = now if value is None else value + now
                totals.append(value)
            for k in range(vecs):
                vector = img_row_in[place, piece, pl.ds(k * 16, 16)].reshape(2, width_x, width_y)
                for s in range(sources):
                    totals[s] = totals[s] + vector * coef[s, k][None]
            for s in range(sources):
                at = pl.ds(pl.multiple_of(s * tiles + piece * 16, 8), 16)
                row[place, at] = totals[s].reshape(16, width_y)
            return 0

        lax.fori_loop(0, 2 * chunks, body, 0)
        values = [None] * 4
        for (_, ref, _), w in zip(terms, wide):
            scale = by_lane(w)
            for place in range(4):
                now = ref[place] * scale
                values[place] = now if values[place] is None else values[place] + now
        for k in range(vecs):
            scale = by_lane([coef[s, k] for s in range(sources)])
            for place in range(4):
                values[place] = values[place] + img_col_in[place, k] * scale
        for place in range(4):
            col[place] = values[place]

    def apply(field, row_halo, col_halo, out):
        def columns(place, at):
            packed = col_halo[place][None]
            return jnp.sum(jnp.where(lane3 == layer3 + at, packed, 0.0), axis=2, keepdims=True)

        def corner(place, row, at):
            packed = col_halo[place, row : row + 1]
            return jnp.sum(jnp.where(lane2 == layer2 + at, packed, 0.0), axis=1, keepdims=True)

        def plus_y(f, edge):
            return jnp.where(lane3 == width_y - 1, edge, pltpu.roll(f, width_y - 1, 2))

        def minus_y(f, edge):
            return jnp.where(lane3 == 0, edge, pltpu.roll(f, 1, 2))

        def plus_x(f, row):
            return jnp.where(row3 == width_x - 1, row[:, None, :], pltpu.roll(f, width_x - 1, 1))

        def minus_x(f, row):
            return jnp.where(row3 == 0, row[:, None, :], pltpu.roll(f, 1, 1))

        zero = jnp.zeros((1, width_x, width_y), F32)

        def plus_z(f):
            return jnp.concatenate([f[1:], zero], axis=0)

        def minus_z(f):
            return jnp.concatenate([zero, f[:-1]], axis=0)

        for s in range(sources):
            for p in range(2):
                def comp(c):
                    return field[s, pl.ds(p * half + c * depth, depth)]

                def at(c):
                    return s * tiles + p * half + c * depth

                def row(place, c):
                    return row_halo[place, pl.ds(at(c), depth)]

                e_x, e_y, e_z = comp(0), comp(1), comp(2)
                xp_y = plus_y(e_x, columns(1, at(0)))
                xm_y = minus_y(e_x, columns(0, at(0)))
                t = xp_y - e_x
                hx = row(0, 0)
                hx_up = jnp.where(lane2 == width_y - 1, corner(3, width_x - 1, at(0)), pltpu.roll(hx, width_y - 1, 1))
                dt = t - minus_x(t, hx_up - hx)
                c = e_x - minus_x(e_x, hx)
                a = e_y - minus_y(e_y, columns(0, at(1)))
                hy = row(1, 1)
                hy_down = jnp.where(lane2 == 0, corner(2, 0, at(1)), pltpu.roll(hy, 1, 1))
                da = plus_x(a, hy - hy_down) - a
                y2 = plus_x(e_y, hy) + minus_x(e_y, row(0, 1)) - 2.0 * e_y
                zp_x = plus_x(e_z, row(1, 2))
                zp_y = plus_y(e_z, columns(1, at(2)))
                z2 = zp_x + minus_x(e_z, row(0, 2)) + zp_y + minus_y(e_z, columns(0, at(2))) - 4.0 * e_z
                fx_z = zp_x - e_z
                fy_z = zp_y - e_z
                k_x = da - (xp_y + xm_y + plus_z(e_x) + minus_z(e_x) - 4.0 * e_x) + (fx_z - minus_z(fx_z))
                k_y = (fy_z - minus_z(fy_z)) - (plus_z(e_y) + minus_z(e_y) - 2.0 * e_y) - y2 + dt
                ca = c + a
                k_z = (plus_z(ca) - ca) - z2
                for number, value in enumerate((k_x, k_y, k_z)):
                    cross = induct[number] * field[s, pl.ds((1 - p) * half + number * depth, depth)]
                    value = value - cross if p == 0 else value + cross
                    out[s, pl.ds(p * half + number * depth, depth)] = value

    exchange_start(0, res_ref)
    total[...] = jnp.zeros_like(total)

    def gram_body(j, _):
        block = full_c[:, pl.ds(pl.multiple_of(j * 16, 16), 16), :].reshape(vecs * 16, width_y)
        total[...] += lax.dot_general(block, block, (((1,), (1,)), ((), ())), preferred_element_type=F32)
        return 0

    wide = vecs * 16
    halves = wide // width_y
    start = blank(base)
    own[0].wait()
    for piece in range(chunks):
        for step in range(1, n_tx - 1):
            gather_forward(0, step, piece)
        if piece + 1 == chunks:
            for way in range(2):
                gather_start(1, way, 0, forwards(way, 1))
        gather_rest(0, piece)
        lax.fori_loop(piece * (chunk // 16), (piece + 1) * (chunk // 16), gram_body, 0)
        start = products(res_ref, [], piece * 8, 8, start)
        if piece + 1 < chunks:
            image_pack(piece)
    same = lax.rem(lax.broadcasted_iota(jnp.int32, (wide, wide), 0), 16) == lax.rem(
        lax.broadcasted_iota(jnp.int32, (wide, wide), 1), 16
    )
    folded = jnp.sum(jnp.where(same, total[...], 0.0).reshape(vecs, 16, wide), axis=1)
    gram = jnp.zeros((vecs, width_y), F32)
    lane = lax.broadcasted_iota(jnp.int32, (width_y, width_y), 0)
    column = lax.broadcasted_iota(jnp.int32, (width_y, width_y), 1)
    for h in range(halves):
        pick = (lax.div(lane, 16) + h * (width_y // 16) == column).astype(F32)
        gram = gram + jnp.dot(
            folded[:, h * width_y : (h + 1) * width_y], pick,
            precision=lax.Precision.HIGHEST, preferred_element_type=F32,
        )
    part[0, pl.ds(0, vecs)] = gram
    part[0, pl.ds(vecs, 8)] = pack_sums(start)
    group_send(0, vecs + 8)
    image_pack(chunks - 1)
    for number in range(2, len(links)):
        image_start(number, 0)
    first_sum = group_sum(0, vecs + 8)
    gram = first_sum[:vecs, :vecs]
    start = unpack_sums(first_sum[vecs:], base)
    row_id = lax.broadcasted_iota(jnp.int32, (vecs, vecs), 0)
    eye = (row_id == lax.broadcasted_iota(jnp.int32, (vecs, vecs), 1)).astype(F32)
    wide_row = lax.broadcasted_iota(jnp.int32, (vecs, 2 * vecs), 0)
    system = jnp.concatenate([gram, eye], axis=1)
    for k in range(0, vecs, 2):
        col_0 = jnp.broadcast_to(system[:, k : k + 1], (vecs, 2 * vecs))
        col_1 = jnp.broadcast_to(system[:, k + 1 : k + 2], (vecs, 2 * vecs))
        top, low = system[k : k + 1], system[k + 1 : k + 2]
        p_00, p_01 = col_0[k : k + 1], col_1[k : k + 1]
        p_10, p_11 = col_0[k + 1 : k + 2], col_1[k + 1 : k + 2]
        scale = 1.0 / (p_00 * p_11 - p_01 * p_10)
        new_0 = (p_11 * top - p_01 * low) * scale
        new_1 = (p_00 * low - p_10 * top) * scale
        system = system - col_0 * new_0 - col_1 * new_1
        system = jnp.where(wide_row == k, new_0, jnp.where(wide_row == k + 1, new_1, system))
    inverse[...] = system[:, vecs:]

    def solve(column):
        answer = jnp.sum(inverse[...] * column, axis=0, keepdims=True)
        flat = jnp.sum(eye * column, axis=0, keepdims=True)
        return answer, jnp.sum(answer * flat, axis=1, keepdims=True)

    weights = [solve(start[s * vecs : (s + 1) * vecs])[0] for s in range(sources)]
    one = jnp.ones((1, 1), F32)
    combine(held.at[0], [(res_ref, [one] * sources)], [-w for w in weights], full_c)
    exchange_wait(0)
    image_wait()
    combine_halo(row_r, col_r, [(row_in.at[0], col_in.at[0], [one] * sources)])

    every = range(sources)
    for cycle in range(CYCLES):
        index = 2 * cycle
        resid = held.at[cycle]
        apply(resid, row_r, col_r, work)

        def meanwhile():
            exchange_start(index + 1, work)
            if index + 1 < n_tx - 1:
                gather_forward(1, index + 1, 0)
            if cycle:
                accumulate(cycle - 1, *update)

        sums = step_sums(index + 1, work, [(resid, resid), (resid, work), (work, work)], meanwhile)
        state = []
        for s in every:
            def got(i):
                return sums[base + 3 * s + i : base + 3 * s + i + 1]

            beta = jnp.sqrt(got(0) + EPS)
            scale = 1.0 / beta
            raw, quad = solve(sums[s * vecs : (s + 1) * vecs])
            g_0 = raw * scale
            n_00 = got(0) * scale * scale
            h_00 = got(1) * scale * scale
            left = (got(2) - quad) * scale * scale - 2.0 * h_00 * h_00 + h_00 * h_00 * n_00
            left = jnp.maximum(left, 0.0)
            h_10 = jnp.sqrt(left + EPS)
            state.append((beta, scale, g_0, n_00, h_00, left, h_10))
        of_w = [v[1] / v[6] for v in state]
        of_r = [-v[4] * v[1] / v[6] for v in state]
        combine(krylov, [(work, of_w), (resid, of_r)], [-v[2] / v[6] for v in state], full_c)
        exchange_wait(index + 1)
        now = (row_in.at[index + 1], col_in.at[index + 1])
        combine_halo(row_v, col_v, [now + (of_w,), (row_r, col_r, of_r)])
        apply(krylov, row_v, col_v, work)

        def meanwhile():
            if cycle + 1 < CYCLES:
                exchange_start(index + 2, work)
            if index + 2 < n_tx - 1:
                gather_forward(1, index + 2, 0)

        pairs = [(resid, work), (krylov, work), (work, work), (krylov, krylov)]
        sums = step_sums(index + 2, work, pairs, meanwhile)
        in_r, in_v, in_w, in_g, out_r, out_v = [], [], [], [], [], []
        for s in every:
            def got(i):
                return sums[base + 4 * s + i : base + 4 * s + i + 1]

            beta, scale, g_0, n_00, h_00, _, h_10 = state[s]
            g_1, quad = solve(sums[s * vecs : (s + 1) * vecs])
            h_01 = got(0) * scale
            h_11 = got(1)
            n_11 = got(3)
            n_01 = h_00 * (1.0 - n_00) / h_10
            left = (
                got(2) - quad - 2.0 * (h_01 * h_01 + h_11 * h_11)
                + h_01 * h_01 * n_00 + h_11 * h_11 * n_11 + 2.0 * h_01 * h_11 * n_01
            )
            h_21 = jnp.sqrt(jnp.maximum(left, 0.0) + EPS)
            a_00 = h_00 * h_00 + h_10 * h_10
            a_01 = h_00 * h_01 + h_10 * h_11
            a_11 = h_01 * h_01 + h_11 * h_11 + h_21 * h_21
            l_00 = jnp.sqrt(a_00)
            l_10 = a_01 / l_00
            l_11 = jnp.sqrt(a_11 - l_10 * l_10)
            f_0 = beta * h_00 / l_00
            f_1 = (beta * h_01 - l_10 * f_0) / l_11
            y_1 = f_1 / l_11
            y_0 = (f_0 - l_10 * y_1) / l_00
            t_0 = beta - h_00 * y_0 - h_01 * y_1
            t_1 = -(h_10 * y_0 + h_11 * y_1)
            t_2 = -h_21 * y_1
            share = t_2 / h_21
            in_r.append((t_0 - share * h_01) * scale)
            in_v.append(t_1 - share * h_11)
            in_w.append(share)
            in_g.append(-share * g_1)
            out_r.append(y_0 * scale)
            out_v.append(y_1)
            weights[s] = weights[s] - (g_0 * y_0 + g_1 * y_1)
        update = (out_r, out_v)
        target = held.at[cycle + 1] if cycle + 1 < CYCLES else res_ref
        combine(target, [(resid, in_r), (krylov, in_v), (work, in_w)], in_g, full_c)
        if cycle + 1 < CYCLES:
            exchange_wait(index + 2)
            now = (row_in.at[index + 2], col_in.at[index + 2])
            combine_halo(row_r, col_r, [(row_r, col_r, in_r), (row_v, col_v, in_v), now + (in_w,)])

    for step in range(2 * CYCLES + 1, n_tx - 1):
        gather_forward(1, step, 0)
    gather_rest(1, 0)
    own[1].wait()
    terms = [(held.at[CYCLES - 1], update[0]), (krylov, update[1])]
    if CYCLES > 1:
        terms.append((sol_ref, [one] * sources))
    combine(sol_ref, terms, weights, full_u)
    gather_sent(0)
    gather_sent(1)
    for index in range(2 * CYCLES):
        for number in range(len(links)):
            @pl.when(links[number][5])
            def _():
                halo_copy(index, number).wait_send()
    for number, piece in image_copies:
        @pl.when(links[number][5])
        def _():
            image_copy(number, piece).wait_send()


def on_device(dims, src_cell, basis, images, induction):
    n_gx, n_gy, n_tx = dims
    per_dev, _, _, depth, width_x, width_y = basis.shape
    sources = src_cell.shape[0]
    tiles = 6 * depth
    rows = tiles * width_x
    vecs = per_dev * n_tx
    group = n_gx * n_gy
    field = (sources, tiles, width_x, width_y)
    ind_rows = 3 * induction.shape[1] * width_x
    most = vecs + 8
    sums, halos = 2 * CYCLES + 1, 2 * CYCLES
    dma = pltpu.SemaphoreType.DMA
    vmem = pl.BlockSpec(memory_space=pltpu.VMEM)
    hbm = pl.BlockSpec(memory_space=pltpu.HBM)
    chunks = tiles // 16
    out = pl.pallas_call(
        functools.partial(kernel, dims),
        out_shape=(jax.ShapeDtypeStruct(field, F32),) * 2,
        in_specs=[pl.BlockSpec(memory_space=pltpu.SMEM), hbm, hbm, hbm],
        out_specs=(vmem, vmem),
        scratch_shapes=[
            pltpu.VMEM((vecs, rows, width_y), jnp.bfloat16),
            pltpu.VMEM((vecs, rows, width_y), jnp.bfloat16),
            pltpu.VMEM((n_tx, ind_rows, width_y), jnp.bfloat16),
            pltpu.VMEM((3, depth, width_x, width_y), F32),
            pltpu.VMEM(field, F32),
            pltpu.VMEM(field, F32),
            pltpu.VMEM((vecs * 16, vecs * 16), F32),
            pltpu.VMEM((vecs, vecs), F32),
            pltpu.VMEM((sources, vecs, width_x, width_y), F32),
            pltpu.VMEM((CYCLES,) + field, F32),
            pltpu.VMEM((sums, most, width_y), F32),
            pltpu.VMEM((sums, group, most, width_y), F32),
            pltpu.VMEM((halos, 2, sources * tiles, width_y), F32),
            pltpu.VMEM((halos, 2, sources * tiles, width_y), F32),
            pltpu.VMEM((halos, 2, width_x, width_y), F32),
            pltpu.VMEM((halos, 4, width_x, width_y), F32),
            pltpu.VMEM((2, chunks, vecs * 16, width_y), F32),
            pltpu.VMEM((2, chunks, vecs * 16, width_y), F32),
            pltpu.VMEM((2, vecs, width_x, width_y), F32),
            pltpu.VMEM((4, vecs, width_x, width_y), F32),
            pltpu.VMEM((2, sources * tiles, width_y), F32),
            pltpu.VMEM((2, sources * tiles, width_y), F32),
            pltpu.VMEM((4, width_x, width_y), F32),
            pltpu.VMEM((4, width_x, width_y), F32),
            dma((3,)),
            dma((2, 2, n_tx - 1, chunks)),
            dma((2, 2, n_tx - 1, chunks)),
            dma((n_tx - 1,)),
            dma((n_tx - 1,)),
            dma((sums, group - 1)),
            dma((sums, group - 1)),
            dma((halos, 6)),
            dma((halos, 6)),
            dma((2 * chunks + 4,)),
            dma((2 * chunks + 4,)),
        ],
        compiler_params=pltpu.CompilerParams(
            collective_id=0, has_side_effects=True, vmem_limit_bytes=48 * 1024 * 1024
        ),
        cost_estimate=pl.CostEstimate(flops=400_000_000, bytes_accessed=2_000_000, transcendentals=20_000),
    )(
        src_cell,
        basis.reshape(per_dev, rows, width_y),
        images.reshape(per_dev, rows, width_y),
        induction.reshape(ind_rows, width_y),
    )
    shape = (sources, 2, 3, depth, width_x, width_y)
    return tuple(o.reshape(shape) for o in out)


def solution(mesh):
    dims = (mesh.shape["gx"], mesh.shape["gy"], mesh.shape["tx"])
    spec = P("tx", None, None, None, "gx", "gy")
    return jax.shard_map(
        functools.partial(on_device, dims),
        mesh=mesh,
        in_specs=(P("tx"), spec, spec, P(None, "tx", "gx", "gy")),
        out_specs=(spec, spec),
        check_vma=False,
    )
```

```python
import functools

import jax
import jax.numpy as jnp
from jax import lax
from jax.experimental import pallas as pl
from jax.experimental.pallas import tpu as pltpu
from jax.sharding import PartitionSpec as P

CYCLES = 2
ARNOLDI = 2
EPS = 1e-06
MESH = pl.DeviceIdType.MESH
F32 = jnp.float32


def kernel(
    dims, pos_ref, u_ref, c_ref, m_ref, sol_ref, res_ref,
    full_c, full_u, ind_all, induct, krylov, work, total, inverse, coef, held, wide_c,
    part, parts, row_out, row_in, col_out, col_in,
    img_row_out, img_row_in, img_col_out, img_col_in, row_r, row_v, col_r, col_v,
    own_sem, gather_send, gather_recv, ind_send, ind_recv, sum_send, sum_recv, halo_send, halo_recv,
    img_send, img_recv,
):
    n_gx, n_gy, n_tx = dims
    gx, gy, tx = lax.axis_index("gx"), lax.axis_index("gy"), lax.axis_index("tx")
    group = n_gx * n_gy
    rank = gx * n_gy + gy
    sources = pos_ref.shape[0]
    per_dev = c_ref.shape[0]
    rows = c_ref.shape[1]
    width_y = c_ref.shape[2]
    width_x = 8
    depth = induct.shape[1]
    tiles = rows // width_x
    vecs = full_c.shape[0]
    half = tiles // 2
    chunk = 16 * width_x
    chunks = rows // chunk

    def peer_of(offset):
        other = lax.rem(rank + offset, group)
        return (lax.div(other, n_gy), lax.rem(other, n_gy), tx)

    def along(offset):
        return (gx, gy, lax.rem(tx + offset, n_tx))

    barrier = pltpu.get_barrier_semaphore()
    for offset in range(1, group):
        pl.semaphore_signal(barrier, inc=1, device_id=peer_of(offset), device_id_type=MESH)
    for offset in range(1, n_tx):
        pl.semaphore_signal(barrier, inc=1, device_id=along(offset), device_id_type=MESH)
    pl.semaphore_wait(barrier, group - 1 + n_tx - 1)

    def slot(shard):
        return pl.ds(shard * per_dev, per_dev)

    def rows_at(which, piece):
        return pl.ds(piece * chunk, chunk) if which == 0 else pl.ds(0, rows)

    pieces = (chunks, 1)

    def hop(which, way, step, piece):
        full = (full_c, full_u)[which]
        at = rows_at(which, piece)
        sign = 1 if way == 0 else -1
        shard = tx - sign * (step - 1)
        source = (c_ref, u_ref)[which].at[:, at] if step == 1 else full.at[slot(shard), at]
        return pltpu.make_async_remote_copy(
            src_ref=source,
            dst_ref=full.at[slot(shard), at],
            send_sem=gather_send.at[which, way, step - 1, piece],
            recv_sem=gather_recv.at[which, way, step - 1, piece],
            device_id=(gx, gy, tx + sign),
            device_id_type=MESH,
        )

    def sends(way, step):
        if way == 0:
            return jnp.logical_and(tx + 1 < n_tx, tx - step + 1 >= 0)
        return jnp.logical_and(tx - 1 >= 0, tx + step - 1 < n_tx)

    def receives(way, step):
        return tx - step >= 0 if way == 0 else tx + step < n_tx

    def forwards(way, step):
        return sends(way, step + 1)

    def gather_start(which, way, piece, when):
        @pl.when(jnp.logical_and(sends(way, 1), when))
        def _():
            hop(which, way, 1, piece).start()

    def gather_arrive(which, way, step, piece, when):
        @pl.when(jnp.logical_and(receives(way, step), when))
        def _():
            full = (full_c, full_u)[which]
            at = rows_at(which, piece)
            shard = tx - step if way == 0 else tx + step
            pltpu.make_async_remote_copy(
                src_ref=full.at[slot(shard), at],
                dst_ref=full.at[slot(shard), at],
                send_sem=gather_send.at[which, way, step - 1, piece],
                recv_sem=gather_recv.at[which, way, step - 1, piece],
                device_id=along(1),
                device_id_type=MESH,
            ).wait_recv()

    def gather_forward(which, step, piece):
        for way in range(2):
            gather_arrive(which, way, step, piece, forwards(way, step))

            @pl.when(forwards(way, step))
            def _():
                hop(which, way, step + 1, piece).start()

    def gather_rest(which, piece):
        for step in range(1, n_tx):
            for way in range(2):
                gather_arrive(which, way, step, piece, jnp.logical_not(forwards(way, step)))

    def gather_sent(which):
        for piece in range(pieces[which]):
            for step in range(1, n_tx):
                for way in range(2):
                    @pl.when(sends(way, step))
                    def _():
                        hop(which, way, step, piece).wait_send()

    own = [
        pltpu.make_async_copy(ref, full.at[slot(tx)], own_sem.at[number])
        for number, (ref, full) in enumerate(((c_ref, full_c), (u_ref, full_u)))
    ]
    own.append(pltpu.make_async_copy(m_ref, ind_all.at[tx], own_sem.at[2]))

    def ind_copy(offset):
        return pltpu.make_async_remote_copy(
            src_ref=m_ref,
            dst_ref=ind_all.at[tx],
            send_sem=ind_send.at[offset - 1],
            recv_sem=ind_recv.at[offset - 1],
            device_id=along(offset),
            device_id_type=MESH,
        )

    for offset in range(1, n_tx):
        ind_copy(offset).start()
    for piece in range(min(2, chunks)):
        for way in range(2):
            gather_start(0, way, piece, True)
    for copy in own:
        copy.start()
    own[2].wait()
    for offset in range(1, n_tx):
        ind_copy(offset).wait()
    layers = depth // n_tx
    for owner in range(n_tx):
        piece = ind_all[owner].astype(F32).reshape(3, layers, width_x, width_y)
        for layer in range(layers):
            induct[:, owner * layers + layer] = piece[:, layer]

    size_x, size_y = width_x * n_gx, width_y * n_gy
    shape = (depth, width_x, width_y)
    z_pos = lax.broadcasted_iota(jnp.int32, shape, 0).astype(F32)
    x_pos = (gx * width_x + lax.broadcasted_iota(jnp.int32, shape, 1)).astype(F32)
    y_pos = (gy * width_y + lax.broadcasted_iota(jnp.int32, shape, 2)).astype(F32)
    for s in range(sources):
        cell = pos_ref[s]
        rest = lax.rem(cell, size_x * size_y)
        d_z = z_pos - lax.div(cell, size_x * size_y).astype(F32)
        d_x = x_pos - lax.div(rest, size_y).astype(F32)
        d_y = y_pos - lax.rem(rest, size_y).astype(F32)
        dist = jnp.sqrt(d_z * d_z + d_x * d_x + d_y * d_y)
        primary = jnp.exp(-dist / ((size_x + size_y) / 8.0))
        for comp, weight in enumerate((1.0, 0.5, 0.25)):
            real = (induct[comp] - 1.0) * weight * primary
            res_ref[s, pl.ds(comp * depth, depth)] = real
            res_ref[s, pl.ds(half + comp * depth, depth)] = 0.5 * real

    base = sources * vecs

    def sum_copy(index, count, offset):
        return pltpu.make_async_remote_copy(
            src_ref=part.at[index, pl.ds(0, count)],
            dst_ref=parts.at[index, rank, pl.ds(0, count)],
            send_sem=sum_send.at[index, offset - 1],
            recv_sem=sum_recv.at[index, offset - 1],
            device_id=peer_of(offset),
            device_id_type=MESH,
        )

    def group_send(index, count):
        for offset in range(1, group):
            sum_copy(index, count, offset).start()
        parts[index, pl.ds(rank, 1), pl.ds(0, count)] = part[index, pl.ds(0, count)][None]

    def group_sum(index, count):
        for offset in range(1, group):
            sum_copy(index, count, offset).wait()
        return jnp.sum(parts[index, :, pl.ds(0, count)], axis=0)

    def widen(piece):
        def body(k, _):
            vector = full_c[k, pl.ds(piece * chunk, chunk)].astype(F32)
            wide_c[k, pl.ds(piece * 16, 16)] = vector.reshape(16, width_x, width_y)
            return 0

        lax.fori_loop(0, vecs, body, 0, unroll=2)

    def products(field, pairs, first, count, sums):
        def body(j, sums):
            sums = list(sums)
            pair = pl.ds(j * 2, 2)
            values = [field[s, pair] for s in range(sources)]
            for k in range(vecs):
                vector = wide_c[k, pair]
                for s in range(sources):
                    sums[s * vecs + k] += jnp.sum(vector * values[s], axis=0)
            for i, (left, right) in enumerate(pairs):
                for s in range(sources):
                    sums[base + s * len(pairs) + i] += jnp.sum(left[s, pair] * right[s, pair], axis=0)
            return tuple(sums)

        return lax.fori_loop(first, first + count, body, tuple(sums), unroll=2)

    def blank(count):
        return [jnp.zeros((width_x, width_y), F32)] * count

    def pack_sums(sums):
        lane = lax.broadcasted_iota(jnp.int32, (width_x, width_y), 1)
        packed = jnp.zeros((width_x, width_y), F32)
        for i, value in enumerate(sums):
            packed = jnp.where(lane == i, jnp.sum(value, axis=1, keepdims=True), packed)
        return packed

    def unpack_sums(packed, count):
        row = jnp.sum(packed, axis=0, keepdims=True)
        size = (count, width_y)
        mask = lax.broadcasted_iota(jnp.int32, size, 0) == lax.broadcasted_iota(jnp.int32, size, 1)
        return jnp.sum(jnp.where(mask, row, 0.0), axis=1, keepdims=True)

    def step_sums(index, field, pairs, meanwhile):
        count = base + sources * len(pairs)
        part[index, pl.ds(0, 8)] = pack_sums(products(field, pairs, 0, tiles // 2, blank(count)))
        group_send(index, 8)
        meanwhile()
        return unpack_sums(group_sum(index, 8), count)

    def spread(value):
        return jnp.broadcast_to(value, (width_x, width_y))

    span = 6

    def combine(out, terms, rows_of, stack):
        for s in range(sources):
            for k in range(vecs):
                coef[s, k] = spread(rows_of[s][:, k : k + 1])
        wide = [[spread(c[s]) for s in range(sources)] for _, c in terms]

        def body(j, _):
            at = pl.ds(pl.multiple_of(j * (span * width_x), 16), span * width_x)
            pair = pl.ds(j * span, span)
            totals = []
            for s in range(sources):
                value = None
                for (ref, _), w in zip(terms, wide):
                    now = ref[s, pair] * w[s][None]
                    value = now if value is None else value + now
                totals.append(value)
            for k in range(vecs):
                if stack is wide_c:
                    vector = stack[k, pair]
                else:
                    vector = stack[k, at].astype(F32).reshape(span, width_x, width_y)
                for s in range(sources):
                    totals[s] = totals[s] + vector * coef[s, k][None]
            for s in range(sources):
                out[s, pair] = totals[s]
            return 0

        lax.fori_loop(0, tiles // span, body, 0)

    def accumulate(cycle, of_r, of_v):
        wide = [[spread(c[s]) for s in range(sources)] for c in (of_r, of_v)]

        def body(j, _):
            pair = pl.ds(j * 4, 4)
            for s in range(sources):
                value = held[cycle, s, pair] * wide[0][s][None] + krylov[s, pair] * wide[1][s][None]
                if cycle:
                    value = value + sol_ref[s, pair]
                sol_ref[s, pair] = value
            return 0

        lax.fori_loop(0, tiles // 4, body, 0)

    east, west = gx + 1 < n_gx, gx >= 1
    north, south = gy + 1 < n_gy, gy >= 1
    lane2 = lax.broadcasted_iota(jnp.int32, (depth, width_y), 1)
    layer2 = lax.broadcasted_iota(jnp.int32, (depth, width_y), 0)
    layer3 = lax.broadcasted_iota(jnp.int32, shape, 0)
    row3 = lax.broadcasted_iota(jnp.int32, shape, 1)
    lane3 = lax.broadcasted_iota(jnp.int32, shape, 2)
    both = jnp.logical_and
    links = (
        (row_out, 1, row_in, 0, (1, 0), east, west),
        (row_out, 0, row_in, 1, (-1, 0), west, east),
        (col_out, 1, col_in, 0, (0, 1), north, south),
        (col_out, 0, col_in, 1, (0, -1), south, north),
        (col_out, 1, col_in, 2, (-1, 1), both(west, north), both(east, south)),
        (col_out, 0, col_in, 3, (1, -1), both(east, south), both(west, north)),
    )

    def halo_copy(index, number):
        src, which, dst, place, (d_x, d_y), _, _ = links[number]
        return pltpu.make_async_remote_copy(
            src_ref=src.at[index, which],
            dst_ref=dst.at[index, place],
            send_sem=halo_send.at[index, number],
            recv_sem=halo_recv.at[index, number],
            device_id=(gx + d_x, gy + d_y, tx),
            device_id_type=MESH,
        )

    lanes = lax.broadcasted_iota(jnp.int32, (tiles, width_x, width_y), 2)
    places = lax.broadcasted_iota(jnp.int32, (tiles, width_x, width_y), 0)

    def exchange_start(index, field):
        first = jnp.zeros((width_x, width_y), F32)
        last = jnp.zeros((width_x, width_y), F32)
        for s in range(sources):
            value = field[s]
            here = lanes == places + s * tiles
            first = first + jnp.sum(jnp.where(here, value[:, :, 0:1], 0.0), axis=0)
            last = last + jnp.sum(jnp.where(here, value[:, :, width_y - 1 : width_y], 0.0), axis=0)
            row_out[index, 0, pl.ds(s * tiles, tiles)] = value[:, 0, :]
            row_out[index, 1, pl.ds(s * tiles, tiles)] = value[:, width_x - 1, :]
        col_out[index, 0] = first
        col_out[index, 1] = last
        for number in range(len(links)):
            @pl.when(links[number][5])
            def _():
                halo_copy(index, number).start()

    def exchange_wait(index):
        for number in range(len(links)):
            dst, place, got = links[number][2], links[number][3], links[number][6]

            @pl.when(jnp.logical_not(got))
            def _():
                dst[index, place] = jnp.zeros(dst.shape[2:], F32)

            @pl.when(got)
            def _():
                halo_copy(index, number).wait_recv()

    def image_copy(number, piece):
        _, which, _, place, (d_x, d_y), _, _ = links[number]
        if number < 2:
            src, dst, sem = img_row_out.at[which, piece], img_row_in.at[place, piece], number * chunks + piece
        else:
            src, dst, sem = img_col_out.at[which], img_col_in.at[place], 2 * chunks + number - 2
        return pltpu.make_async_remote_copy(
            src_ref=src,
            dst_ref=dst,
            send_sem=img_send.at[sem],
            recv_sem=img_recv.at[sem],
            device_id=(gx + d_x, gy + d_y, tx),
            device_id_type=MESH,
        )

    image_copies = [(number, piece) for number in range(2) for piece in range(chunks)]
    image_copies += [(number, 0) for number in range(2, len(links))]

    def image_start(number, piece):
        @pl.when(links[number][5])
        def _():
            image_copy(number, piece).start()

    def image_pack(piece):
        size = (16, width_x, width_y)
        lane = lax.broadcasted_iota(jnp.int32, size, 2)
        tile = lax.broadcasted_iota(jnp.int32, size, 0) + piece * 16
        here = lane == tile
        for s in range(1, sources):
            here = jnp.logical_or(here, lane == tile + s * tiles)

        def body(k, _):
            value = wide_c[k, pl.ds(piece * 16, 16)]
            for side, (row, col) in enumerate(((0, 0), (width_x - 1, width_y - 1))):
                img_row_out[side, piece, pl.ds(pl.multiple_of(k * 16, 16), 16)] = value[:, row, :]
                column = jnp.sum(jnp.where(here, value[:, :, col : col + 1], 0.0), axis=0)
                if piece:
                    column = column + img_col_out[side, k]
                img_col_out[side, k] = column
            return 0

        lax.fori_loop(0, vecs, body, 0, unroll=4)
        for number in range(2):
            image_start(number, piece)

    def image_wait():
        for number, piece in image_copies:
            place, got = links[number][3], links[number][6]

            @pl.when(jnp.logical_not(got))
            def _():
                if number < 2:
                    img_row_in[place, piece] = jnp.zeros(img_row_in.shape[2:], F32)
                else:
                    img_col_in[place] = jnp.zeros(img_col_in.shape[1:], F32)

            @pl.when(got)
            def _():
                image_copy(number, piece).wait_recv()

    def by_lane(values):
        lane = lax.broadcasted_iota(jnp.int32, (width_x, width_y), 1)
        result = values[0]
        for s in range(1, sources):
            result = jnp.where(lane >= s * tiles, values[s], result)
        return result

    def combine_halo(row, col, terms):
        wide = [[spread(c[s]) for s in range(sources)] for _, _, c in terms]

        def body(i, _):
            place, piece = lax.div(i, chunks), lax.rem(i, chunks)
            totals = []
            for s in range(sources):
                at = pl.ds(pl.multiple_of(s * tiles + piece * 16, 8), 16)
                value = None
                for (ref, _, _), w in zip(terms, wide):
                    now = ref[place, at].reshape(2, width_x, width_y) * w[s][None]
                    value = now if value is None else value + now
                totals.append(value)
            for k in range(vecs):
                vector = img_row_in[place, piece, pl.ds(k * 16, 16)].reshape(2, width_x, width_y)
                for s in range(sources):
                    totals[s] = totals[s] + vector * coef[s, k][None]
            for s in range(sources):
                at = pl.ds(pl.multiple_of(s * tiles + piece * 16, 8), 16)
                row[place, at] = totals[s].reshape(16, width_y)
            return 0

        lax.fori_loop(0, 2 * chunks, body, 0)
        values = [None] * 4
        for (_, ref, _), w in zip(terms, wide):
            scale = by_lane(w)
            for place in range(4):
                now = ref[place] * scale
                values[place] = now if values[place] is None else values[place] + now
        for k in range(vecs):
            scale = by_lane([coef[s, k] for s in range(sources)])
            for place in range(4):
                values[place] = values[place] + img_col_in[place, k] * scale
        for place in range(4):
            col[place] = values[place]

    def apply(field, row_halo, col_halo, out):
        def columns(place, at):
            packed = col_halo[place][None]
            return jnp.sum(jnp.where(lane3 == layer3 + at, packed, 0.0), axis=2, keepdims=True)

        def corner(place, row, at):
            packed = col_halo[place, row : row + 1]
            return jnp.sum(jnp.where(lane2 == layer2 + at, packed, 0.0), axis=1, keepdims=True)

        def plus_y(f, edge):
            return jnp.where(lane3 == width_y - 1, edge, pltpu.roll(f, width_y - 1, 2))

        def minus_y(f, edge):
            return jnp.where(lane3 == 0, edge, pltpu.roll(f, 1, 2))

        def plus_x(f, row):
            return jnp.where(row3 == width_x - 1, row[:, None, :], pltpu.roll(f, width_x - 1, 1))

        def minus_x(f, row):
            return jnp.where(row3 == 0, row[:, None, :], pltpu.roll(f, 1, 1))

        zero = jnp.zeros((1, width_x, width_y), F32)

        def plus_z(f):
            return jnp.concatenate([f[1:], zero], axis=0)

        def minus_z(f):
            return jnp.concatenate([zero, f[:-1]], axis=0)

        for s in range(sources):
            for p in range(2):
                def comp(c):
                    return field[s, pl.ds(p * half + c * depth, depth)]

                def at(c):
                    return s * tiles + p * half + c * depth

                def row(place, c):
                    return row_halo[place, pl.ds(at(c), depth)]

                e_x, e_y, e_z = comp(0), comp(1), comp(2)
                xp_y = plus_y(e_x, columns(1, at(0)))
                xm_y = minus_y(e_x, columns(0, at(0)))
                t = xp_y - e_x
                hx = row(0, 0)
                hx_up = jnp.where(lane2 == width_y - 1, corner(3, width_x - 1, at(0)), pltpu.roll(hx, width_y - 1, 1))
                dt = t - minus_x(t, hx_up - hx)
                c = e_x - minus_x(e_x, hx)
                a = e_y - minus_y(e_y, columns(0, at(1)))
                hy = row(1, 1)
                hy_down = jnp.where(lane2 == 0, corner(2, 0, at(1)), pltpu.roll(hy, 1, 1))
                da = plus_x(a, hy - hy_down) - a
                y2 = plus_x(e_y, hy) + minus_x(e_y, row(0, 1)) - 2.0 * e_y
                zp_x = plus_x(e_z, row(1, 2))
                zp_y = plus_y(e_z, columns(1, at(2)))
                z2 = zp_x + minus_x(e_z, row(0, 2)) + zp_y + minus_y(e_z, columns(0, at(2))) - 4.0 * e_z
                fx_z = zp_x - e_z
                fy_z = zp_y - e_z
                k_x = da - (xp_y + xm_y + plus_z(e_x) + minus_z(e_x) - 4.0 * e_x) + (fx_z - minus_z(fx_z))
                k_y = (fy_z - minus_z(fy_z)) - (plus_z(e_y) + minus_z(e_y) - 2.0 * e_y) - y2 + dt
                ca = c + a
                k_z = (plus_z(ca) - ca) - z2
                for number, value in enumerate((k_x, k_y, k_z)):
                    cross = induct[number] * field[s, pl.ds((1 - p) * half + number * depth, depth)]
                    value = value - cross if p == 0 else value + cross
                    out[s, pl.ds(p * half + number * depth, depth)] = value

    exchange_start(0, res_ref)
    total[...] = jnp.zeros_like(total)

    def gram_body(j, _):
        block = full_c[:, pl.ds(pl.multiple_of(j * 16, 16), 16), :].reshape(vecs * 16, width_y)
        total[...] += lax.dot_general(block, block, (((1,), (1,)), ((), ())), preferred_element_type=F32)
        return 0

    wide = vecs * 16
    halves = wide // width_y
    start = blank(base)
    own[0].wait()
    for piece in range(chunks):
        if piece + 1 == chunks:
            for way in range(2):
                gather_start(1, way, 0, jnp.logical_not(forwards(way, 1)))
        for step in range(1, n_tx - 1):
            gather_forward(0, step, piece)
        if piece + 2 < chunks:
            for way in range(2):
                gather_start(0, way, piece + 2, True)
        if piece + 1 == chunks:
            for way in range(2):
                gather_start(1, way, 0, forwards(way, 1))
        gather_rest(0, piece)
        widen(piece)
        lax.fori_loop(piece * (chunk // 16), (piece + 1) * (chunk // 16), gram_body, 0)
        start = products(res_ref, [], piece * 8, 8, start)
        if piece + 1 < chunks:
            image_pack(piece)
    same = lax.rem(lax.broadcasted_iota(jnp.int32, (wide, wide), 0), 16) == lax.rem(
        lax.broadcasted_iota(jnp.int32, (wide, wide), 1), 16
    )
    folded = jnp.sum(jnp.where(same, total[...], 0.0).reshape(vecs, 16, wide), axis=1)
    gram = jnp.zeros((vecs, width_y), F32)
    lane = lax.broadcasted_iota(jnp.int32, (width_y, width_y), 0)
    column = lax.broadcasted_iota(jnp.int32, (width_y, width_y), 1)
    for h in range(halves):
        pick = (lax.div(lane, 16) + h * (width_y // 16) == column).astype(F32)
        gram = gram + jnp.dot(
            folded[:, h * width_y : (h + 1) * width_y], pick,
            precision=lax.Precision.HIGHEST, preferred_element_type=F32,
        )
    part[0, pl.ds(0, vecs)] = gram
    part[0, pl.ds(vecs, 8)] = pack_sums(start)
    group_send(0, vecs + 8)
    image_pack(chunks - 1)
    for number in range(2, len(links)):
        image_start(number, 0)
    first_sum = group_sum(0, vecs + 8)
    gram = first_sum[:vecs, :vecs]
    start = unpack_sums(first_sum[vecs:], base)
    row_id = lax.broadcasted_iota(jnp.int32, (vecs, vecs), 0)
    eye = (row_id == lax.broadcasted_iota(jnp.int32, (vecs, vecs), 1)).astype(F32)
    wide_row = lax.broadcasted_iota(jnp.int32, (vecs, 2 * vecs), 0)
    system = jnp.concatenate([gram, eye], axis=1)
    for k in range(0, vecs, 2):
        col_0 = jnp.broadcast_to(system[:, k : k + 1], (vecs, 2 * vecs))
        col_1 = jnp.broadcast_to(system[:, k + 1 : k + 2], (vecs, 2 * vecs))
        top, low = system[k : k + 1], system[k + 1 : k + 2]
        p_00, p_01 = col_0[k : k + 1], col_1[k : k + 1]
        p_10, p_11 = col_0[k + 1 : k + 2], col_1[k + 1 : k + 2]
        scale = 1.0 / (p_00 * p_11 - p_01 * p_10)
        new_0 = (p_11 * top - p_01 * low) * scale
        new_1 = (p_00 * low - p_10 * top) * scale
        system = system - col_0 * new_0 - col_1 * new_1
        system = jnp.where(wide_row == k, new_0, jnp.where(wide_row == k + 1, new_1, system))
    inverse[...] = system[:, vecs:]

    def solve(column):
        answer = jnp.sum(inverse[...] * column, axis=0, keepdims=True)
        flat = jnp.sum(eye * column, axis=0, keepdims=True)
        return answer, jnp.sum(answer * flat, axis=1, keepdims=True)

    weights = [solve(start[s * vecs : (s + 1) * vecs])[0] for s in range(sources)]
    one = jnp.ones((1, 1), F32)
    combine(held.at[0], [(res_ref, [one] * sources)], [-w for w in weights], wide_c)
    exchange_wait(0)
    image_wait()
    combine_halo(row_r, col_r, [(row_in.at[0], col_in.at[0], [one] * sources)])

    every = range(sources)
    for cycle in range(CYCLES):
        index = 2 * cycle
        resid = held.at[cycle]
        apply(resid, row_r, col_r, work)

        def meanwhile():
            exchange_start(index + 1, work)
            if index + 1 < n_tx - 1:
                gather_forward(1, index + 1, 0)
            if cycle:
                accumulate(cycle - 1, *update)

        sums = step_sums(index + 1, work, [(resid, resid), (resid, work), (work, work)], meanwhile)
        state = []
        for s in every:
            def got(i):
                return sums[base + 3 * s + i : base + 3 * s + i + 1]

            beta = jnp.sqrt(got(0) + EPS)
            scale = 1.0 / beta
            raw, quad = solve(sums[s * vecs : (s + 1) * vecs])
            g_0 = raw * scale
            n_00 = got(0) * scale * scale
            h_00 = got(1) * scale * scale
            left = (got(2) - quad) * scale * scale - 2.0 * h_00 * h_00 + h_00 * h_00 * n_00
            left = jnp.maximum(left, 0.0)
            h_10 = jnp.sqrt(left + EPS)
            state.append((beta, scale, g_0, n_00, h_00, left, h_10))
        of_w = [v[1] / v[6] for v in state]
        of_r = [-v[4] * v[1] / v[6] for v in state]
        combine(krylov, [(work, of_w), (resid, of_r)], [-v[2] / v[6] for v in state], wide_c)
        exchange_wait(index + 1)
        now = (row_in.at[index + 1], col_in.at[index + 1])
        combine_halo(row_v, col_v, [now + (of_w,), (row_r, col_r, of_r)])
        apply(krylov, row_v, col_v, work)

        def meanwhile():
            if cycle + 1 < CYCLES:
                exchange_start(index + 2, work)
            if index + 2 < n_tx - 1:
                gather_forward(1, index + 2, 0)

        pairs = [(resid, work), (krylov, work), (work, work), (krylov, krylov)]
        sums = step_sums(index + 2, work, pairs, meanwhile)
        in_r, in_v, in_w, in_g, out_r, out_v = [], [], [], [], [], []
        for s in every:
            def got(i):
                return sums[base + 4 * s + i : base + 4 * s + i + 1]

            beta, scale, g_0, n_00, h_00, _, h_10 = state[s]
            g_1, quad = solve(sums[s * vecs : (s + 1) * vecs])
            h_01 = got(0) * scale
            h_11 = got(1)
            n_11 = got(3)
            n_01 = h_00 * (1.0 - n_00) / h_10
            left = (
                got(2) - quad - 2.0 * (h_01 * h_01 + h_11 * h_11)
                + h_01 * h_01 * n_00 + h_11 * h_11 * n_11 + 2.0 * h_01 * h_11 * n_01
            )
            h_21 = jnp.sqrt(jnp.maximum(left, 0.0) + EPS)
            a_00 = h_00 * h_00 + h_10 * h_10
            a_01 = h_00 * h_01 + h_10 * h_11
            a_11 = h_01 * h_01 + h_11 * h_11 + h_21 * h_21
            l_00 = jnp.sqrt(a_00)
            l_10 = a_01 / l_00
            l_11 = jnp.sqrt(a_11 - l_10 * l_10)
            f_0 = beta * h_00 / l_00
            f_1 = (beta * h_01 - l_10 * f_0) / l_11
            y_1 = f_1 / l_11
            y_0 = (f_0 - l_10 * y_1) / l_00
            t_0 = beta - h_00 * y_0 - h_01 * y_1
            t_1 = -(h_10 * y_0 + h_11 * y_1)
            t_2 = -h_21 * y_1
            share = t_2 / h_21
            in_r.append((t_0 - share * h_01) * scale)
            in_v.append(t_1 - share * h_11)
            in_w.append(share)
            in_g.append(-share * g_1)
            out_r.append(y_0 * scale)
            out_v.append(y_1)
            weights[s] = weights[s] - (g_0 * y_0 + g_1 * y_1)
        update = (out_r, out_v)
        target = held.at[cycle + 1] if cycle + 1 < CYCLES else res_ref
        combine(target, [(resid, in_r), (krylov, in_v), (work, in_w)], in_g, wide_c)
        if cycle + 1 < CYCLES:
            exchange_wait(index + 2)
            now = (row_in.at[index + 2], col_in.at[index + 2])
            combine_halo(row_r, col_r, [(row_r, col_r, in_r), (row_v, col_v, in_v), now + (in_w,)])

    for step in range(2 * CYCLES + 1, n_tx - 1):
        gather_forward(1, step, 0)
    gather_rest(1, 0)
    own[1].wait()
    terms = [(held.at[CYCLES - 1], update[0]), (krylov, update[1])]
    if CYCLES > 1:
        terms.append((sol_ref, [one] * sources))
    combine(sol_ref, terms, weights, full_u)
    gather_sent(0)
    gather_sent(1)
    for index in range(2 * CYCLES):
        for number in range(len(links)):
            @pl.when(links[number][5])
            def _():
                halo_copy(index, number).wait_send()
    for number, piece in image_copies:
        @pl.when(links[number][5])
        def _():
            image_copy(number, piece).wait_send()


def on_device(dims, src_cell, basis, images, induction):
    n_gx, n_gy, n_tx = dims
    per_dev, _, _, depth, width_x, width_y = basis.shape
    sources = src_cell.shape[0]
    tiles = 6 * depth
    rows = tiles * width_x
    vecs = per_dev * n_tx
    group = n_gx * n_gy
    field = (sources, tiles, width_x, width_y)
    ind_rows = 3 * induction.shape[1] * width_x
    most = vecs + 8
    sums, halos = 2 * CYCLES + 1, 2 * CYCLES
    dma = pltpu.SemaphoreType.DMA
    vmem = pl.BlockSpec(memory_space=pltpu.VMEM)
    hbm = pl.BlockSpec(memory_space=pl.ANY)
    chunks = tiles // 16
    out = pl.pallas_call(
        functools.partial(kernel, dims),
        out_shape=(jax.ShapeDtypeStruct(field, F32),) * 2,
        in_specs=[pl.BlockSpec(memory_space=pltpu.SMEM), hbm, hbm, hbm],
        out_specs=(vmem, vmem),
        scratch_shapes=[
            pltpu.VMEM((vecs, rows, width_y), jnp.bfloat16),
            pltpu.VMEM((vecs, rows, width_y), jnp.bfloat16),
            pltpu.VMEM((n_tx, ind_rows, width_y), jnp.bfloat16),
            pltpu.VMEM((3, depth, width_x, width_y), F32),
            pltpu.VMEM(field, F32),
            pltpu.VMEM(field, F32),
            pltpu.VMEM((vecs * 16, vecs * 16), F32),
            pltpu.VMEM((vecs, vecs), F32),
            pltpu.VMEM((sources, vecs, width_x, width_y), F32),
            pltpu.VMEM((CYCLES,) + field, F32),
            pltpu.VMEM((vecs, tiles, width_x, width_y), F32),
            pltpu.VMEM((sums, most, width_y), F32),
            pltpu.VMEM((sums, group, most, width_y), F32),
            pltpu.VMEM((halos, 2, sources * tiles, width_y), F32),
            pltpu.VMEM((halos, 2, sources * tiles, width_y), F32),
            pltpu.VMEM((halos, 2, width_x, width_y), F32),
            pltpu.VMEM((halos, 4, width_x, width_y), F32),
            pltpu.VMEM((2, chunks, vecs * 16, width_y), F32),
            pltpu.VMEM((2, chunks, vecs * 16, width_y), F32),
            pltpu.VMEM((2, vecs, width_x, width_y), F32),
            pltpu.VMEM((4, vecs, width_x, width_y), F32),
            pltpu.VMEM((2, sources * tiles, width_y), F32),
            pltpu.VMEM((2, sources * tiles, width_y), F32),
            pltpu.VMEM((4, width_x, width_y), F32),
            pltpu.VMEM((4, width_x, width_y), F32),
            dma((3,)),
            dma((2, 2, n_tx - 1, chunks)),
            dma((2, 2, n_tx - 1, chunks)),
            dma((n_tx - 1,)),
            dma((n_tx - 1,)),
            dma((sums, group - 1)),
            dma((sums, group - 1)),
            dma((halos, 6)),
            dma((halos, 6)),
            dma((2 * chunks + 4,)),
            dma((2 * chunks + 4,)),
        ],
        compiler_params=pltpu.CompilerParams(
            collective_id=0, has_side_effects=True, vmem_limit_bytes=60 * 1024 * 1024
        ),
        cost_estimate=pl.CostEstimate(flops=400_000_000, bytes_accessed=2_000_000, transcendentals=20_000),
    )(
        src_cell,
        basis.reshape(per_dev, rows, width_y),
        images.reshape(per_dev, rows, width_y),
        induction.reshape(ind_rows, width_y),
    )
    shape = (sources, 2, 3, depth, width_x, width_y)
    return tuple(o.reshape(shape) for o in out)


def solution(mesh):
    dims = (mesh.shape["gx"], mesh.shape["gy"], mesh.shape["tx"])
    spec = P("tx", None, None, None, "gx", "gy")
    return jax.shard_map(
        functools.partial(on_device, dims),
        mesh=mesh,
        in_specs=(P("tx"), spec, spec, P(None, "tx", "gx", "gy")),
        out_specs=(spec, spec),
        check_vma=False,
    )
```

```python
import functools

import jax
import jax.numpy as jnp
from jax import lax
from jax.experimental import pallas as pl
from jax.experimental.pallas import tpu as pltpu
from jax.sharding import PartitionSpec as P

CYCLES = 2
ARNOLDI = 2
EPS = 1e-06
MESH = pl.DeviceIdType.MESH
F32 = jnp.float32


def kernel(
    dims, pos_ref, u_ref, c_ref, m_ref, sol_ref, res_ref,
    full_c, full_u, ind_all, induct, krylov, work, total, inverse, coef, held, wide_c,
    part, parts, row_out, row_in, col_out, col_in,
    img_row_out, img_row_in, img_col_out, img_col_in, row_r, row_v, col_r, col_v,
    own_sem, gather_send, gather_recv, ind_send, ind_recv, sum_send, sum_recv, halo_send, halo_recv,
    img_send, img_recv,
):
    n_gx, n_gy, n_tx = dims
    gx, gy, tx = lax.axis_index("gx"), lax.axis_index("gy"), lax.axis_index("tx")
    group = n_gx * n_gy
    rank = gx * n_gy + gy
    sources = pos_ref.shape[0]
    per_dev = c_ref.shape[0]
    rows = c_ref.shape[1]
    width_y = c_ref.shape[2]
    width_x = 8
    depth = induct.shape[1]
    tiles = rows // width_x
    vecs = full_c.shape[0]
    half = tiles // 2
    chunk = 16 * width_x
    chunks = rows // chunk

    def peer_of(offset):
        other = lax.rem(rank + offset, group)
        return (lax.div(other, n_gy), lax.rem(other, n_gy), tx)

    def along(offset):
        return (gx, gy, lax.rem(tx + offset, n_tx))

    barrier = pltpu.get_barrier_semaphore()
    for offset in range(1, group):
        pl.semaphore_signal(barrier, inc=1, device_id=peer_of(offset), device_id_type=MESH)
    for offset in range(1, n_tx):
        pl.semaphore_signal(barrier, inc=1, device_id=along(offset), device_id_type=MESH)
    pl.semaphore_wait(barrier, group - 1 + n_tx - 1)

    def slot(shard):
        return pl.ds(shard * per_dev, per_dev)

    def rows_at(which, piece):
        return pl.ds(piece * chunk, chunk)

    pieces = (chunks, chunks)

    def hop(which, way, step, piece):
        full = (full_c, full_u)[which]
        at = rows_at(which, piece)
        sign = 1 if way == 0 else -1
        shard = tx - sign * (step - 1)
        source = (c_ref, u_ref)[which].at[:, at] if step == 1 else full.at[slot(shard), at]
        return pltpu.make_async_remote_copy(
            src_ref=source,
            dst_ref=full.at[slot(shard), at],
            send_sem=gather_send.at[which, way, step - 1, piece],
            recv_sem=gather_recv.at[which, way, step - 1, piece],
            device_id=(gx, gy, tx + sign),
            device_id_type=MESH,
        )

    def sends(way, step):
        if way == 0:
            return jnp.logical_and(tx + 1 < n_tx, tx - step + 1 >= 0)
        return jnp.logical_and(tx - 1 >= 0, tx + step - 1 < n_tx)

    def receives(way, step):
        return tx - step >= 0 if way == 0 else tx + step < n_tx

    def forwards(way, step):
        return sends(way, step + 1)

    def gather_start(which, way, piece, when):
        @pl.when(jnp.logical_and(sends(way, 1), when))
        def _():
            hop(which, way, 1, piece).start()

    def gather_arrive(which, way, step, piece, when):
        @pl.when(jnp.logical_and(receives(way, step), when))
        def _():
            full = (full_c, full_u)[which]
            at = rows_at(which, piece)
            shard = tx - step if way == 0 else tx + step
            pltpu.make_async_remote_copy(
                src_ref=full.at[slot(shard), at],
                dst_ref=full.at[slot(shard), at],
                send_sem=gather_send.at[which, way, step - 1, piece],
                recv_sem=gather_recv.at[which, way, step - 1, piece],
                device_id=along(1),
                device_id_type=MESH,
            ).wait_recv()

    def gather_forward(which, step, piece):
        for way in range(2):
            gather_arrive(which, way, step, piece, forwards(way, step))

            @pl.when(forwards(way, step))
            def _():
                hop(which, way, step + 1, piece).start()

    def gather_rest(which, piece):
        for step in range(1, n_tx):
            for way in range(2):
                gather_arrive(which, way, step, piece, jnp.logical_not(forwards(way, step)))

    def gather_sent(which):
        for piece in range(pieces[which]):
            for step in range(1, n_tx):
                for way in range(2):
                    @pl.when(sends(way, step))
                    def _():
                        hop(which, way, step, piece).wait_send()

    own = [
        pltpu.make_async_copy(ref, full.at[slot(tx)], own_sem.at[number])
        for number, (ref, full) in enumerate(((c_ref, full_c), (u_ref, full_u)))
    ]
    own.append(pltpu.make_async_copy(m_ref, ind_all.at[tx], own_sem.at[2]))

    def ind_copy(offset):
        return pltpu.make_async_remote_copy(
            src_ref=m_ref,
            dst_ref=ind_all.at[tx],
            send_sem=ind_send.at[offset - 1],
            recv_sem=ind_recv.at[offset - 1],
            device_id=along(offset),
            device_id_type=MESH,
        )

    for offset in range(1, n_tx):
        ind_copy(offset).start()
    for piece in range(min(2, chunks)):
        for way in range(2):
            gather_start(0, way, piece, True)
    for copy in own:
        copy.start()
    own[2].wait()
    for offset in range(1, n_tx):
        ind_copy(offset).wait()
    layers = depth // n_tx
    for owner in range(n_tx):
        piece = ind_all[owner].astype(F32).reshape(3, layers, width_x, width_y)
        for layer in range(layers):
            induct[:, owner * layers + layer] = piece[:, layer]

    size_x, size_y = width_x * n_gx, width_y * n_gy
    shape = (depth, width_x, width_y)
    z_pos = lax.broadcasted_iota(jnp.int32, shape, 0).astype(F32)
    x_pos = (gx * width_x + lax.broadcasted_iota(jnp.int32, shape, 1)).astype(F32)
    y_pos = (gy * width_y + lax.broadcasted_iota(jnp.int32, shape, 2)).astype(F32)
    for s in range(sources):
        cell = pos_ref[s]
        rest = lax.rem(cell, size_x * size_y)
        d_z = z_pos - lax.div(cell, size_x * size_y).astype(F32)
        d_x = x_pos - lax.div(rest, size_y).astype(F32)
        d_y = y_pos - lax.rem(rest, size_y).astype(F32)
        dist = jnp.sqrt(d_z * d_z + d_x * d_x + d_y * d_y)
        primary = jnp.exp(-dist / ((size_x + size_y) / 8.0))
        for comp, weight in enumerate((1.0, 0.5, 0.25)):
            real = (induct[comp] - 1.0) * weight * primary
            res_ref[s, pl.ds(comp * depth, depth)] = real
            res_ref[s, pl.ds(half + comp * depth, depth)] = 0.5 * real

    base = sources * vecs

    def sum_copy(index, count, offset):
        return pltpu.make_async_remote_copy(
            src_ref=part.at[index, pl.ds(0, count)],
            dst_ref=parts.at[index, rank, pl.ds(0, count)],
            send_sem=sum_send.at[index, offset - 1],
            recv_sem=sum_recv.at[index, offset - 1],
            device_id=peer_of(offset),
            device_id_type=MESH,
        )

    def group_send(index, count):
        for offset in range(1, group):
            sum_copy(index, count, offset).start()
        parts[index, pl.ds(rank, 1), pl.ds(0, count)] = part[index, pl.ds(0, count)][None]

    def group_sum(index, count):
        for offset in range(1, group):
            sum_copy(index, count, offset).wait()
        return jnp.sum(parts[index, :, pl.ds(0, count)], axis=0)

    def widen(piece):
        def body(k, _):
            vector = full_c[k, pl.ds(piece * chunk, chunk)].astype(F32)
            wide_c[k, pl.ds(piece * 16, 16)] = vector.reshape(16, width_x, width_y)
            return 0

        lax.fori_loop(0, vecs, body, 0, unroll=2)

    def products(field, pairs, first, count, sums):
        def body(j, sums):
            sums = list(sums)
            pair = pl.ds(j * 2, 2)
            values = [field[s, pair] for s in range(sources)]
            for k in range(vecs):
                vector = wide_c[k, pair]
                for s in range(sources):
                    sums[s * vecs + k] += jnp.sum(vector * values[s], axis=0)
            for i, (left, right) in enumerate(pairs):
                for s in range(sources):
                    sums[base + s * len(pairs) + i] += jnp.sum(left[s, pair] * right[s, pair], axis=0)
            return tuple(sums)

        return lax.fori_loop(first, first + count, body, tuple(sums), unroll=2)

    def blank(count):
        return [jnp.zeros((width_x, width_y), F32)] * count

    def pack_sums(sums):
        lane = lax.broadcasted_iota(jnp.int32, (width_x, width_y), 1)
        packed = jnp.zeros((width_x, width_y), F32)
        for i, value in enumerate(sums):
            packed = jnp.where(lane == i, jnp.sum(value, axis=1, keepdims=True), packed)
        return packed

    def unpack_sums(packed, count):
        row = jnp.sum(packed, axis=0, keepdims=True)
        size = (count, width_y)
        mask = lax.broadcasted_iota(jnp.int32, size, 0) == lax.broadcasted_iota(jnp.int32, size, 1)
        return jnp.sum(jnp.where(mask, row, 0.0), axis=1, keepdims=True)

    def step_sums(index, field, pairs, meanwhile):
        count = base + sources * len(pairs)
        part[index, pl.ds(0, 8)] = pack_sums(products(field, pairs, 0, tiles // 2, blank(count)))
        group_send(index, 8)
        meanwhile()
        return unpack_sums(group_sum(index, 8), count)

    def spread(value):
        return jnp.broadcast_to(value, (width_x, width_y))

    span = 6

    def combine(out, terms, rows_of, stack):
        for s in range(sources):
            for k in range(vecs):
                coef[s, k] = spread(rows_of[s][:, k : k + 1])
        wide = [[spread(c[s]) for s in range(sources)] for _, c in terms]

        def body(j, _):
            at = pl.ds(pl.multiple_of(j * (span * width_x), 16), span * width_x)
            pair = pl.ds(j * span, span)
            totals = []
            for s in range(sources):
                value = None
                for (ref, _), w in zip(terms, wide):
                    now = ref[s, pair] * w[s][None]
                    value = now if value is None else value + now
                totals.append(value)
            for k in range(vecs):
                if stack is wide_c:
                    vector = stack[k, pair]
                else:
                    vector = stack[k, at].astype(F32).reshape(span, width_x, width_y)
                for s in range(sources):
                    totals[s] = totals[s] + vector * coef[s, k][None]
            for s in range(sources):
                out[s, pair] = totals[s]
            return 0

        lax.fori_loop(0, tiles // span, body, 0)

    def accumulate(cycle, of_r, of_v):
        wide = [[spread(c[s]) for s in range(sources)] for c in (of_r, of_v)]

        def body(j, _):
            pair = pl.ds(j * 4, 4)
            for s in range(sources):
                value = held[cycle, s, pair] * wide[0][s][None] + krylov[s, pair] * wide[1][s][None]
                if cycle:
                    value = value + sol_ref[s, pair]
                sol_ref[s, pair] = value
            return 0

        lax.fori_loop(0, tiles // 4, body, 0)

    east, west = gx + 1 < n_gx, gx >= 1
    north, south = gy + 1 < n_gy, gy >= 1
    lane2 = lax.broadcasted_iota(jnp.int32, (depth, width_y), 1)
    layer2 = lax.broadcasted_iota(jnp.int32, (depth, width_y), 0)
    layer3 = lax.broadcasted_iota(jnp.int32, shape, 0)
    row3 = lax.broadcasted_iota(jnp.int32, shape, 1)
    lane3 = lax.broadcasted_iota(jnp.int32, shape, 2)
    both = jnp.logical_and
    links = (
        (row_out, 1, row_in, 0, (1, 0), east, west),
        (row_out, 0, row_in, 1, (-1, 0), west, east),
        (col_out, 1, col_in, 0, (0, 1), north, south),
        (col_out, 0, col_in, 1, (0, -1), south, north),
        (col_out, 1, col_in, 2, (-1, 1), both(west, north), both(east, south)),
        (col_out, 0, col_in, 3, (1, -1), both(east, south), both(west, north)),
    )

    def halo_copy(index, number):
        src, which, dst, place, (d_x, d_y), _, _ = links[number]
        return pltpu.make_async_remote_copy(
            src_ref=src.at[index, which],
            dst_ref=dst.at[index, place],
            send_sem=halo_send.at[index, number],
            recv_sem=halo_recv.at[index, number],
            device_id=(gx + d_x, gy + d_y, tx),
            device_id_type=MESH,
        )

    lanes = lax.broadcasted_iota(jnp.int32, (tiles, width_x, width_y), 2)
    places = lax.broadcasted_iota(jnp.int32, (tiles, width_x, width_y), 0)

    def exchange_start(index, field):
        first = jnp.zeros((width_x, width_y), F32)
        last = jnp.zeros((width_x, width_y), F32)
        for s in range(sources):
            value = field[s]
            here = lanes == places + s * tiles
            first = first + jnp.sum(jnp.where(here, value[:, :, 0:1], 0.0), axis=0)
            last = last + jnp.sum(jnp.where(here, value[:, :, width_y - 1 : width_y], 0.0), axis=0)
            row_out[index, 0, pl.ds(s * tiles, tiles)] = value[:, 0, :]
            row_out[index, 1, pl.ds(s * tiles, tiles)] = value[:, width_x - 1, :]
        col_out[index, 0] = first
        col_out[index, 1] = last
        for number in range(len(links)):
            @pl.when(links[number][5])
            def _():
                halo_copy(index, number).start()

    def exchange_wait(index):
        for number in range(len(links)):
            dst, place, got = links[number][2], links[number][3], links[number][6]

            @pl.when(jnp.logical_not(got))
            def _():
                dst[index, place] = jnp.zeros(dst.shape[2:], F32)

            @pl.when(got)
            def _():
                halo_copy(index, number).wait_recv()

    def image_copy(number, piece):
        _, which, _, place, (d_x, d_y), _, _ = links[number]
        if number < 2:
            src, dst, sem = img_row_out.at[which, piece], img_row_in.at[place, piece], number * chunks + piece
        else:
            src, dst, sem = img_col_out.at[which], img_col_in.at[place], 2 * chunks + number - 2
        return pltpu.make_async_remote_copy(
            src_ref=src,
            dst_ref=dst,
            send_sem=img_send.at[sem],
            recv_sem=img_recv.at[sem],
            device_id=(gx + d_x, gy + d_y, tx),
            device_id_type=MESH,
        )

    image_copies = [(number, piece) for number in range(2) for piece in range(chunks)]
    image_copies += [(number, 0) for number in range(2, len(links))]

    def image_start(number, piece):
        @pl.when(links[number][5])
        def _():
            image_copy(number, piece).start()

    def image_pack(piece):
        size = (16, width_x, width_y)
        lane = lax.broadcasted_iota(jnp.int32, size, 2)
        tile = lax.broadcasted_iota(jnp.int32, size, 0) + piece * 16
        here = lane == tile
        for s in range(1, sources):
            here = jnp.logical_or(here, lane == tile + s * tiles)

        def body(k, _):
            value = wide_c[k, pl.ds(piece * 16, 16)]
            for side, (row, col) in enumerate(((0, 0), (width_x - 1, width_y - 1))):
                img_row_out[side, piece, pl.ds(pl.multiple_of(k * 16, 16), 16)] = value[:, row, :]
                column = jnp.sum(jnp.where(here, value[:, :, col : col + 1], 0.0), axis=0)
                if piece:
                    column = column + img_col_out[side, k]
                img_col_out[side, k] = column
            return 0

        lax.fori_loop(0, vecs, body, 0, unroll=4)
        for number in range(2):
            image_start(number, piece)

    def image_wait():
        for number, piece in image_copies:
            place, got = links[number][3], links[number][6]

            @pl.when(jnp.logical_not(got))
            def _():
                if number < 2:
                    img_row_in[place, piece] = jnp.zeros(img_row_in.shape[2:], F32)
                else:
                    img_col_in[place] = jnp.zeros(img_col_in.shape[1:], F32)

            @pl.when(got)
            def _():
                image_copy(number, piece).wait_recv()

    def by_lane(values):
        lane = lax.broadcasted_iota(jnp.int32, (width_x, width_y), 1)
        result = values[0]
        for s in range(1, sources):
            result = jnp.where(lane >= s * tiles, values[s], result)
        return result

    def combine_halo(row, col, terms):
        wide = [[spread(c[s]) for s in range(sources)] for _, _, c in terms]

        def body(i, _):
            place, piece = lax.div(i, chunks), lax.rem(i, chunks)
            totals = []
            for s in range(sources):
                at = pl.ds(pl.multiple_of(s * tiles + piece * 16, 8), 16)
                value = None
                for (ref, _, _), w in zip(terms, wide):
                    now = ref[place, at].reshape(2, width_x, width_y) * w[s][None]
                    value = now if value is None else value + now
                totals.append(value)
            for k in range(vecs):
                vector = img_row_in[place, piece, pl.ds(k * 16, 16)].reshape(2, width_x, width_y)
                for s in range(sources):
                    totals[s] = totals[s] + vector * coef[s, k][None]
            for s in range(sources):
                at = pl.ds(pl.multiple_of(s * tiles + piece * 16, 8), 16)
                row[place, at] = totals[s].reshape(16, width_y)
            return 0

        lax.fori_loop(0, 2 * chunks, body, 0)
        values = [None] * 4
        for (_, ref, _), w in zip(terms, wide):
            scale = by_lane(w)
            for place in range(4):
                now = ref[place] * scale
                values[place] = now if values[place] is None else values[place] + now
        for k in range(vecs):
            scale = by_lane([coef[s, k] for s in range(sources)])
            for place in range(4):
                values[place] = values[place] + img_col_in[place, k] * scale
        for place in range(4):
            col[place] = values[place]

    def apply(field, row_halo, col_halo, out):
        def columns(place, at):
            packed = col_halo[place][None]
            return jnp.sum(jnp.where(lane3 == layer3 + at, packed, 0.0), axis=2, keepdims=True)

        def corner(place, row, at):
            packed = col_halo[place, row : row + 1]
            return jnp.sum(jnp.where(lane2 == layer2 + at, packed, 0.0), axis=1, keepdims=True)

        def plus_y(f, edge):
            return jnp.where(lane3 == width_y - 1, edge, pltpu.roll(f, width_y - 1, 2))

        def minus_y(f, edge):
            return jnp.where(lane3 == 0, edge, pltpu.roll(f, 1, 2))

        def plus_x(f, row):
            return jnp.where(row3 == width_x - 1, row[:, None, :], pltpu.roll(f, width_x - 1, 1))

        def minus_x(f, row):
            return jnp.where(row3 == 0, row[:, None, :], pltpu.roll(f, 1, 1))

        zero = jnp.zeros((1, width_x, width_y), F32)

        def plus_z(f):
            return jnp.concatenate([f[1:], zero], axis=0)

        def minus_z(f):
            return jnp.concatenate([zero, f[:-1]], axis=0)

        for s in range(sources):
            for p in range(2):
                def comp(c):
                    return field[s, pl.ds(p * half + c * depth, depth)]

                def at(c):
                    return s * tiles + p * half + c * depth

                def row(place, c):
                    return row_halo[place, pl.ds(at(c), depth)]

                e_x, e_y, e_z = comp(0), comp(1), comp(2)
                xp_y = plus_y(e_x, columns(1, at(0)))
                xm_y = minus_y(e_x, columns(0, at(0)))
                t = xp_y - e_x
                hx = row(0, 0)
                hx_up = jnp.where(lane2 == width_y - 1, corner(3, width_x - 1, at(0)), pltpu.roll(hx, width_y - 1, 1))
                dt = t - minus_x(t, hx_up - hx)
                c = e_x - minus_x(e_x, hx)
                a = e_y - minus_y(e_y, columns(0, at(1)))
                hy = row(1, 1)
                hy_down = jnp.where(lane2 == 0, corner(2, 0, at(1)), pltpu.roll(hy, 1, 1))
                da = plus_x(a, hy - hy_down) - a
                y2 = plus_x(e_y, hy) + minus_x(e_y, row(0, 1)) - 2.0 * e_y
                zp_x = plus_x(e_z, row(1, 2))
                zp_y = plus_y(e_z, columns(1, at(2)))
                z2 = zp_x + minus_x(e_z, row(0, 2)) + zp_y + minus_y(e_z, columns(0, at(2))) - 4.0 * e_z
                fx_z = zp_x - e_z
                fy_z = zp_y - e_z
                k_x = da - (xp_y + xm_y + plus_z(e_x) + minus_z(e_x) - 4.0 * e_x) + (fx_z - minus_z(fx_z))
                k_y = (fy_z - minus_z(fy_z)) - (plus_z(e_y) + minus_z(e_y) - 2.0 * e_y) - y2 + dt
                ca = c + a
                k_z = (plus_z(ca) - ca) - z2
                for number, value in enumerate((k_x, k_y, k_z)):
                    cross = induct[number] * field[s, pl.ds((1 - p) * half + number * depth, depth)]
                    value = value - cross if p == 0 else value + cross
                    out[s, pl.ds(p * half + number * depth, depth)] = value

    exchange_start(0, res_ref)
    total[...] = jnp.zeros_like(total)

    def gram_body(j, _):
        block = full_c[:, pl.ds(pl.multiple_of(j * 16, 16), 16), :].reshape(vecs * 16, width_y)
        total[...] += lax.dot_general(block, block, (((1,), (1,)), ((), ())), preferred_element_type=F32)
        return 0

    wide = vecs * 16
    halves = wide // width_y
    start = blank(base)
    own[0].wait()
    for piece in range(chunks):
        if piece + 1 == chunks:
            for way in range(2):
                [gather_start(1, way, u, jnp.logical_not(forwards(way, 1))) for u in range(chunks)]
        for step in range(1, n_tx - 1):
            gather_forward(0, step, piece)
        if piece + 2 < chunks:
            for way in range(2):
                gather_start(0, way, piece + 2, True)
        if piece + 1 == chunks:
            for way in range(2):
                [gather_start(1, way, u, forwards(way, 1)) for u in range(chunks)]
        gather_rest(0, piece)
        widen(piece)
        lax.fori_loop(piece * (chunk // 16), (piece + 1) * (chunk // 16), gram_body, 0)
        start = products(res_ref, [], piece * 8, 8, start)
        if piece + 1 < chunks:
            image_pack(piece)
    same = lax.rem(lax.broadcasted_iota(jnp.int32, (wide, wide), 0), 16) == lax.rem(
        lax.broadcasted_iota(jnp.int32, (wide, wide), 1), 16
    )
    folded = jnp.sum(jnp.where(same, total[...], 0.0).reshape(vecs, 16, wide), axis=1)
    gram = jnp.zeros((vecs, width_y), F32)
    lane = lax.broadcasted_iota(jnp.int32, (width_y, width_y), 0)
    column = lax.broadcasted_iota(jnp.int32, (width_y, width_y), 1)
    for h in range(halves):
        pick = (lax.div(lane, 16) + h * (width_y // 16) == column).astype(F32)
        gram = gram + jnp.dot(
            folded[:, h * width_y : (h + 1) * width_y], pick,
            precision=lax.Precision.HIGHEST, preferred_element_type=F32,
        )
    part[0, pl.ds(0, vecs)] = gram
    part[0, pl.ds(vecs, 8)] = pack_sums(start)
    group_send(0, vecs + 8)
    image_pack(chunks - 1)
    for number in range(2, len(links)):
        image_start(number, 0)
    first_sum = group_sum(0, vecs + 8)
    gram = first_sum[:vecs, :vecs]
    start = unpack_sums(first_sum[vecs:], base)
    row_id = lax.broadcasted_iota(jnp.int32, (vecs, vecs), 0)
    eye = (row_id == lax.broadcasted_iota(jnp.int32, (vecs, vecs), 1)).astype(F32)
    wide_row = lax.broadcasted_iota(jnp.int32, (vecs, 2 * vecs), 0)
    system = jnp.concatenate([gram, eye], axis=1)
    for k in range(0, vecs, 2):
        col_0 = jnp.broadcast_to(system[:, k : k + 1], (vecs, 2 * vecs))
        col_1 = jnp.broadcast_to(system[:, k + 1 : k + 2], (vecs, 2 * vecs))
        top, low = system[k : k + 1], system[k + 1 : k + 2]
        p_00, p_01 = col_0[k : k + 1], col_1[k : k + 1]
        p_10, p_11 = col_0[k + 1 : k + 2], col_1[k + 1 : k + 2]
        scale = 1.0 / (p_00 * p_11 - p_01 * p_10)
        new_0 = (p_11 * top - p_01 * low) * scale
        new_1 = (p_00 * low - p_10 * top) * scale
        system = system - col_0 * new_0 - col_1 * new_1
        system = jnp.where(wide_row == k, new_0, jnp.where(wide_row == k + 1, new_1, system))
    inverse[...] = system[:, vecs:]

    def solve(column):
        answer = jnp.sum(inverse[...] * column, axis=0, keepdims=True)
        flat = jnp.sum(eye * column, axis=0, keepdims=True)
        return answer, jnp.sum(answer * flat, axis=1, keepdims=True)

    weights = [solve(start[s * vecs : (s + 1) * vecs])[0] for s in range(sources)]
    one = jnp.ones((1, 1), F32)
    combine(held.at[0], [(res_ref, [one] * sources)], [-w for w in weights], wide_c)
    exchange_wait(0)
    image_wait()
    combine_halo(row_r, col_r, [(row_in.at[0], col_in.at[0], [one] * sources)])

    every = range(sources)
    for cycle in range(CYCLES):
        index = 2 * cycle
        resid = held.at[cycle]
        apply(resid, row_r, col_r, work)

        def meanwhile():
            exchange_start(index + 1, work)
            if index + 1 < n_tx - 1:
                [gather_forward(1, index + 1, u) for u in range(chunks)]
            if cycle:
                accumulate(cycle - 1, *update)

        sums = step_sums(index + 1, work, [(resid, resid), (resid, work), (work, work)], meanwhile)
        state = []
        for s in every:
            def got(i):
                return sums[base + 3 * s + i : base + 3 * s + i + 1]

            beta = jnp.sqrt(got(0) + EPS)
            scale = 1.0 / beta
            raw, quad = solve(sums[s * vecs : (s + 1) * vecs])
            g_0 = raw * scale
            n_00 = got(0) * scale * scale
            h_00 = got(1) * scale * scale
            left = (got(2) - quad) * scale * scale - 2.0 * h_00 * h_00 + h_00 * h_00 * n_00
            left = jnp.maximum(left, 0.0)
            h_10 = jnp.sqrt(left + EPS)
            state.append((beta, scale, g_0, n_00, h_00, left, h_10))
        of_w = [v[1] / v[6] for v in state]
        of_r = [-v[4] * v[1] / v[6] for v in state]
        combine(krylov, [(work, of_w), (resid, of_r)], [-v[2] / v[6] for v in state], wide_c)
        exchange_wait(index + 1)
        now = (row_in.at[index + 1], col_in.at[index + 1])
        combine_halo(row_v, col_v, [now + (of_w,), (row_r, col_r, of_r)])
        apply(krylov, row_v, col_v, work)

        def meanwhile():
            if cycle + 1 < CYCLES:
                exchange_start(index + 2, work)
            if index + 2 < n_tx - 1:
                [gather_forward(1, index + 2, u) for u in range(chunks)]

        pairs = [(resid, work), (krylov, work), (work, work), (krylov, krylov)]
        sums = step_sums(index + 2, work, pairs, meanwhile)
        in_r, in_v, in_w, in_g, out_r, out_v = [], [], [], [], [], []
        for s in every:
            def got(i):
                return sums[base + 4 * s + i : base + 4 * s + i + 1]

            beta, scale, g_0, n_00, h_00, _, h_10 = state[s]
            g_1, quad = solve(sums[s * vecs : (s + 1) * vecs])
            h_01 = got(0) * scale
            h_11 = got(1)
            n_11 = got(3)
            n_01 = h_00 * (1.0 - n_00) / h_10
            left = (
                got(2) - quad - 2.0 * (h_01 * h_01 + h_11 * h_11)
                + h_01 * h_01 * n_00 + h_11 * h_11 * n_11 + 2.0 * h_01 * h_11 * n_01
            )
            h_21 = jnp.sqrt(jnp.maximum(left, 0.0) + EPS)
            a_00 = h_00 * h_00 + h_10 * h_10
            a_01 = h_00 * h_01 + h_10 * h_11
            a_11 = h_01 * h_01 + h_11 * h_11 + h_21 * h_21
            l_00 = jnp.sqrt(a_00)
            l_10 = a_01 / l_00
            l_11 = jnp.sqrt(a_11 - l_10 * l_10)
            f_0 = beta * h_00 / l_00
            f_1 = (beta * h_01 - l_10 * f_0) / l_11
            y_1 = f_1 / l_11
            y_0 = (f_0 - l_10 * y_1) / l_00
            t_0 = beta - h_00 * y_0 - h_01 * y_1
            t_1 = -(h_10 * y_0 + h_11 * y_1)
            t_2 = -h_21 * y_1
            share = t_2 / h_21
            in_r.append((t_0 - share * h_01) * scale)
            in_v.append(t_1 - share * h_11)
            in_w.append(share)
            in_g.append(-share * g_1)
            out_r.append(y_0 * scale)
            out_v.append(y_1)
            weights[s] = weights[s] - (g_0 * y_0 + g_1 * y_1)
        update = (out_r, out_v)
        target = held.at[cycle + 1] if cycle + 1 < CYCLES else res_ref
        combine(target, [(resid, in_r), (krylov, in_v), (work, in_w)], in_g, wide_c)
        if cycle + 1 < CYCLES:
            exchange_wait(index + 2)
            now = (row_in.at[index + 2], col_in.at[index + 2])
            combine_halo(row_r, col_r, [(row_r, col_r, in_r), (row_v, col_v, in_v), now + (in_w,)])

    for step in range(2 * CYCLES + 1, n_tx - 1):
        [gather_forward(1, step, u) for u in range(chunks)]
    for u in range(chunks):
        gather_rest(1, u)
    own[1].wait()
    terms = [(held.at[CYCLES - 1], update[0]), (krylov, update[1])]
    if CYCLES > 1:
        terms.append((sol_ref, [one] * sources))
    combine(sol_ref, terms, weights, full_u)
    gather_sent(0)
    gather_sent(1)
    for index in range(2 * CYCLES):
        for number in range(len(links)):
            @pl.when(links[number][5])
            def _():
                halo_copy(index, number).wait_send()
    for number, piece in image_copies:
        @pl.when(links[number][5])
        def _():
            image_copy(number, piece).wait_send()


def on_device(dims, src_cell, basis, images, induction):
    n_gx, n_gy, n_tx = dims
    per_dev, _, _, depth, width_x, width_y = basis.shape
    sources = src_cell.shape[0]
    tiles = 6 * depth
    rows = tiles * width_x
    vecs = per_dev * n_tx
    group = n_gx * n_gy
    field = (sources, tiles, width_x, width_y)
    ind_rows = 3 * induction.shape[1] * width_x
    most = vecs + 8
    sums, halos = 2 * CYCLES + 1, 2 * CYCLES
    dma = pltpu.SemaphoreType.DMA
    vmem = pl.BlockSpec(memory_space=pltpu.VMEM)
    hbm = pl.BlockSpec(memory_space=pl.ANY)
    chunks = tiles // 16
    out = pl.pallas_call(
        functools.partial(kernel, dims),
        out_shape=(jax.ShapeDtypeStruct(field, F32),) * 2,
        in_specs=[pl.BlockSpec(memory_space=pltpu.SMEM), hbm, hbm, hbm],
        out_specs=(vmem, vmem),
        scratch_shapes=[
            pltpu.VMEM((vecs, rows, width_y), jnp.bfloat16),
            pltpu.VMEM((vecs, rows, width_y), jnp.bfloat16),
            pltpu.VMEM((n_tx, ind_rows, width_y), jnp.bfloat16),
            pltpu.VMEM((3, depth, width_x, width_y), F32),
            pltpu.VMEM(field, F32),
            pltpu.VMEM(field, F32),
            pltpu.VMEM((vecs * 16, vecs * 16), F32),
            pltpu.VMEM((vecs, vecs), F32),
            pltpu.VMEM((sources, vecs, width_x, width_y), F32),
            pltpu.VMEM((CYCLES,) + field, F32),
            pltpu.VMEM((vecs, tiles, width_x, width_y), F32),
            pltpu.VMEM((sums, most, width_y), F32),
            pltpu.VMEM((sums, group, most, width_y), F32),
            pltpu.VMEM((halos, 2, sources * tiles, width_y), F32),
            pltpu.VMEM((halos, 2, sources * tiles, width_y), F32),
            pltpu.VMEM((halos, 2, width_x, width_y), F32),
            pltpu.VMEM((halos, 4, width_x, width_y), F32),
            pltpu.VMEM((2, chunks, vecs * 16, width_y), F32),
            pltpu.VMEM((2, chunks, vecs * 16, width_y), F32),
            pltpu.VMEM((2, vecs, width_x, width_y), F32),
            pltpu.VMEM((4, vecs, width_x, width_y), F32),
            pltpu.VMEM((2, sources * tiles, width_y), F32),
            pltpu.VMEM((2, sources * tiles, width_y), F32),
            pltpu.VMEM((4, width_x, width_y), F32),
            pltpu.VMEM((4, width_x, width_y), F32),
            dma((3,)),
            dma((2, 2, n_tx - 1, chunks)),
            dma((2, 2, n_tx - 1, chunks)),
            dma((n_tx - 1,)),
            dma((n_tx - 1,)),
            dma((sums, group - 1)),
            dma((sums, group - 1)),
            dma((halos, 6)),
            dma((halos, 6)),
            dma((2 * chunks + 4,)),
            dma((2 * chunks + 4,)),
        ],
        compiler_params=pltpu.CompilerParams(
            collective_id=0, has_side_effects=True, vmem_limit_bytes=60 * 1024 * 1024
        ),
        cost_estimate=pl.CostEstimate(flops=400_000_000, bytes_accessed=2_000_000, transcendentals=20_000),
    )(
        src_cell,
        basis.reshape(per_dev, rows, width_y),
        images.reshape(per_dev, rows, width_y),
        induction.reshape(ind_rows, width_y),
    )
    shape = (sources, 2, 3, depth, width_x, width_y)
    return tuple(o.reshape(shape) for o in out)


def solution(mesh):
    dims = (mesh.shape["gx"], mesh.shape["gy"], mesh.shape["tx"])
    spec = P("tx", None, None, None, "gx", "gy")
    return jax.shard_map(
        functools.partial(on_device, dims),
        mesh=mesh,
        in_specs=(P("tx"), spec, spec, P(None, "tx", "gx", "gy")),
        out_specs=(spec, spec),
        check_vma=False,
    )
```
